128 devices in a mesh: expert: 4 (over x_hi, core), context: 8 (over x_lo, y), dp: 4 (over z).
Axes of the slice: x: 4 (x_hi: 2, x_lo: 2; x = x_hi * 2 + x_lo), y: 4, z: 4, core: 2. Of those that a mesh axis runs over, the one named last changes fastest.
Arguments:
- tokens: bfloat16 [16, 1024, 1536], P(('expert', 'dp'), 'context'), may hold values from -6 to 6
- expert_ids: int32 [16, 1024, 8], P(('expert', 'dp'), 'context'), may hold values from 0 to 31, all different within a row; in each aligned block of 128 rows (0 to 127, 128 to 255, ..., all dimensions but the last counted through in order) at most 40 rows name the same one
- w_query: bfloat16 [1536, 1536], replicated, may hold values from -0.15625 to 0.15625
- w_key: bfloat16 [1536, 512], replicated, may hold values from -0.15625 to 0.15625
- w_value: bfloat16 [1536, 512], replicated, may hold values from -0.15625 to 0.15625
- w_out: bfloat16 [1536, 1536], replicated, may hold values from -1.25 to 1.25
- gain_attn: float32 [1536], replicated, may hold values from 0.5 to 1.5
- gain_moe: float32 [1536], replicated, may hold values from 0.5 to 1.5
- w_router: bfloat16 [1536, 32], replicated, may hold values from -0.078125 to 0.078125
- w_gate: bfloat16 [32, 1536, 512], P(('expert', 'dp')), may hold values from -0.15625 to 0.15625
- w_up: bfloat16 [32, 1536, 512], P(('expert', 'dp')), may hold values from -0.15625 to 0.15625
- w_down: bfloat16 [32, 512, 1536], P(('expert', 'dp')), may hold values from -1 to 1
- cotangent: bfloat16 [16, 1024, 1536], P(('expert', 'dp'), 'context'), may hold values from -6 to 6
Outputs:
- mixed: bfloat16 [16, 1024, 1536], P(('expert', 'dp'), 'context')
- grad_tokens: float32 [16, 1024, 1536], P(('expert', 'dp'), 'context')
- grad_w_query: float32 [1536, 1536], P(('context', 'dp'))
- grad_w_key: float32 [1536, 512], P(('context', 'dp'))
- grad_w_value: float32 [1536, 512], P(('context', 'dp'))
- grad_w_out: float32 [1536, 1536], P(('context', 'dp'))
- grad_gain_attn: float32 [1536], P(('context', 'dp'))
- grad_gain_moe: float32 [1536], P(('context', 'dp'))
- grad_w_router: float32 [1536, 32], P(('context', 'dp'))
- grad_w_gate: float32 [32, 1536, 512], P(('expert', 'dp'), 'context')
- grad_w_up: float32 [32, 1536, 512], P(('expert', 'dp'), 'context')
- grad_w_down: float32 [32, 512, 1536], P(('expert', 'dp'), None, 'context')
The draws below stay inside these ranges and needn't reach their ends.
Inputs may be any that keep to these rules, and one draw needn't show every extreme that they name: `expert_ids`: each token names 8 different experts; among the 128 tokens of one device no expert is named more than 40 times, a bound that some block reaches.
All inputs are finite; a program needn't handle non-finite values.
Results may differ from the reference program's by a relative error of at most 0.03.
Values may be sent and summed in bfloat16 or wider, within the bound.
A program may use at most 192 MiB of HBM per device.

```python
import math
import jax
import jax.numpy as jnp
import numpy as np
from jax import lax

D = 1536
HEADS = 24
KV_HEADS = 8
HEAD_DIM = 64
FF = 512
TOP = 8
EXPERTS = 32
LENGTH = 1024
ROWS = 128
SEQS = 16
CAP = 40
N_CONTEXT = 8


def steps_of(rng, dims, split, least, top_value):
    level, own = 1.0, jax.random.fold_in(rng, 6)
    for axis_at, blocks in split:
        heights = jnp.exp(jax.random.uniform(jax.random.fold_in(own, axis_at), (blocks,), jnp.float32, least / len(split), top_value / len(split)))
        level = level * jnp.repeat(heights, dims[axis_at] // blocks).reshape([-1 if axis == axis_at else 1 for axis in range(len(dims))])
    return level


def routed_block(key, own, number, rows, count, top, limit, skew):
    order = jax.random.permutation(key, count)
    heavy_load, usual = shares(count, rows * top, limit, skew, True), shares(count, rows * top, limit, skew, False)
    places = jnp.arange(count)

    def named(tallies, offset_by):
        used = int((tallies > 0).sum())
        fixed = max(1, used // 4)
        moved = fixed + (places - fixed + offset_by * (used - fixed)) % max(1, count - fixed)
        return jnp.zeros((count,), jnp.int32).at[order[jnp.where(places < fixed, places, moved)]].set(jnp.asarray(tallies, jnp.int32))

    tallies = jnp.where(number % 4 == 0, named(heavy_load, number // 4), named(usual, number - number // 4 - 1))
    mixed = jax.random.permutation(jax.random.fold_in(own, 3), count)
    source_of, taker = mixed[0:count // 2 * 2:2], mixed[1:count // 2 * 2:2]
    slack = jnp.minimum(tallies[source_of] - 1, limit - tallies[taker]) // 2
    slack = jnp.where((source_of == order[0]) | (taker == order[0]) | (tallies[taker] == 0), 0, jnp.maximum(slack, 0))
    moved = jax.random.randint(jax.random.fold_in(own, 4), (count // 2,), 0, 1 << 20) % (slack + 1)
    tallies = tallies.at[source_of].add(-moved).at[taker].add(moved)
    labels = jnp.searchsorted(jnp.cumsum(tallies), jnp.arange(rows * top), side="right").astype(jnp.int32)
    grid = labels.reshape(top, rows).T
    grid = grid[jax.random.permutation(jax.random.fold_in(own, 1), rows)]
    offset_by = jax.random.randint(jax.random.fold_in(own, 2), (rows, 1), 0, top)
    return jnp.take_along_axis(grid, (jnp.arange(top)[None, :] + offset_by) % top, axis=1)


def shares(amount, total, reach, skew, full):
    portions = [(1 << 20) // math.isqrt(rank ** skew) + 1 for rank in range(1, amount + 1)]
    largest = reach if full else min(reach, max(-(-total // amount), total * portions[0] // sum(portions)))
    least = 1 if total - largest >= amount - 1 else 0
    given, surplus = [largest] + [least] * (amount - 1), total - largest - least * (amount - 1)
    while surplus > 0:
        movable = [i for i in range(1, amount) if given[i] < largest] or [i for i in range(1, amount) if given[i] < reach]
        whole, budget = sum([portions[i] for i in movable]), surplus
        for i in movable:
            more = min(reach - given[i], max(1, budget * portions[i] // whole), surplus)
            given[i] = given[i] + more
            surplus = surplus - more
    return np.array(given)


def gaussian(key, shape, scale, bound, split=(), kind=jnp.bfloat16):
    values = jax.random.normal(key, shape, jnp.float32) * scale
    if len(split) > 0:
        values = steps_of(key, shape, split, -0.22, 0.18) * values
    return jnp.clip(values, min=-bound, max=bound).astype(kind)


def setup_inputs(seed: int = 0) -> dict:
    seeds = jax.random.split(jax.random.key(seed), 14)
    tokens = gaussian(seeds[0], (SEQS, LENGTH, D), 1.0, 6.0, ((0, 16), (1, 8)))
    expert_ids_keys = jax.random.split(jax.random.fold_in(seeds[1], 1), SEQS * LENGTH // ROWS)
    expert_ids_turns = jax.random.permutation(jax.random.fold_in(seeds[1], 3), SEQS * LENGTH // ROWS)
    expert_ids = jax.vmap(lambda own, number: routed_block(jax.random.fold_in(seeds[1], 2), own, number, ROWS, EXPERTS, TOP, CAP, 2))(expert_ids_keys, expert_ids_turns).reshape((SEQS, LENGTH, TOP))
    w_query = gaussian(seeds[2], (D, HEADS * HEAD_DIM), D ** -0.5, 0.15625)
    w_key = gaussian(seeds[3], (D, KV_HEADS * HEAD_DIM), D ** -0.5, 0.15625)
    w_value = gaussian(seeds[4], (D, KV_HEADS * HEAD_DIM), D ** -0.5, 0.15625)
    w_out = gaussian(seeds[5], (HEADS * HEAD_DIM, D), (D // 64) ** -0.5, 1.25)
    gain_attn = jnp.clip(1.0 + 0.1 * jax.random.normal(seeds[6], (D,), jnp.float32), 0.5, 1.5)
    gain_moe = jnp.clip(1.0 + 0.1 * jax.random.normal(seeds[7], (D,), jnp.float32), 0.5, 1.5)
    w_router = gaussian(seeds[8], (D, EXPERTS), (4 * D) ** -0.5, 0.078125)
    w_gate = gaussian(seeds[9], (EXPERTS, D, FF), D ** -0.5, 0.15625, ((0, 16),))
    w_up = gaussian(seeds[10], (EXPERTS, D, FF), D ** -0.5, 0.15625, ((0, 16),))
    w_down = gaussian(seeds[11], (EXPERTS, FF, D), (FF // 16) ** -0.5, 1.0, ((0, 16),))
    cotangent = gaussian(seeds[12], (SEQS, LENGTH, D), 1.0, 6.0, ((0, 16), (1, 8)))
    return {"tokens": tokens, "expert_ids": expert_ids, "w_query": w_query, "w_key": w_key, "w_value": w_value, "w_out": w_out, "gain_attn": gain_attn, "gain_moe": gain_moe, "w_router": w_router, "w_gate": w_gate, "w_up": w_up, "w_down": w_down, "cotangent": cotangent}


epsilon = 1e-06
floor_score = -1e+30
highest = lax.Precision.HIGHEST

@jax.custom_vjp
def low(v):
    return lax.optimization_barrier(v.astype(jnp.bfloat16)).astype(jnp.float32)

@jax.custom_vjp
def low_back(v):
    return v

def low_keep(v):
    return (low(v), None)

def low_pass(kept, grad):
    return (grad,)

def back_keep(v):
    return (v, None)

def back_low(kept, grad):
    return (low(grad),)
low.defvjp(low_keep, low_pass)
low_back.defvjp(back_keep, back_low)

def matmul(left, right):
    return jnp.dot(left, right, precision=highest, preferred_element_type=jnp.float32)

def normalize(values, gain):
    return values * lax.rsqrt(lax.optimization_barrier(jnp.mean(values * values, axis=-1, keepdims=True)) + epsilon) * gain

def rotary_tables(positions, half):
    index = lax.iota(jnp.float32, half)
    freqs = jnp.exp(index * (-math.log(10000.0) / half))
    angles = positions[:, None] * freqs[None, :]
    return (jnp.cos(angles)[:, None, :], jnp.sin(angles)[:, None, :])

def rotate(values, cosine, sine):
    half = values.shape[-1] // 2
    first = values[..., :half]
    second = values[..., half:]
    return jnp.concatenate([first * cosine - second * sine, second * cosine + first * sine], axis=-1)

def sequence_forward(x, ids, w_query, w_key, w_value, w_out, gain_attn, gain_moe, w_router, w_gate, w_up, w_down):
    length = x.shape[0]
    group = HEADS // KV_HEADS
    scale = HEAD_DIM ** (-0.5)
    positions = lax.iota(jnp.int32, length)
    cosine, sine = rotary_tables(positions.astype(jnp.float32), HEAD_DIM // 2)
    n1 = low(normalize(x, gain_attn))
    q_raw = low_back(matmul(n1, w_query)).reshape(length, HEADS, HEAD_DIM)
    k_raw = low_back(matmul(n1, w_key)).reshape(length, KV_HEADS, HEAD_DIM)
    value = low(low_back(matmul(n1, w_value))).reshape(length, KV_HEADS, HEAD_DIM)
    query = low(rotate(q_raw, cosine, sine)).reshape(length, KV_HEADS, group, HEAD_DIM)
    key = low(rotate(k_raw, cosine, sine))
    q_block = min(1024, length)
    query_blocks = query.reshape(length // q_block, q_block, KV_HEADS, group, HEAD_DIM)
    block_starts = lax.iota(jnp.int32, length // q_block) * q_block

    def attend(block_item):
        q_part, q_start = block_item
        q_positions = q_start + lax.iota(jnp.int32, q_block)
        scores = low_back(jnp.einsum('qkgd,skd->kgqs', q_part, key, precision=highest) * scale)
        scores = jnp.where(positions[None, None, None, :] <= q_positions[None, None, :, None], scores, floor_score)
        probs = low(jax.nn.softmax(scores, axis=-1))
        return jnp.einsum('kgqs,skd->qkgd', probs, value, precision=highest)
    attn = lax.map(jax.checkpoint(attend), (query_blocks, block_starts)).reshape(length, HEADS * HEAD_DIM)
    attn = low(low_back(attn))
    y_mid = x + low_back(matmul(attn, w_out))
    n2 = low(normalize(y_mid, gain_moe))
    logits = low_back(matmul(n2, w_router))
    gates = jax.nn.softmax(jnp.take_along_axis(logits, ids, axis=1), axis=-1)
    match = ids[:, :, None] == lax.iota(jnp.int32, EXPERTS)[None, None, :]
    counts = lax.optimization_barrier(jnp.sum(match.astype(jnp.int32), axis=1))
    before = jnp.cumsum(counts, axis=0) - counts
    slot = lax.optimization_barrier(jnp.sum(jnp.where(match, before[:, None, :], 0), axis=2))
    slot_count = N_CONTEXT * CAP
    target = (ids * slot_count + slot).reshape(-1)
    spread = low_back(jnp.broadcast_to(n2[:, None, :], (length, TOP, D)))
    buffer = jnp.zeros((EXPERTS * slot_count, D), jnp.float32).at[target].set(spread.reshape(length * TOP, D))
    buffer = buffer.reshape(EXPERTS, slot_count, D)
    hidden_gate = low_back(jnp.einsum('esd,edf->esf', buffer, w_gate, precision=highest))
    hidden_up = low_back(jnp.einsum('esd,edf->esf', buffer, w_up, precision=highest))
    active = low(jax.nn.silu(hidden_gate) * hidden_up)
    produced = low(low_back(jnp.einsum('esf,efd->esd', active, w_down, precision=highest)))
    picked = produced.reshape(EXPERTS * slot_count, D)[target].reshape(length, TOP, D)
    return y_mid + lax.optimization_barrier(jnp.sum(gates[:, :, None] * picked, axis=1))

def reference(tokens, expert_ids, w_query, w_key, w_value, w_out, gain_attn, gain_moe, w_router, w_gate, w_up, w_down, cotangent):

    def forward(x, wq, wk, wv, wo, ga, gm, wr, wg, wu, wd):

        def one_sequence(carry, seq_item):
            seq_x, seq_ids = seq_item
            result = jax.checkpoint(sequence_forward)(seq_x, seq_ids, wq, wk, wv, wo, ga, gm, wr, wg, wu, wd)
            return (carry, result)
        _, result = lax.scan(one_sequence, jnp.zeros((), jnp.float32), (x, expert_ids))
        return result
    inputs = (tokens, w_query, w_key, w_value, w_out, gain_attn, gain_moe, w_router, w_gate, w_up, w_down)
    floats = tuple((v.astype(jnp.float32) for v in inputs))
    result, pull = jax.vjp(forward, *floats)
    grads = pull(cotangent.astype(jnp.float32))
    return (result.astype(jnp.bfloat16), grads[0], grads[1], grads[2], grads[3], grads[4], grads[5], grads[6], grads[7], grads[8], grads[9], grads[10])
```

```python
import functools
import math

import jax
import jax.numpy as jnp
from jax import lax
from jax.experimental import pallas as pl
from jax.experimental.pallas import tpu as pltpu
from jax.sharding import PartitionSpec as P

MESH = pl.DeviceIdType.MESH
BF = jnp.bfloat16
F32 = jnp.float32


class Place:
    def __init__(self):
        e, c = lax.axis_index("expert"), lax.axis_index("context")
        self.hi, self.core = e // 2, e % 2
        self.lo, self.y = c // 4, c % 4
        self.z = lax.axis_index("dp")

    def at(self, hi=0, core=0, lo=0, y=0, z=0):
        e = (self.hi + hi) % 2 * 2 + (self.core + core) % 2
        c = (self.lo + lo) % 2 * 4 + (self.y + y) % 4
        return (e, c, (self.z + z) % 4)

    def line(self, axis):
        if axis == "y":
            return [((self.y + d) % 4, self.at(y=d)) for d in (1, 2, 3)]
        if axis == "z":
            return [((self.z + d) % 4, self.at(z=d)) for d in (1, 2, 3)]
        return [
            ((self.hi + a) % 2 * 2 + (self.lo + b) % 2, self.at(hi=a, lo=b))
            for a, b in ((0, 1), (1, 0), (1, 1))
        ]

    def own(self, axis):
        return {"y": self.y, "z": self.z, "x": self.hi * 2 + self.lo}[axis]


def greet(devices):
    barrier = pltpu.get_barrier_semaphore()
    for device in devices:
        pl.semaphore_signal(barrier, inc=1, device_id=device, device_id_type=MESH)
    pl.semaphore_wait(barrier, len(devices))


def send(src, dst, sems, device):
    copy = pltpu.make_async_remote_copy(
        src_ref=src, dst_ref=dst, send_sem=sems[0], recv_sem=sems[1],
        device_id=device, device_id_type=MESH,
    )
    copy.start()
    return copy


def scatter_start(place, axis, src, landing, sems, begin):
    copies = []
    for d, (index, device) in enumerate(place.line(axis)):
        pair = (sems.at[0, begin + d], sems.at[1, begin + d])
        copies.append(send(src.at[index], landing.at[d], pair, device))
    return copies


def add_up(out, own, landing, lead):
    count = landing.shape[0]

    def body(i, carry):
        total = own[i].astype(F32)
        for d in range(count):
            total = total + landing[d, i].astype(F32)
        out[i] = total.astype(out.dtype)
        return carry

    lax.fori_loop(0, lead, body, 0)


WIDE = 384
ORDERS = {"o": "xyz", "q": "zyx", "s": "yzx"}


def stream_index(order, block, half):
    at = {"x": half * 2 + block // 16, "y": block // 4 % 4, "z": block % 4}
    return tuple(at[axis] for axis in order)


def fill_stream(out, order, left, right, width):
    for half in range(2):
        columns = right[:, half * width : (half + 1) * width]
        for tile in range(4):
            grads = lax.dot_general(
                left[:, tile * 384 : (tile + 1) * 384], columns,
                (((0,), (0,)), ((), ())), preferred_element_type=F32,
            ).astype(BF)
            for j in range(8):
                index = stream_index(order, tile * 8 + j, half)
                out[(*index, slice(None), slice(0, width))] = grads[j * 48 : (j + 1) * 48]


def reduce_kernel(
    n1, attn, dq, dkv, dbr, narrow, eg, eu, ed,
    gq, gk, gv, go, gs, og, ou, od,
    n1c, attnc, dqc, dkvc, dbrc, pair_sems,
    send_o, send_q, send_s, land1_o, land1_q, land1_s, mid_o, mid_q, mid_s,
    land2_o, land2_q, land2_s, last_o, last_q, last_s, land3_o, land3_q, land3_s, dense_sems,
    mine, quarters, quarter_sems,
    own_p, own_q, land_p1, land_q1, sum_p, sum_q, land_p2, land_q2, expert_sems, local_sems,
):
    place = Place()
    y_line, z_line, x_line = (place.line(axis) for axis in "yzx")
    sibling = place.at(core=1)
    cross = place.at(hi=1, core=1)
    greet([device for line in (y_line, z_line, x_line) for _, device in line] + [sibling, cross])
    pending = []

    pairs = []
    for i, (rows, both, part) in enumerate(
        ((attn, attnc, None), (dbr, dbrc, 1), (n1, n1c, None), (dq, dqc, 1), (dkv, dkvc, 1))
    ):
        source = rows if part is None else rows.at[1 - place.core]
        pair = (pair_sems.at[0, i], pair_sems.at[1, i])
        pairs.append(send(source, both.at[pl.ds(128, 128)], pair, sibling))
        both[0:128, :] = rows[...] if part is None else rows[place.core]

    mats = (eg, eu, ed)
    stage_p, stage_q = [], []
    other_lo = (place.lo + 1) % 2
    lo_device = place.at(lo=1)
    at = 0
    for m, mat in enumerate(mats):
        for d, (index, device) in enumerate(y_line):
            pair = (expert_sems.at[0, at], expert_sems.at[1, at])
            stage_p.append(send(mat.at[0, :, index], land_p1.at[d, m], pair, device))
            at += 1
        pair = (expert_sems.at[0, at], expert_sems.at[1, at])
        stage_q.append(send(mat.at[1, other_lo], land_q1.at[m], pair, lo_device))
        at += 1
    local = []
    for m, mat in enumerate(mats):
        local.append(pltpu.make_async_copy(mat.at[0, :, place.y], own_p.at[m], local_sems.at[0, m]))
        local.append(pltpu.make_async_copy(mat.at[1, place.lo], own_q.at[m], local_sems.at[1, m]))
    for copy in local:
        copy.start()

    sends = {"o": send_o, "q": send_q, "s": send_s}
    lands = {
        "o": (land1_o, land2_o, land3_o), "q": (land1_q, land2_q, land3_q),
        "s": (land1_s, land2_s, land3_s),
    }
    mids = {"o": (mid_o, last_o), "q": (mid_q, last_q), "s": (mid_s, last_s)}
    begin = {"o": 0, "q": 9, "s": 18}
    flight = {}

    def launch(name, phase):
        source = sends[name] if phase == 0 else mids[name][phase - 1]
        flight[name] = scatter_start(
            place, ORDERS[name][phase], source, lands[name][phase], dense_sems,
            begin[name] + 3 * phase,
        )

    def land(name, phase):
        for copy in flight[name]:
            copy.wait_recv()
        pending.extend(flight[name])
        source = sends[name] if phase == 0 else mids[name][phase - 1]
        own = source.at[place.own(ORDERS[name][phase])]
        landing = lands[name][phase]
        if phase == 0:
            out = mids[name][0]

            def body(i, carry):
                a, b = i // 4, i % 4
                total = own[a, b].astype(F32)
                for d in range(3):
                    total = total + landing[d, a, b].astype(F32)
                out[a, b] = total.astype(BF)
                return carry

            lax.fori_loop(0, 16, body, 0)
        elif phase == 1:
            add_up(mids[name][1], own, landing, 4)
        else:
            total = own[...].astype(F32)
            for d in range(3):
                total = total + landing[d].astype(F32)
            mine["oqs".index(name)] = total.astype(BF)

    for copy in pairs[:2]:
        copy.wait_recv()
    fill_stream(send_o, ORDERS["o"], attnc, dbrc, 384)
    launch("o", 0)
    for copy in pairs[2:4]:
        copy.wait_recv()
    fill_stream(send_q, ORDERS["q"], n1c, dqc, 384)
    launch("q", 0)
    pairs[4].wait_recv()
    fill_stream(send_s, ORDERS["s"], n1c, dkvc, 256)
    for block in range(32):
        for half in range(2):
            index = stream_index(ORDERS["s"], block, half)
            send_s[(*index, slice(None), slice(256, 384))] = narrow[block * 48 : (block + 1) * 48, :]
    launch("s", 0)
    pending.extend(pairs)
    for phase in range(3):
        for name in "oqs":
            land(name, phase)
            if phase < 2:
                launch(name, phase + 1)

    own_quarter = place.core * 2 + place.hi
    gathered = []
    for i, (a, b) in enumerate(((0, 1), (1, 0), (1, 1))):
        pair = (quarter_sems.at[0, i], quarter_sems.at[1, i])
        gathered.append(send(mine, quarters.at[own_quarter], pair, place.at(hi=a, core=b)))
    quarters[own_quarter] = mine[...]

    for copy in stage_p + stage_q:
        copy.wait_recv()
    for copy in local:
        copy.wait()
    pending.extend(stage_p + stage_q)

    def fold_p(i, carry):
        m, lo, part = i // 8, i // 4 % 2, pl.ds(i % 4 * 48, 48)
        total = own_p[m, lo, part].astype(F32)
        for d in range(3):
            total = total + land_p1[d, m, lo, part].astype(F32)
        sum_p[lo, m, part] = total.astype(BF)
        return carry

    lax.fori_loop(0, 24, fold_p, 0)
    pair = (expert_sems.at[0, 12], expert_sems.at[1, 12])
    second = [send(sum_p.at[other_lo], land_p2, pair, lo_device)]

    def fold_q(i, carry):
        m, y, part = i // 16, i // 4 % 4, pl.ds(i % 4 * 48, 48)
        total = own_q[m, y, part].astype(F32) + land_q1[m, y, part].astype(F32)
        sum_q[y, m, part] = total.astype(BF)
        return carry

    lax.fori_loop(0, 48, fold_q, 0)
    for d, (index, device) in enumerate(y_line):
        pair = (expert_sems.at[0, 13 + d], expert_sems.at[1, 13 + d])
        second.append(send(sum_q.at[index], land_q2.at[d], pair, device))

    for copy in gathered:
        copy.wait_recv()
    pending.extend(gathered)
    for q in range(4):
        go[:, q * 384 : (q + 1) * 384] = quarters[q, 0].astype(F32)
        gq[:, q * 384 : (q + 1) * 384] = quarters[q, 1].astype(F32)
        gk[:, q * 128 : (q + 1) * 128] = quarters[q, 2, :, 0:128].astype(F32)
        gv[:, q * 128 : (q + 1) * 128] = quarters[q, 2, :, 128:256].astype(F32)
    gs[...] = quarters[0, 2, :, 256:384].astype(F32) + quarters[2, 2, :, 256:384].astype(F32)

    for copy in second:
        copy.wait_recv()
    pending.extend(second)
    for m, out in enumerate((og, ou, od)):
        def finish(i, carry):
            part = pl.ds(i * 48, 48)
            out[0, part] = sum_p[place.lo, m, part].astype(F32) + land_p2[m, part].astype(F32)
            total = sum_q[place.y, m, part].astype(F32)
            for d in range(3):
                total = total + land_q2[d, m, part].astype(F32)
            out[1, part] = total
            return carry

        lax.fori_loop(0, 4, finish, 0)
    for copy in pending:
        copy.wait_send()


def reduce_gradients(n1, attn, dq, dkv, dbr, narrow, eg, eu, ed):
    vmem = pl.BlockSpec(memory_space=pltpu.VMEM)
    sems = pltpu.SemaphoreType.DMA
    f32 = lambda *shape: jax.ShapeDtypeStruct(shape, F32)
    low = lambda *shape: pltpu.VMEM(shape, BF)
    streams = 3
    return pl.pallas_call(
        reduce_kernel,
        out_shape=(
            f32(48, 1536), f32(48, 512), f32(48, 512), f32(48, 1536), f32(48, 128),
            f32(2, 192, 512), f32(2, 192, 512), f32(2, 192, 512),
        ),
        in_specs=[vmem] * 6 + [pl.BlockSpec(memory_space=pl.ANY)] * 3,
        out_specs=[vmem] * 8,
        scratch_shapes=[
            low(256, 1536), low(256, 1536), low(256, 768), low(256, 512), low(256, 768),
            sems((2, 5)),
            *[low(4, 4, 4, 48, WIDE)] * streams,
            *[low(3, 4, 4, 48, WIDE)] * streams,
            *[low(4, 4, 48, WIDE)] * streams,
            *[low(3, 4, 48, WIDE)] * streams,
            *[low(4, 48, WIDE)] * streams,
            *[low(3, 48, WIDE)] * streams,
            sems((2, 27)),
            low(3, 48, WIDE), low(4, 3, 48, WIDE), sems((2, 3)),
            low(3, 2, 192, 512), low(3, 4, 192, 512),
            low(3, 3, 2, 192, 512), low(3, 4, 192, 512),
            low(2, 3, 192, 512), low(4, 3, 192, 512),
            low(3, 192, 512), low(3, 3, 192, 512),
            sems((2, 16)), sems((2, 3)),
        ],
        compiler_params=pltpu.CompilerParams(
            collective_id=0, has_side_effects=True, vmem_limit_bytes=60 << 20
        ),
    )(n1, attn, dq, dkv, dbr, narrow, eg, eu, ed)


HEADS = 24
KV_HEADS = 8
HEAD_DIM = 64


epsilon = 1e-06
floor_score = -1e30


def normalize(values, gain):
    return values * lax.rsqrt(jnp.mean(values * values, axis=-1, keepdims=True) + epsilon) * gain


def rotary_tables(positions, half):
    index = lax.iota(jnp.float32, half)
    freqs = jnp.exp(index * (-math.log(10000.0) / half))
    angles = positions[:, None] * freqs[None, :]
    return (jnp.cos(angles)[:, None, :], jnp.sin(angles)[:, None, :])


def rotate(values, cosine, sine):
    half = values.shape[-1] // 2
    first = values[..., :half]
    second = values[..., half:]
    return jnp.concatenate(
        [first * cosine - second * sine, second * cosine + first * sine], axis=-1
    )


def block_scores(query, key_block, key_start, positions, scale):
    kv_count = query.shape[1]
    key_heads = key_block.reshape(key_block.shape[0], kv_count, -1)
    scores = (
        jnp.einsum("qkgd,skd->kgqs", query, key_heads, preferred_element_type=jnp.float32) * scale
    )
    key_positions = key_start + lax.iota(jnp.int32, key_block.shape[0])
    return jnp.where(
        key_positions[None, None, None, :] <= positions[None, None, :, None], scores, floor_score
    )


def split_blocks(key_all, value_all, block):
    count = key_all.shape[0] // block
    starts = lax.iota(jnp.int32, count) * block
    return (key_all.reshape(count, block, -1), value_all.reshape(count, block, -1), starts)


def attention_forward(query, key_all, value_all, positions, scale, block):
    key_blocks, value_blocks, starts = split_blocks(key_all, value_all, block)
    stat_shape = (query.shape[1], query.shape[2], query.shape[0])

    def gather_stats(carry, block_item):
        top_score, total = carry
        key_block, key_start = block_item
        scores = block_scores(query, key_block, key_start, positions, scale)
        new_top = jnp.maximum(top_score, jnp.max(scores, axis=-1))
        total = total * jnp.exp(top_score - new_top) + jnp.sum(
            jnp.exp(scores - new_top[..., None]), axis=-1
        )
        return ((new_top, total), None)

    start_stats = (
        jnp.full(stat_shape, floor_score, jnp.float32),
        jnp.zeros(stat_shape, jnp.float32),
    )
    (top_score, total), _ = lax.scan(gather_stats, start_stats, (key_blocks, starts))

    def weigh_values(accum, block_item):
        key_block, value_block, key_start = block_item
        scores = block_scores(query, key_block, key_start, positions, scale)
        probs = (jnp.exp(scores - top_score[..., None]) / total[..., None]).astype(jnp.bfloat16)
        value_heads = value_block.reshape(value_block.shape[0], query.shape[1], -1)
        return (
            accum
            + jnp.einsum("kgqs,skd->qkgd", probs, value_heads, preferred_element_type=jnp.float32),
            None,
        )

    accum, _ = lax.scan(
        weigh_values, jnp.zeros(query.shape, jnp.float32), (key_blocks, value_blocks, starts)
    )
    return (accum, top_score, total)


def attention_backward(
    query, key_all, value_all, positions, scale, block, top_score, total, grad_heads, attn_full
):
    key_blocks, value_blocks, starts = split_blocks(key_all, value_all, block)
    delta = jnp.einsum("qkgd,qkgd->kgq", grad_heads.astype(jnp.float32), attn_full)

    def block_grads(grad_query, block_item):
        key_block, value_block, key_start = block_item
        span = key_block.shape[0]
        scores = block_scores(query, key_block, key_start, positions, scale)
        probs = jnp.exp(scores - top_score[..., None]) / total[..., None]
        probs_low = probs.astype(jnp.bfloat16)
        key_heads = key_block.reshape(span, query.shape[1], -1)
        value_heads = value_block.reshape(span, query.shape[1], -1)
        grad_values = jnp.einsum(
            "kgqs,qkgd->skd", probs_low, grad_heads, preferred_element_type=jnp.float32
        )
        grad_probs = jnp.einsum(
            "qkgd,skd->kgqs", grad_heads, value_heads, preferred_element_type=jnp.float32
        )
        grad_scores = (probs * (grad_probs - delta[..., None])).astype(jnp.bfloat16)
        grad_query = (
            grad_query
            + jnp.einsum(
                "kgqs,skd->qkgd", grad_scores, key_heads, preferred_element_type=jnp.float32
            )
            * scale
        )
        grad_keys = (
            jnp.einsum("kgqs,qkgd->skd", grad_scores, query, preferred_element_type=jnp.float32)
            * scale
        )
        return (grad_query, (grad_keys.reshape(span, -1), grad_values.reshape(span, -1)))

    grad_query, (grad_keys, grad_values) = lax.scan(
        block_grads, jnp.zeros(query.shape, jnp.float32), (key_blocks, value_blocks, starts)
    )
    return (
        grad_query,
        grad_keys.reshape(key_all.shape[0], -1),
        grad_values.reshape(key_all.shape[0], -1),
    )


def shards(
    tokens,
    expert_ids,
    w_query,
    w_key,
    w_value,
    w_out,
    gain_attn,
    gain_moe,
    w_router,
    w_gate,
    w_up,
    w_down,
    cotangent,
):
    row_count = tokens.shape[1]
    model_width = tokens.shape[2]
    group = HEADS // KV_HEADS
    kv_width = KV_HEADS * HEAD_DIM
    route_count = expert_ids.shape[2]
    expert_count = w_router.shape[1]
    local_experts = w_gate.shape[0]
    capacity = row_count * route_count // expert_count + row_count * route_count // (
        4 * expert_count
    )
    scale = HEAD_DIM ** (-0.5)
    sources = lax.axis_size(("expert", "dp"))
    seq_length = row_count * lax.axis_size("context")
    block = min(512, seq_length)
    positions = lax.axis_index("context") * row_count + lax.iota(jnp.int32, row_count)
    cosine, sine = rotary_tables(positions.astype(jnp.float32), HEAD_DIM // 2)
    x_rows = tokens[0].astype(jnp.float32)
    route_ids = expert_ids[0]
    n_first = normalize(x_rows, gain_attn).astype(jnp.bfloat16)
    q_raw = jnp.dot(n_first, w_query, preferred_element_type=jnp.float32).reshape(
        row_count, HEADS, HEAD_DIM
    )
    k_raw = jnp.dot(n_first, w_key, preferred_element_type=jnp.float32).reshape(
        row_count, KV_HEADS, HEAD_DIM
    )
    value_rows = jnp.dot(n_first, w_value, preferred_element_type=jnp.float32).astype(jnp.bfloat16)
    query = (
        rotate(q_raw, cosine, sine)
        .astype(jnp.bfloat16)
        .reshape(row_count, KV_HEADS, group, HEAD_DIM)
    )
    key_rows = rotate(k_raw, cosine, sine).astype(jnp.bfloat16).reshape(row_count, kv_width)
    key_all, value_all = (
        lax.all_gather(key_rows, "context", axis=0, tiled=True),
        lax.all_gather(value_rows, "context", axis=0, tiled=True),
    )
    attn_full, top_score, total = attention_forward(
        query, key_all, value_all, positions, scale, block
    )
    attn_low = attn_full.reshape(row_count, model_width).astype(jnp.bfloat16)
    y_mid = x_rows + jnp.dot(attn_low, w_out, preferred_element_type=jnp.float32)
    n_second = normalize(y_mid, gain_moe).astype(jnp.bfloat16)
    logits = jnp.dot(n_second, w_router, preferred_element_type=jnp.float32)

    def gate_values(logit_rows):
        return jax.nn.softmax(jnp.take_along_axis(logit_rows, route_ids, axis=1), axis=-1)

    gates, gate_pull = jax.vjp(gate_values, logits)
    match = route_ids[:, :, None] == lax.iota(jnp.int32, expert_count)[None, None, :]
    counts = jnp.sum(match.astype(jnp.int32), axis=1)
    before = jnp.cumsum(counts, axis=0) - counts
    slot = jnp.sum(jnp.where(match, before[:, None, :], 0), axis=2)
    target = (route_ids * capacity + slot).reshape(-1)

    def dispatch_rows(route_rows):
        filled = (
            jnp.zeros((expert_count * capacity, model_width), jnp.bfloat16)
            .at[target]
            .set(route_rows)
        )
        return filled.reshape(expert_count, capacity, model_width)

    def collect_rows(returned_rows):
        return returned_rows.reshape(expert_count * capacity, model_width)[target].reshape(
            row_count, route_count, model_width
        )

    spread = jnp.broadcast_to(n_second[:, None, :], (row_count, route_count, model_width)).reshape(
        -1, model_width
    )
    received_rows = lax.all_to_all(
        dispatch_rows(spread), ("expert", "dp"), split_axis=0, concat_axis=0, tiled=True
    )
    grouped = received_rows.reshape(sources, local_experts, -1, model_width)
    hidden_gate = jnp.einsum("sxcd,xdf->sxcf", grouped, w_gate, preferred_element_type=jnp.float32)
    hidden_up = jnp.einsum("sxcd,xdf->sxcf", grouped, w_up, preferred_element_type=jnp.float32)
    active = (jax.nn.silu(hidden_gate) * hidden_up).astype(jnp.bfloat16)
    produced = jnp.einsum("sxcf,xfd->sxcd", active, w_down, preferred_element_type=jnp.float32)
    produced = produced.astype(jnp.bfloat16).reshape(received_rows.shape)
    returned = lax.all_to_all(produced, ("expert", "dp"), split_axis=0, concat_axis=0, tiled=True)
    picked = collect_rows(returned).astype(jnp.float32)
    y_out = y_mid + jnp.sum(gates[:, :, None] * picked, axis=1)
    grad_out = cotangent[0].astype(jnp.float32)
    grad_gate_values = jnp.sum(grad_out[:, None, :] * picked, axis=2)
    weighted = (
        (gates[:, :, None] * grad_out[:, None, :]).astype(jnp.bfloat16).reshape(-1, model_width)
    )
    grad_back = lax.all_to_all(
        dispatch_rows(weighted), ("expert", "dp"), split_axis=0, concat_axis=0, tiled=True
    )
    grouped = received_rows.reshape(sources, local_experts, -1, model_width)
    grad_grouped = grad_back.reshape(sources, local_experts, -1, model_width)
    hidden_gate = jnp.einsum("sxcd,xdf->sxcf", grouped, w_gate, preferred_element_type=jnp.float32)
    hidden_up = jnp.einsum("sxcd,xdf->sxcf", grouped, w_up, preferred_element_type=jnp.float32)

    def activate(gate_part, up_part):
        return jax.nn.silu(gate_part) * up_part

    active_full, act_pull = jax.vjp(activate, hidden_gate, hidden_up)
    active = active_full.astype(jnp.bfloat16)
    grad_w_down = jnp.einsum(
        "sxcd,sxcf->xdf", grad_grouped, active, preferred_element_type=jnp.float32
    )
    grad_active = jnp.einsum(
        "sxcd,xfd->sxcf", grad_grouped, w_down, preferred_element_type=jnp.float32
    )
    grad_hg, grad_hu = act_pull(grad_active)
    grad_hg = grad_hg.astype(jnp.bfloat16)
    grad_hu = grad_hu.astype(jnp.bfloat16)
    grad_w_gate = jnp.einsum("sxcd,sxcf->xdf", grouped, grad_hg, preferred_element_type=jnp.float32)
    grad_w_up = jnp.einsum("sxcd,sxcf->xdf", grouped, grad_hu, preferred_element_type=jnp.float32)
    grad_rows = jnp.einsum("sxcf,xdf->sxcd", grad_hg, w_gate, preferred_element_type=jnp.float32)
    grad_rows = grad_rows + jnp.einsum(
        "sxcf,xdf->sxcd", grad_hu, w_up, preferred_element_type=jnp.float32
    )
    grad_rows = grad_rows.astype(jnp.bfloat16).reshape(expert_count, capacity, model_width)
    grad_home = lax.all_to_all(grad_rows, ("expert", "dp"), split_axis=0, concat_axis=0, tiled=True)
    grad_n_second = jnp.sum(collect_rows(grad_home).astype(jnp.float32), axis=1)
    grad_logits = gate_pull(grad_gate_values)[0].astype(jnp.bfloat16)
    grad_w_router = jnp.einsum(
        "td,te->de", n_second, grad_logits, preferred_element_type=jnp.float32
    )
    grad_n_second = grad_n_second + jnp.einsum(
        "te,de->td", grad_logits, w_router, preferred_element_type=jnp.float32
    )
    _, norm_second_pull = jax.vjp(normalize, y_mid, gain_moe)
    grad_mid_norm, grad_gain_moe = norm_second_pull(grad_n_second)
    grad_mid = grad_out + grad_mid_norm
    grad_branch = grad_mid.astype(jnp.bfloat16)
    grad_w_out = jnp.einsum("td,te->de", attn_low, grad_branch, preferred_element_type=jnp.float32)
    grad_heads = jnp.einsum(
        "te,de->td", grad_branch, w_out, preferred_element_type=jnp.float32
    ).astype(jnp.bfloat16)
    key_again, value_again = (
        lax.all_gather(key_rows, "context", axis=0, tiled=True),
        lax.all_gather(value_rows, "context", axis=0, tiled=True),
    )
    grad_query, grad_key_all, grad_value_all = attention_backward(
        query,
        key_again,
        value_again,
        positions,
        scale,
        block,
        top_score,
        total,
        grad_heads.reshape(row_count, KV_HEADS, group, HEAD_DIM),
        attn_full,
    )
    grad_key_rot, grad_value_rows = (
        lax.psum_scatter(
            grad_key_all.astype(jnp.bfloat16), "context", scatter_dimension=0, tiled=True
        ).astype(jnp.float32),
        lax.psum_scatter(
            grad_value_all.astype(jnp.bfloat16), "context", scatter_dimension=0, tiled=True
        ).astype(jnp.float32),
    )
    grad_q_raw = rotate(grad_query.reshape(row_count, HEADS, HEAD_DIM), cosine, -sine)
    grad_q_raw = grad_q_raw.astype(jnp.bfloat16).reshape(row_count, model_width)
    grad_k_raw = rotate(grad_key_rot.reshape(row_count, KV_HEADS, HEAD_DIM), cosine, -sine)
    grad_k_raw = grad_k_raw.astype(jnp.bfloat16).reshape(row_count, kv_width)
    grad_v_raw = grad_value_rows.astype(jnp.bfloat16)
    grad_w_query = jnp.einsum("td,te->de", n_first, grad_q_raw, preferred_element_type=jnp.float32)
    grad_w_key = jnp.einsum("td,te->de", n_first, grad_k_raw, preferred_element_type=jnp.float32)
    grad_w_value = jnp.einsum("td,te->de", n_first, grad_v_raw, preferred_element_type=jnp.float32)
    grad_n_first = jnp.einsum("te,de->td", grad_q_raw, w_query, preferred_element_type=jnp.float32)
    grad_n_first = grad_n_first + jnp.einsum(
        "te,de->td", grad_k_raw, w_key, preferred_element_type=jnp.float32
    )
    grad_n_first = grad_n_first + jnp.einsum(
        "te,de->td", grad_v_raw, w_value, preferred_element_type=jnp.float32
    )
    _, norm_first_pull = jax.vjp(normalize, x_rows, gain_attn)
    grad_x_norm, grad_gain_attn = norm_first_pull(grad_n_first)
    grad_input = grad_mid + grad_x_norm
    halves = lambda rows: rows.reshape(row_count, 2, -1).transpose(1, 0, 2)
    grad_kv = jnp.stack(
        [grad_k_raw.reshape(row_count, 2, 2, 128), grad_v_raw.reshape(row_count, 2, 2, 128)],
        axis=3,
    )
    grad_kv = grad_kv.transpose(1, 0, 2, 3, 4).reshape(2, row_count, kv_width)
    narrow = jnp.concatenate(
        [grad_w_router, grad_gain_attn[:, None], grad_gain_moe[:, None],
         jnp.zeros((model_width, 94), jnp.float32)], axis=1).astype(jnp.bfloat16)
    blocks = lambda grads: grads.astype(jnp.bfloat16).reshape(local_experts, 2, 4, 192, -1)
    sums = reduce_gradients(
        n_first, attn_low, halves(grad_q_raw), grad_kv, halves(grad_branch), narrow,
        blocks(grad_w_gate), blocks(grad_w_up), blocks(grad_w_down),
    )
    return (
        y_out.astype(jnp.bfloat16)[None],
        grad_input[None],
        sums[0],
        sums[1],
        sums[2],
        sums[3],
        sums[4][:, 32],
        sums[4][:, 33],
        sums[4][:, :32],
        sums[5],
        sums[6],
        sums[7].transpose(0, 2, 1),
    )


def solution(mesh):
    in_specs = (
        P(("expert", "dp"), "context", None),
        P(("expert", "dp"), "context", None),
        P(),
        P(),
        P(),
        P(),
        P(),
        P(),
        P(),
        P(("expert", "dp"), None, None),
        P(("expert", "dp"), None, None),
        P(("expert", "dp"), None, None),
        P(("expert", "dp"), "context", None),
    )
    out_specs = (
        P(("expert", "dp"), "context", None),
        P(("expert", "dp"), "context", None),
        P(("context", "dp"), None),
        P(("context", "dp"), None),
        P(("context", "dp"), None),
        P(("context", "dp"), None),
        P(("context", "dp")),
        P(("context", "dp")),
        P(("context", "dp"), None),
        P(("expert", "dp"), "context", None),
        P(("expert", "dp"), "context", None),
        P(("expert", "dp"), None, "context"),
    )
    return jax.shard_map(shards, mesh=mesh, in_specs=in_specs, out_specs=out_specs, check_vma=False)
```

```python
import functools
import math

import jax
import jax.numpy as jnp
from jax import lax
from jax.experimental import pallas as pl
from jax.experimental.pallas import tpu as pltpu
from jax.sharding import PartitionSpec as P

MESH = pl.DeviceIdType.MESH
BF = jnp.bfloat16
F32 = jnp.float32


class Place:
    def __init__(self):
        e, c = lax.axis_index("expert"), lax.axis_index("context")
        self.hi, self.core = e // 2, e % 2
        self.lo, self.y = c // 4, c % 4
        self.z = lax.axis_index("dp")

    def at(self, hi=0, core=0, lo=0, y=0, z=0):
        e = (self.hi + hi) % 2 * 2 + (self.core + core) % 2
        c = (self.lo + lo) % 2 * 4 + (self.y + y) % 4
        return (e, c, (self.z + z) % 4)

    def line(self, axis):
        if axis == "y":
            return [((self.y + d) % 4, self.at(y=d)) for d in (1, 2, 3)]
        if axis == "z":
            return [((self.z + d) % 4, self.at(z=d)) for d in (1, 2, 3)]
        return [
            ((self.hi + a) % 2 * 2 + (self.lo + b) % 2, self.at(hi=a, lo=b))
            for a, b in ((0, 1), (1, 0), (1, 1))
        ]

    def own(self, axis):
        return {"y": self.y, "z": self.z, "x": self.hi * 2 + self.lo}[axis]


def greet(devices):
    barrier = pltpu.get_barrier_semaphore()
    for device in devices:
        pl.semaphore_signal(barrier, inc=1, device_id=device, device_id_type=MESH)
    pl.semaphore_wait(barrier, len(devices))


def send(src, dst, sems, device):
    copy = pltpu.make_async_remote_copy(
        src_ref=src, dst_ref=dst, send_sem=sems[0], recv_sem=sems[1],
        device_id=device, device_id_type=MESH,
    )
    copy.start()
    return copy


def scatter_start(place, axis, src, landing, sems, begin):
    copies = []
    for d, (index, device) in enumerate(place.line(axis)):
        pair = (sems.at[0, begin + d], sems.at[1, begin + d])
        copies.append(send(src.at[index], landing.at[d], pair, device))
    return copies


def add_up(out, own, landing, lead):
    count = landing.shape[0]

    def body(i, carry):
        total = own[i].astype(F32)
        for d in range(count):
            total = total + landing[d, i].astype(F32)
        out[i] = total.astype(out.dtype)
        return carry

    lax.fori_loop(0, lead, body, 0)


def group_peers(place):
    return {
        (c, h, d): place.at(core=c, hi=h, z=d)
        for c in (0, 1) for h in (0, 1) for d in range(4) if (c, h, d) != (0, 0, 0)
    }


def group_index(place, core=0, hi=0, z=0):
    return ((place.hi + hi) % 2 * 2 + (place.core + core) % 2) * 4 + (place.z + z) % 4


class Spread:
    def __init__(self, place, held, sems):
        self.place, self.held, self.sems = place, held, sems
        self.sent, self.waits = [], {}

    def pair(self, c, h, d):
        slot = c * 8 + h * 4 + d
        return (self.sems.at[0, slot], self.sems.at[1, slot])

    def push(self, origin, target, slot):
        c, h, d = target
        index = group_index(self.place, hi=origin[0], z=origin[1])
        block = self.held.at[index]
        copy = send(block, block, self.pair(*slot), self.place.at(core=c, hi=h, z=d))
        self.sent.append(copy)
        self.waits[slot] = copy

    def land(self, slot):
        self.waits[slot].wait_recv()

    def first(self):
        for d in (1, 3, 2):
            self.push((0, 0), (0, 0, d), (0, 0, (4 - d) % 4))
        self.push((0, 0), (0, 1, 0), (0, 1, 0))
        self.push((0, 0), (1, 0, 0), (1, 0, 0))

    def relay(self):
        self.land((0, 1, 0))
        for d in (1, 3):
            self.push((1, 0), (0, 0, d), (0, 1, (4 - d) % 4))
        self.push((1, 0), (1, 0, 0), (1, 1, 0))
        self.land((0, 0, 2))
        self.push((0, 2), (0, 1, 0), (0, 1, 2))
        self.push((0, 2), (1, 0, 0), (1, 0, 2))
        for d in (1, 3):
            self.land((0, 0, d))
            self.push((0, d), (1, 0, 0), (1, 0, d))

    def finish_near(self):
        for d in range(4):
            self.land((1, 0, d))

    def relay_far(self):
        for d in (1, 3, 2):
            self.land((0, 1, d))
            self.push((1, d), (1, 0, 0), (1, 1, d))

    def finish_far(self):
        for d in range(4):
            self.land((1, 1, d))

    def drain(self):
        for copy in self.sent:
            copy.wait_send()


def add_rows(out, terms):
    def body(i, carry):
        part = pl.ds(pl.multiple_of(i * 16, 16), 16)
        total = terms[0][part].astype(F32)
        for term in terms[1:]:
            total = total + term[part].astype(F32)
        out[part] = total.astype(out.dtype)
        return carry

    lax.fori_loop(0, 8, body, 0)


class Gather:
    def __init__(self, place, parts, pool, landing, sems, own=None):
        self.place, self.parts, self.pool, self.landing, self.sems = place, parts, pool, landing, sems
        self.own = own
        self.sent = []

    def pair(self, slot):
        return (self.sems.at[0, slot], self.sems.at[1, slot])

    def push(self, src, dst, slot, device):
        copy = send(src, dst, self.pair(slot), device)
        self.sent.append(copy)
        return copy

    def swap(self, hi):
        half = (self.place.hi + hi) % 2
        start = group_index(self.place, core=1, hi=hi) - self.place.z
        return self.push(
            self.parts.at[pl.ds(start, 4)], self.pool.at[pl.ds(half * 4, 4)], hi, self.place.at(core=1)
        )

    def chunk(self, hi, z):
        return self.pool.at[(self.place.hi + hi) % 2 * 4 + (self.place.z + z) % 4]

    def mine(self, hi, z):
        if self.own is not None:
            return self.own.at[(self.place.hi + hi) % 2 * 4 + (self.place.z + z) % 4]
        return self.parts.at[group_index(self.place, hi=hi, z=z)]

    def join(self, hi, z, more=()):
        block = self.chunk(hi, z)
        add_rows(block, [block, self.mine(hi, z), *more])
        return block

    def first(self):
        place, land = self.place, self.landing
        self.cross, self.direct = [], []
        for i, d in enumerate((1, 3)):
            self.cross.append(self.push(self.join(1, d), land.at[i], 2 + i, place.at(z=d)))
        self.far = self.push(self.join(1, 2), land.at[2], 4, place.at(hi=1))
        for i, d in enumerate((1, 3)):
            self.direct.append(self.push(self.join(0, d), land.at[3 + i], 5 + i, place.at(z=d)))

    def second(self):
        place, land = self.place, self.landing
        for copy in self.cross:
            copy.wait_recv()
        block = self.join(1, 0, [land.at[0], land.at[1]])
        self.last = [self.push(block, land.at[5], 7, place.at(hi=1))]
        self.far.wait_recv()
        block = self.join(0, 2, [land.at[2]])
        self.last.append(self.push(block, land.at[6], 8, place.at(z=2)))

    def finish(self, out):
        for copy in self.direct + self.last:
            copy.wait_recv()
        land = self.landing
        add_rows(out, [self.chunk(0, 0), self.mine(0, 0), land.at[3], land.at[4], land.at[5], land.at[6]])

    def drain(self):
        for copy in self.sent:
            copy.wait_send()


def contract(left, right, dims):
    return lax.dot_general(left, right, (dims, ((), ())), preferred_element_type=F32)


def expert_kernel(
    n2, cot, table, wg, wu, wd,
    dn2, dgate, eo, eg, eu, ed,
    rows, cots, tables, table_sems, rows_sems, cots_sems,
    x_rows, c_rows, pick, gate, dhg, dhu, gact, dg, drow,
    pool, landing, gather_sems, dgate_out, dgate_sems, stage, stage_sems,
):
    place = Place()
    peers = group_peers(place)
    greet(list(peers.values()))
    me = group_index(place)

    small = []
    tables[me] = table[me]
    for (c, h, d), device in peers.items():
        slot = c * 8 + h * 4 + d
        pair = (table_sems.at[0, slot], table_sems.at[1, c * 8 + h * 4 + (4 - d) % 4])
        small.append(send(table.at[group_index(place, c, h, d)], tables.at[me], pair, device))
    rows[me] = n2[...]
    cots[me] = cot[...]
    spread_rows = Spread(place, rows, rows_sems)
    spread_cots = Spread(place, cots, cots_sems)
    spread_rows.first()
    spread_cots.first()
    spread_rows.relay()
    spread_cots.relay()
    for copy in small:
        copy.wait_recv()

    slots = lax.broadcasted_iota(jnp.int32, (80, 256), 0).astype(F32)
    second = lax.broadcasted_iota(jnp.int32, (1, 256), 1) >= 128

    def select(pair_index):
        parts = []
        for e in range(2):
            here = jnp.concatenate(
                [tables[pair_index * 2, e : e + 1, :], tables[pair_index * 2 + 1, e : e + 1, :]], axis=1
            )
            here = jnp.where(here < 0.0, -1000.0, here + jnp.where(second, 40.0, 0.0))
            weight = jnp.concatenate(
                [tables[pair_index * 2, 2 + e : 3 + e, :], tables[pair_index * 2 + 1, 2 + e : 3 + e, :]],
                axis=1,
            )
            hit = slots == here
            parts.append(jnp.where(hit, 1.0, 0.0).astype(BF))
            place_rows = pl.ds(pl.multiple_of(pair_index * 80, 80), 80)
            gate[e, place_rows, :] = jnp.sum(jnp.where(hit, weight, 0.0), axis=1, keepdims=True)
        pick[pair_index] = jnp.concatenate(parts, axis=0)

    def pull(pair_index, held, out):
        both = jnp.concatenate([held[pair_index * 2], held[pair_index * 2 + 1]], axis=0)
        picked = contract(pick[pair_index], both, ((1,), (0,))).astype(BF)
        place_rows = pl.ds(pl.multiple_of(pair_index * 80, 80), 80)
        out[0, place_rows, :] = picked[0:80]
        out[1, place_rows, :] = picked[80:160]

    def all_pairs(body):
        def step(i, carry):
            body(i)
            return carry
        lax.fori_loop(0, 8, step, 0)

    all_pairs(select)

    def pull_side(c, h, held, out):
        start = group_index(place, core=c, hi=h) - place.z
        base = start // 2

        def step(i, carry):
            pull(base + i, held, out)
            return carry

        lax.fori_loop(0, 2, step, 0)

    spread_rows.finish_near()
    pull_side(0, 0, rows, x_rows)
    pull_side(1, 0, rows, x_rows)
    spread_rows.relay_far()
    pull_side(0, 1, rows, x_rows)
    spread_rows.finish_far()
    pull_side(1, 1, rows, x_rows)
    spread_cots.finish_near()
    pull_side(0, 0, cots, c_rows)
    pull_side(1, 0, cots, c_rows)
    spread_cots.relay_far()
    pull_side(0, 1, cots, c_rows)
    spread_cots.finish_far()
    pull_side(1, 1, cots, c_rows)

    def work(i, carry):
        e, m = i // 2, i % 2
        part = pl.ds(pl.multiple_of(m * 320, 320), 320)
        x = x_rows[e, part, :]
        hg = contract(x, wg[e], ((1,), (0,)))
        hu = contract(x, wu[e], ((1,), (0,)))
        back = contract(c_rows[e, part, :], wd[e], ((1,), (1,)))
        weight = gate[e, part, :]
        sig = 1.0 / (1.0 + jnp.exp(-hg))
        silu = hg * sig
        act = silu * hu
        dg[e, part, :] = jnp.sum(act * back, axis=1, keepdims=True)
        gact[e, part, :] = (weight * act).astype(BF)
        dact = weight * back
        low_hg = (dact * hu * (sig + silu * (1.0 - sig))).astype(BF)
        low_hu = (dact * silu).astype(BF)
        dhg[e, part, :] = low_hg
        dhu[e, part, :] = low_hu
        back_rows = (
            contract(low_hg, wg[e], ((1,), (1,))) + contract(low_hu, wu[e], ((1,), (1,)))
        ).astype(BF)
        for j in range(4):
            drow[m * 4 + j, pl.ds(pl.multiple_of(e * 80, 80), 80), :] = back_rows[j * 80 : (j + 1) * 80]
        return carry

    lax.fori_loop(0, 4, work, 0)
    spread_rows.drain()
    spread_cots.drain()

    def put_back(pair_index, out):
        both = contract(pick[pair_index], drow[pair_index], ((0,), (0,))).astype(BF)
        out[pair_index * 2] = both[0:128]
        out[pair_index * 2 + 1] = both[128:256]

    def put_side(c, h, out):
        base = (group_index(place, core=c, hi=h) - place.z) // 2

        def step(i, carry):
            put_back(base + i, out)
            return carry

        lax.fori_loop(0, 2, step, 0)

    home = Gather(place, rows, pool, landing, gather_sems)
    put_side(1, 1, rows)
    swaps = [home.swap(1)]
    put_side(1, 0, rows)
    swaps.append(home.swap(0))

    def gate_grads(pair_index):
        chosen = pick[pair_index].astype(F32)
        for e in range(2):
            column = dg[e, pl.ds(pl.multiple_of(pair_index * 80, 80), 80), :]
            line = jnp.sum(chosen[e * 80 : (e + 1) * 80] * column, axis=0, keepdims=True)
            dgate_out[pair_index * 2, e : e + 1, :] = line[:, 0:128]
            dgate_out[pair_index * 2 + 1, e : e + 1, :] = line[:, 128:256]

    dgate_out[...] = jnp.zeros_like(dgate_out)
    all_pairs(gate_grads)
    small_back = []
    dgate[me] = dgate_out[me]
    for (c, h, d), device in peers.items():
        slot = c * 8 + h * 4 + d
        pair = (dgate_sems.at[0, slot], dgate_sems.at[1, c * 8 + h * 4 + (4 - d) % 4])
        small_back.append(send(dgate_out.at[group_index(place, c, h, d)], dgate.at[me], pair, device))
    put_side(0, 1, rows)
    swaps[0].wait_recv()
    put_side(0, 0, rows)
    swaps[1].wait_recv()
    home.first()

    def outputs(i, carry):
        e, m = i // 2, i % 2
        part = pl.ds(pl.multiple_of(m * 320, 320), 320)
        made = contract(gact[e, part, :], wd[e], ((1,), (0,))).astype(BF)
        for j in range(4):
            drow[m * 4 + j, pl.ds(pl.multiple_of(e * 80, 80), 80), :] = made[j * 80 : (j + 1) * 80]
        return carry

    lax.fori_loop(0, 4, outputs, 0)
    all_pairs(lambda p: put_back(p, cots))
    eo_copy = pltpu.make_async_copy(cots, eo, stage_sems.at[2])
    eo_copy.start()
    home.second()
    copies = {}
    step = 0
    for e in range(2):
        for left, right, out in ((x_rows, dhg, eg), (x_rows, dhu, eu), (c_rows, gact, ed)):
            slot = step % 2
            if step >= 2:
                copies[step - 2].wait()

            def weight_grad(i, carry):
                tile = pl.ds(pl.multiple_of(i * 256, 256), 256)
                stage[slot, tile, :] = contract(left[e, :, tile], right[e], ((0,), (0,))).astype(BF)
                return carry

            lax.fori_loop(0, 6, weight_grad, 0)
            copies[step] = pltpu.make_async_copy(stage.at[slot], out.at[e], stage_sems.at[slot])
            copies[step].start()
            step += 1
    home.finish(dn2)
    for copy in small_back:
        copy.wait_recv()
    for copy in small + small_back:
        copy.wait_send()
    home.drain()
    copies[4].wait()
    copies[5].wait()
    eo_copy.wait()


def run_experts(n2, cot, table, wg, wu, wd):
    vmem = pl.BlockSpec(memory_space=pltpu.VMEM)
    hbm = pl.BlockSpec(memory_space=pl.ANY)
    sems = pltpu.SemaphoreType.DMA
    low = lambda *shape: pltpu.VMEM(shape, BF)
    struct = jax.ShapeDtypeStruct
    return pl.pallas_call(
        expert_kernel,
        out_shape=(
            struct((128, 1536), F32), struct((16, 8, 128), F32), struct((16, 128, 1536), BF),
            struct((2, 1536, 512), BF), struct((2, 1536, 512), BF), struct((2, 1536, 512), BF),
        ),
        in_specs=[vmem] * 6,
        out_specs=[vmem, vmem, hbm, hbm, hbm, hbm],
        scratch_shapes=[
            low(16, 128, 1536), low(16, 128, 1536), pltpu.VMEM((16, 8, 128), F32),
            sems((2, 16)), sems((2, 16)), sems((2, 16)),
            low(2, 640, 1536), low(2, 640, 1536), low(8, 160, 256), pltpu.VMEM((2, 640, 1), F32),
            low(2, 640, 512), low(2, 640, 512), low(2, 640, 512), pltpu.VMEM((2, 640, 1), F32),
            low(8, 160, 1536),
            low(8, 128, 1536), low(7, 128, 1536), sems((2, 9)),
            pltpu.VMEM((16, 8, 128), F32), sems((2, 16)),
            low(2, 1536, 512), sems((3,)),
        ],
        compiler_params=pltpu.CompilerParams(
            collective_id=1, has_side_effects=True, vmem_limit_bytes=62 << 20
        ),
    )(n2, cot, table, wg, wu, wd)


WIDE = 384
ORDERS = {"o": "xyz", "q": "zyx", "s": "yzx"}


def stream_index(order, block, half):
    at = {"x": half * 2 + block // 16, "y": block // 4 % 4, "z": block % 4}
    return tuple(at[axis] for axis in order)


def fill_stream(out, order, left, right, width):
    for half in range(2):
        columns = right[:, half * width : (half + 1) * width]
        for tile in range(4):
            grads = lax.dot_general(
                left[:, tile * 384 : (tile + 1) * 384], columns,
                (((0,), (0,)), ((), ())), preferred_element_type=F32,
            ).astype(BF)
            for j in range(8):
                index = stream_index(order, tile * 8 + j, half)
                out[(*index, slice(None), slice(0, width))] = grads[j * 48 : (j + 1) * 48]


def reduce_kernel(
    n1, attn, dq, dkv, dbr, narrow, eo, eg, eu, ed,
    moe, gq, gk, gv, go, gs, og, ou, od,
    n1c, attnc, dqc, dkvc, dbrc, pair_sems,
    send_o, send_q, send_s, land1_o, land1_q, land1_s, mid_o, mid_q, mid_s,
    land2_o, land2_q, land2_s, last_o, last_q, last_s, land3_o, land3_q, land3_s, dense_sems,
    mine, quarters, quarter_sems,
    own_p, own_q, land_p1, land_q1, sum_p, sum_q, land_p2, land_q2, expert_sems, local_sems,
    eo_own, eo_pool, eo_landing, eo_sems, eo_local,
):
    place = Place()
    y_line, z_line, x_line = (place.line(axis) for axis in "yzx")
    sibling = place.at(core=1)
    cross = place.at(hi=1, core=1)
    greet([device for line in (y_line, z_line, x_line) for _, device in line] + [sibling, cross])
    pending = []

    pairs = []
    for i, (rows, both, part) in enumerate(
        ((attn, attnc, None), (dbr, dbrc, 1), (n1, n1c, None), (dq, dqc, 1), (dkv, dkvc, 1))
    ):
        source = rows if part is None else rows.at[1 - place.core]
        pair = (pair_sems.at[0, i], pair_sems.at[1, i])
        pairs.append(send(source, both.at[pl.ds(128, 128)], pair, sibling))
        both[0:128, :] = rows[...] if part is None else rows[place.core]

    mats = (eg, eu, ed)
    stage_p, stage_q = [], []
    other_lo = (place.lo + 1) % 2
    lo_device = place.at(lo=1)
    at = 0
    for m, mat in enumerate(mats):
        for d, (index, device) in enumerate(y_line):
            pair = (expert_sems.at[0, at], expert_sems.at[1, at])
            stage_p.append(send(mat.at[0, :, index], land_p1.at[d, m], pair, device))
            at += 1
        pair = (expert_sems.at[0, at], expert_sems.at[1, at])
        stage_q.append(send(mat.at[1, other_lo], land_q1.at[m], pair, lo_device))
        at += 1
    local = []
    for m, mat in enumerate(mats):
        local.append(pltpu.make_async_copy(mat.at[0, :, place.y], own_p.at[m], local_sems.at[0, m]))
        local.append(pltpu.make_async_copy(mat.at[1, place.lo], own_q.at[m], local_sems.at[1, m]))
    for copy in local:
        copy.start()

    home = Gather(place, eo, eo_pool, eo_landing, eo_sems, eo_own)
    swaps = [home.swap(1), home.swap(0)]
    own_rows = []
    for h in range(2):
        start = group_index(place, hi=h) - place.z
        half = (place.hi + h) % 2
        own_rows.append(
            pltpu.make_async_copy(
                eo.at[pl.ds(start, 4)], eo_own.at[pl.ds(half * 4, 4)], eo_local.at[h]
            )
        )
        own_rows[-1].start()

    sends = {"o": send_o, "q": send_q, "s": send_s}
    lands = {
        "o": (land1_o, land2_o, land3_o), "q": (land1_q, land2_q, land3_q),
        "s": (land1_s, land2_s, land3_s),
    }
    mids = {"o": (mid_o, last_o), "q": (mid_q, last_q), "s": (mid_s, last_s)}
    begin = {"o": 0, "q": 9, "s": 18}
    flight = {}

    def launch(name, phase):
        source = sends[name] if phase == 0 else mids[name][phase - 1]
        flight[name] = scatter_start(
            place, ORDERS[name][phase], source, lands[name][phase], dense_sems,
            begin[name] + 3 * phase,
        )

    def land(name, phase):
        for copy in flight[name]:
            copy.wait_recv()
        pending.extend(flight[name])
        source = sends[name] if phase == 0 else mids[name][phase - 1]
        own = source.at[place.own(ORDERS[name][phase])]
        landing = lands[name][phase]
        if phase == 0:
            out = mids[name][0]

            def body(i, carry):
                a, b = i // 4, i % 4
                total = own[a, b].astype(F32)
                for d in range(3):
                    total = total + landing[d, a, b].astype(F32)
                out[a, b] = total.astype(BF)
                return carry

            lax.fori_loop(0, 16, body, 0)
        elif phase == 1:
            add_up(mids[name][1], own, landing, 4)
        else:
            total = own[...].astype(F32)
            for d in range(3):
                total = total + landing[d].astype(F32)
            mine["oqs".index(name)] = total.astype(BF)

    for copy in pairs[:2]:
        copy.wait_recv()
    fill_stream(send_o, ORDERS["o"], attnc, dbrc, 384)
    launch("o", 0)
    for copy in pairs[2:4]:
        copy.wait_recv()
    fill_stream(send_q, ORDERS["q"], n1c, dqc, 384)
    launch("q", 0)
    pairs[4].wait_recv()
    fill_stream(send_s, ORDERS["s"], n1c, dkvc, 256)
    for block in range(32):
        for half in range(2):
            index = stream_index(ORDERS["s"], block, half)
            send_s[(*index, slice(None), slice(256, 384))] = narrow[block * 48 : (block + 1) * 48, :]
    launch("s", 0)
    pending.extend(pairs)
    for copy in swaps:
        copy.wait_recv()
    for copy in own_rows:
        copy.wait()
    home.first()
    for phase in range(3):
        if phase == 1:
            home.second()
        for name in "oqs":
            land(name, phase)
            if phase < 2:
                launch(name, phase + 1)

    own_quarter = place.core * 2 + place.hi
    gathered = []
    for i, (a, b) in enumerate(((0, 1), (1, 0), (1, 1))):
        pair = (quarter_sems.at[0, i], quarter_sems.at[1, i])
        gathered.append(send(mine, quarters.at[own_quarter], pair, place.at(hi=a, core=b)))
    quarters[own_quarter] = mine[...]

    for copy in stage_p + stage_q:
        copy.wait_recv()
    for copy in local:
        copy.wait()
    pending.extend(stage_p + stage_q)

    def fold_p(i, carry):
        m, lo, part = i // 8, i // 4 % 2, pl.ds(i % 4 * 48, 48)
        total = own_p[m, lo, part].astype(F32)
        for d in range(3):
            total = total + land_p1[d, m, lo, part].astype(F32)
        sum_p[lo, m, part] = total.astype(BF)
        return carry

    lax.fori_loop(0, 24, fold_p, 0)
    pair = (expert_sems.at[0, 12], expert_sems.at[1, 12])
    second = [send(sum_p.at[other_lo], land_p2, pair, lo_device)]

    def fold_q(i, carry):
        m, y, part = i // 16, i // 4 % 4, pl.ds(i % 4 * 48, 48)
        total = own_q[m, y, part].astype(F32) + land_q1[m, y, part].astype(F32)
        sum_q[y, m, part] = total.astype(BF)
        return carry

    lax.fori_loop(0, 48, fold_q, 0)
    for d, (index, device) in enumerate(y_line):
        pair = (expert_sems.at[0, 13 + d], expert_sems.at[1, 13 + d])
        second.append(send(sum_q.at[index], land_q2.at[d], pair, device))

    home.finish(moe)
    home.drain()
    for copy in gathered:
        copy.wait_recv()
    pending.extend(gathered)
    for q in range(4):
        go[:, q * 384 : (q + 1) * 384] = quarters[q, 0].astype(F32)
        gq[:, q * 384 : (q + 1) * 384] = quarters[q, 1].astype(F32)
        gk[:, q * 128 : (q + 1) * 128] = quarters[q, 2, :, 0:128].astype(F32)
        gv[:, q * 128 : (q + 1) * 128] = quarters[q, 2, :, 128:256].astype(F32)
    gs[...] = quarters[0, 2, :, 256:384].astype(F32) + quarters[2, 2, :, 256:384].astype(F32)

    for copy in second:
        copy.wait_recv()
    pending.extend(second)
    for m, out in enumerate((og, ou, od)):
        def finish(i, carry):
            part = pl.ds(i * 48, 48)
            out[0, part] = sum_p[place.lo, m, part].astype(F32) + land_p2[m, part].astype(F32)
            total = sum_q[place.y, m, part].astype(F32)
            for d in range(3):
                total = total + land_q2[d, m, part].astype(F32)
            out[1, part] = total
            return carry

        lax.fori_loop(0, 4, finish, 0)
    for copy in pending:
        copy.wait_send()


def reduce_gradients(n1, attn, dq, dkv, dbr, narrow, eo, eg, eu, ed):
    vmem = pl.BlockSpec(memory_space=pltpu.VMEM)
    sems = pltpu.SemaphoreType.DMA
    f32 = lambda *shape: jax.ShapeDtypeStruct(shape, F32)
    low = lambda *shape: pltpu.VMEM(shape, BF)
    streams = 3
    return pl.pallas_call(
        reduce_kernel,
        out_shape=(
            f32(128, 1536), f32(48, 1536), f32(48, 512), f32(48, 512), f32(48, 1536), f32(48, 128),
            f32(2, 192, 512), f32(2, 192, 512), f32(2, 192, 512),
        ),
        in_specs=[vmem] * 6 + [pl.BlockSpec(memory_space=pl.ANY)] * 4,
        out_specs=[vmem] * 9,
        scratch_shapes=[
            low(256, 1536), low(256, 1536), low(256, 768), low(256, 512), low(256, 768),
            sems((2, 5)),
            *[low(4, 4, 4, 48, WIDE)] * streams,
            *[low(3, 4, 4, 48, WIDE)] * streams,
            *[low(4, 4, 48, WIDE)] * streams,
            *[low(3, 4, 48, WIDE)] * streams,
            *[low(4, 48, WIDE)] * streams,
            *[low(3, 48, WIDE)] * streams,
            sems((2, 27)),
            low(3, 48, WIDE), low(4, 3, 48, WIDE), sems((2, 3)),
            low(3, 2, 192, 512), low(3, 4, 192, 512),
            low(3, 3, 2, 192, 512), low(3, 4, 192, 512),
            low(2, 3, 192, 512), low(4, 3, 192, 512),
            low(3, 192, 512), low(3, 3, 192, 512),
            sems((2, 16)), sems((2, 3)),
            low(8, 128, 1536), low(8, 128, 1536), low(7, 128, 1536), sems((2, 9)), sems((2,)),
        ],
        compiler_params=pltpu.CompilerParams(
            collective_id=0, has_side_effects=True, vmem_limit_bytes=60 << 20
        ),
    )(n1, attn, dq, dkv, dbr, narrow, eo, eg, eu, ed)


HEADS = 24
KV_HEADS = 8
HEAD_DIM = 64


epsilon = 1e-06
floor_score = -1e30


def normalize(values, gain):
    return values * lax.rsqrt(jnp.mean(values * values, axis=-1, keepdims=True) + epsilon) * gain


def rotary_tables(positions, half):
    index = lax.iota(jnp.float32, half)
    freqs = jnp.exp(index * (-math.log(10000.0) / half))
    angles = positions[:, None] * freqs[None, :]
    return (jnp.cos(angles)[:, None, :], jnp.sin(angles)[:, None, :])


def rotate(values, cosine, sine):
    half = values.shape[-1] // 2
    first = values[..., :half]
    second = values[..., half:]
    return jnp.concatenate(
        [first * cosine - second * sine, second * cosine + first * sine], axis=-1
    )


def block_scores(query, key_block, key_start, positions, scale):
    kv_count = query.shape[1]
    key_heads = key_block.reshape(key_block.shape[0], kv_count, -1)
    scores = (
        jnp.einsum("qkgd,skd->kgqs", query, key_heads, preferred_element_type=jnp.float32) * scale
    )
    key_positions = key_start + lax.iota(jnp.int32, key_block.shape[0])
    return jnp.where(
        key_positions[None, None, None, :] <= positions[None, None, :, None], scores, floor_score
    )


def split_blocks(key_all, value_all, block):
    count = key_all.shape[0] // block
    starts = lax.iota(jnp.int32, count) * block
    return (key_all.reshape(count, block, -1), value_all.reshape(count, block, -1), starts)


def attention_forward(query, key_all, value_all, positions, scale, block):
    key_blocks, value_blocks, starts = split_blocks(key_all, value_all, block)
    stat_shape = (query.shape[1], query.shape[2], query.shape[0])

    def gather_stats(carry, block_item):
        top_score, total = carry
        key_block, key_start = block_item
        scores = block_scores(query, key_block, key_start, positions, scale)
        new_top = jnp.maximum(top_score, jnp.max(scores, axis=-1))
        total = total * jnp.exp(top_score - new_top) + jnp.sum(
            jnp.exp(scores - new_top[..., None]), axis=-1
        )
        return ((new_top, total), None)

    start_stats = (
        jnp.full(stat_shape, floor_score, jnp.float32),
        jnp.zeros(stat_shape, jnp.float32),
    )
    (top_score, total), _ = lax.scan(gather_stats, start_stats, (key_blocks, starts))

    def weigh_values(accum, block_item):
        key_block, value_block, key_start = block_item
        scores = block_scores(query, key_block, key_start, positions, scale)
        probs = (jnp.exp(scores - top_score[..., None]) / total[..., None]).astype(jnp.bfloat16)
        value_heads = value_block.reshape(value_block.shape[0], query.shape[1], -1)
        return (
            accum
            + jnp.einsum("kgqs,skd->qkgd", probs, value_heads, preferred_element_type=jnp.float32),
            None,
        )

    accum, _ = lax.scan(
        weigh_values, jnp.zeros(query.shape, jnp.float32), (key_blocks, value_blocks, starts)
    )
    return (accum, top_score, total)


def attention_backward(
    query, key_all, value_all, positions, scale, block, top_score, total, grad_heads, attn_full
):
    key_blocks, value_blocks, starts = split_blocks(key_all, value_all, block)
    delta = jnp.einsum("qkgd,qkgd->kgq", grad_heads.astype(jnp.float32), attn_full)

    def block_grads(grad_query, block_item):
        key_block, value_block, key_start = block_item
        span = key_block.shape[0]
        scores = block_scores(query, key_block, key_start, positions, scale)
        probs = jnp.exp(scores - top_score[..., None]) / total[..., None]
        probs_low = probs.astype(jnp.bfloat16)
        key_heads = key_block.reshape(span, query.shape[1], -1)
        value_heads = value_block.reshape(span, query.shape[1], -1)
        grad_values = jnp.einsum(
            "kgqs,qkgd->skd", probs_low, grad_heads, preferred_element_type=jnp.float32
        )
        grad_probs = jnp.einsum(
            "qkgd,skd->kgqs", grad_heads, value_heads, preferred_element_type=jnp.float32
        )
        grad_scores = (probs * (grad_probs - delta[..., None])).astype(jnp.bfloat16)
        grad_query = (
            grad_query
            + jnp.einsum(
                "kgqs,skd->qkgd", grad_scores, key_heads, preferred_element_type=jnp.float32
            )
            * scale
        )
        grad_keys = (
            jnp.einsum("kgqs,qkgd->skd", grad_scores, query, preferred_element_type=jnp.float32)
            * scale
        )
        return (grad_query, (grad_keys.reshape(span, -1), grad_values.reshape(span, -1)))

    grad_query, (grad_keys, grad_values) = lax.scan(
        block_grads, jnp.zeros(query.shape, jnp.float32), (key_blocks, value_blocks, starts)
    )
    return (
        grad_query,
        grad_keys.reshape(key_all.shape[0], -1),
        grad_values.reshape(key_all.shape[0], -1),
    )


def shards(
    tokens,
    expert_ids,
    w_query,
    w_key,
    w_value,
    w_out,
    gain_attn,
    gain_moe,
    w_router,
    w_gate,
    w_up,
    w_down,
    cotangent,
):
    row_count = tokens.shape[1]
    model_width = tokens.shape[2]
    group = HEADS // KV_HEADS
    kv_width = KV_HEADS * HEAD_DIM
    route_count = expert_ids.shape[2]
    expert_count = w_router.shape[1]
    local_experts = w_gate.shape[0]
    capacity = row_count * route_count // expert_count + row_count * route_count // (
        4 * expert_count
    )
    scale = HEAD_DIM ** (-0.5)
    sources = lax.axis_size(("expert", "dp"))
    seq_length = row_count * lax.axis_size("context")
    block = min(512, seq_length)
    positions = lax.axis_index("context") * row_count + lax.iota(jnp.int32, row_count)
    cosine, sine = rotary_tables(positions.astype(jnp.float32), HEAD_DIM // 2)
    x_rows = tokens[0].astype(jnp.float32)
    route_ids = expert_ids[0]
    n_first = normalize(x_rows, gain_attn).astype(jnp.bfloat16)
    q_raw = jnp.dot(n_first, w_query, preferred_element_type=jnp.float32).reshape(
        row_count, HEADS, HEAD_DIM
    )
    k_raw = jnp.dot(n_first, w_key, preferred_element_type=jnp.float32).reshape(
        row_count, KV_HEADS, HEAD_DIM
    )
    value_rows = jnp.dot(n_first, w_value, preferred_element_type=jnp.float32).astype(jnp.bfloat16)
    query = (
        rotate(q_raw, cosine, sine)
        .astype(jnp.bfloat16)
        .reshape(row_count, KV_HEADS, group, HEAD_DIM)
    )
    key_rows = rotate(k_raw, cosine, sine).astype(jnp.bfloat16).reshape(row_count, kv_width)
    key_all, value_all = (
        lax.all_gather(key_rows, "context", axis=0, tiled=True),
        lax.all_gather(value_rows, "context", axis=0, tiled=True),
    )
    attn_full, top_score, total = attention_forward(
        query, key_all, value_all, positions, scale, block
    )
    attn_low = attn_full.reshape(row_count, model_width).astype(jnp.bfloat16)
    y_mid = x_rows + jnp.dot(attn_low, w_out, preferred_element_type=jnp.float32)
    n_second = normalize(y_mid, gain_moe).astype(jnp.bfloat16)
    logits = jnp.dot(n_second, w_router, preferred_element_type=jnp.float32)

    chosen = jnp.sum(
        (route_ids[:, :, None] == lax.iota(jnp.int32, expert_count)[None, None, :]).astype(
            jnp.float32
        ),
        axis=1,
    )
    gates = jax.nn.softmax(jnp.where(chosen > 0.0, logits, -jnp.inf), axis=-1)
    before = jnp.cumsum(chosen, axis=0) - chosen
    table = jnp.concatenate(
        [
            jnp.where(chosen > 0.0, before, -1.0).T.reshape(16, 2, row_count),
            gates.T.reshape(16, 2, row_count),
            jnp.zeros((16, 4, row_count), jnp.float32),
        ],
        axis=1,
    )
    grad_out = cotangent[0].astype(jnp.float32)
    grad_n_second, grad_gates, produced, grad_w_gate, grad_w_up, grad_w_down = run_experts(
        n_second, cotangent[0], table, w_gate, w_up, w_down
    )
    grad_gates = grad_gates[:, :2].reshape(expert_count, row_count).T
    grad_logits = (
        gates * (grad_gates - jnp.sum(gates * grad_gates, axis=-1, keepdims=True))
    ).astype(jnp.bfloat16)
    grad_w_router = jnp.einsum(
        "td,te->de", n_second, grad_logits, preferred_element_type=jnp.float32
    )
    grad_n_second = grad_n_second + jnp.einsum(
        "te,de->td", grad_logits, w_router, preferred_element_type=jnp.float32
    )
    _, norm_second_pull = jax.vjp(normalize, y_mid, gain_moe)
    grad_mid_norm, grad_gain_moe = norm_second_pull(grad_n_second)
    grad_mid = grad_out + grad_mid_norm
    grad_branch = grad_mid.astype(jnp.bfloat16)
    grad_w_out = jnp.einsum("td,te->de", attn_low, grad_branch, preferred_element_type=jnp.float32)
    grad_heads = jnp.einsum(
        "te,de->td", grad_branch, w_out, preferred_element_type=jnp.float32
    ).astype(jnp.bfloat16)
    key_again, value_again = (
        lax.all_gather(key_rows, "context", axis=0, tiled=True),
        lax.all_gather(value_rows, "context", axis=0, tiled=True),
    )
    grad_query, grad_key_all, grad_value_all = attention_backward(
        query,
        key_again,
        value_again,
        positions,
        scale,
        block,
        top_score,
        total,
        grad_heads.reshape(row_count, KV_HEADS, group, HEAD_DIM),
        attn_full,
    )
    grad_key_rot, grad_value_rows = (
        lax.psum_scatter(
            grad_key_all.astype(jnp.bfloat16), "context", scatter_dimension=0, tiled=True
        ).astype(jnp.float32),
        lax.psum_scatter(
            grad_value_all.astype(jnp.bfloat16), "context", scatter_dimension=0, tiled=True
        ).astype(jnp.float32),
    )
    grad_q_raw = rotate(grad_query.reshape(row_count, HEADS, HEAD_DIM), cosine, -sine)
    grad_q_raw = grad_q_raw.astype(jnp.bfloat16).reshape(row_count, model_width)
    grad_k_raw = rotate(grad_key_rot.reshape(row_count, KV_HEADS, HEAD_DIM), cosine, -sine)
    grad_k_raw = grad_k_raw.astype(jnp.bfloat16).reshape(row_count, kv_width)
    grad_v_raw = grad_value_rows.astype(jnp.bfloat16)
    grad_w_query = jnp.einsum("td,te->de", n_first, grad_q_raw, preferred_element_type=jnp.float32)
    grad_w_key = jnp.einsum("td,te->de", n_first, grad_k_raw, preferred_element_type=jnp.float32)
    grad_w_value = jnp.einsum("td,te->de", n_first, grad_v_raw, preferred_element_type=jnp.float32)
    grad_n_first = jnp.einsum("te,de->td", grad_q_raw, w_query, preferred_element_type=jnp.float32)
    grad_n_first = grad_n_first + jnp.einsum(
        "te,de->td", grad_k_raw, w_key, preferred_element_type=jnp.float32
    )
    grad_n_first = grad_n_first + jnp.einsum(
        "te,de->td", grad_v_raw, w_value, preferred_element_type=jnp.float32
    )
    _, norm_first_pull = jax.vjp(normalize, x_rows, gain_attn)
    grad_x_norm, grad_gain_attn = norm_first_pull(grad_n_first)
    grad_input = grad_mid + grad_x_norm
    halves = lambda rows: rows.reshape(row_count, 2, -1).transpose(1, 0, 2)
    grad_kv = jnp.stack(
        [grad_k_raw.reshape(row_count, 2, 2, 128), grad_v_raw.reshape(row_count, 2, 2, 128)],
        axis=3,
    )
    grad_kv = grad_kv.transpose(1, 0, 2, 3, 4).reshape(2, row_count, kv_width)
    narrow = jnp.concatenate(
        [grad_w_router, grad_gain_attn[:, None], grad_gain_moe[:, None],
         jnp.zeros((model_width, 94), jnp.float32)], axis=1).astype(jnp.bfloat16)
    blocks = lambda grads: grads.reshape(local_experts, 2, 4, 192, -1)
    sums = reduce_gradients(
        n_first, attn_low, halves(grad_q_raw), grad_kv, halves(grad_branch), narrow, produced,
        blocks(grad_w_gate), blocks(grad_w_up), blocks(grad_w_down),
    )
    y_out = y_mid + sums[0]
    return (
        y_out.astype(jnp.bfloat16)[None],
        grad_input[None],
        sums[1],
        sums[2],
        sums[3],
        sums[4],
        sums[5][:, 32],
        sums[5][:, 33],
        sums[5][:, :32],
        sums[6],
        sums[7],
        sums[8].transpose(0, 2, 1),
    )


def solution(mesh):
    in_specs = (
        P(("expert", "dp"), "context", None),
        P(("expert", "dp"), "context", None),
        P(),
        P(),
        P(),
        P(),
        P(),
        P(),
        P(),
        P(("expert", "dp"), None, None),
        P(("expert", "dp"), None, None),
        P(("expert", "dp"), None, None),
        P(("expert", "dp"), "context", None),
    )
    out_specs = (
        P(("expert", "dp"), "context", None),
        P(("expert", "dp"), "context", None),
        P(("context", "dp"), None),
        P(("context", "dp"), None),
        P(("context", "dp"), None),
        P(("context", "dp"), None),
        P(("context", "dp")),
        P(("context", "dp")),
        P(("context", "dp"), None),
        P(("expert", "dp"), "context", None),
        P(("expert", "dp"), "context", None),
        P(("expert", "dp"), None, "context"),
    )
    return jax.shard_map(shards, mesh=mesh, in_specs=in_specs, out_specs=out_specs, check_vma=False)
```

```python
import math

import jax
import jax.numpy as jnp
from jax import lax
from jax.experimental import pallas as pl
from jax.experimental.pallas import tpu as pltpu
from jax.sharding import PartitionSpec as P

epsilon = 1e-06
floor_score = -1e30
MESH = pl.DeviceIdType.MESH
BF = jnp.bfloat16
F32 = jnp.float32


class Place:
    def __init__(self):
        e, c = lax.axis_index("expert"), lax.axis_index("context")
        self.hi, self.core = e // 2, e % 2
        self.lo, self.y = c // 4, c % 4
        self.z = lax.axis_index("dp")

    def at(self, hi=0, core=0, lo=0, y=0, z=0):
        e = (self.hi + hi) % 2 * 2 + (self.core + core) % 2
        c = (self.lo + lo) % 2 * 4 + (self.y + y) % 4
        return (e, c, (self.z + z) % 4)

    def line(self, axis):
        if axis == "y":
            return [((self.y + d) % 4, self.at(y=d)) for d in (1, 2, 3)]
        if axis == "z":
            return [((self.z + d) % 4, self.at(z=d)) for d in (1, 2, 3)]
        return [
            ((self.hi + a) % 2 * 2 + (self.lo + b) % 2, self.at(hi=a, lo=b))
            for a, b in ((0, 1), (1, 0), (1, 1))
        ]

    def own(self, axis):
        return {"y": self.y, "z": self.z, "x": self.hi * 2 + self.lo}[axis]


def greet(devices):
    barrier = pltpu.get_barrier_semaphore()
    for device in devices:
        pl.semaphore_signal(barrier, inc=1, device_id=device, device_id_type=MESH)
    pl.semaphore_wait(barrier, len(devices))


def send(src, dst, sems, device):
    copy = pltpu.make_async_remote_copy(
        src_ref=src, dst_ref=dst, send_sem=sems[0], recv_sem=sems[1],
        device_id=device, device_id_type=MESH,
    )
    copy.start()
    return copy


def scatter_start(place, axis, src, landing, sems, begin):
    copies = []
    for d, (index, device) in enumerate(place.line(axis)):
        pair = (sems.at[0, begin + d], sems.at[1, begin + d])
        copies.append(send(src.at[index], landing.at[d], pair, device))
    return copies


def add_up(out, own, landing, lead):
    count = landing.shape[0]

    def body(i, carry):
        total = own[i].astype(F32)
        for d in range(count):
            total = total + landing[d, i].astype(F32)
        out[i] = total.astype(out.dtype)
        return carry

    lax.fori_loop(0, lead, body, 0)


def roll_lanes(u, shift):
    return pltpu.roll(u, shift, 1)


def swap_halves(u):
    lane = lax.broadcasted_iota(jnp.int32, u.shape, 1)
    return jnp.where(lane % 64 < 32, roll_lanes(u, 96), roll_lanes(u, 32))


def to_pairs(blocks):
    a, b, c = blocks
    low = lax.broadcasted_iota(jnp.int32, a.shape, 1) < 64
    return [
        jnp.where(low, a, b), jnp.where(low, roll_lanes(a, 64), roll_lanes(c, 64)), jnp.where(low, b, c)
    ]


def from_pairs(blocks):
    a, b, c = blocks
    low = lax.broadcasted_iota(jnp.int32, a.shape, 1) < 64
    turned = roll_lanes(b, 64)
    return [jnp.where(low, a, turned), jnp.where(low, c, a), jnp.where(low, turned, c)]


def inverse_root(values):
    return lax.rsqrt(jnp.mean(values * values, axis=-1, keepdims=True) + epsilon)


def visible(place, start, rows):
    key = lax.broadcasted_iota(jnp.int32, (rows, 384), 0) + start
    query = lax.broadcasted_iota(jnp.int32, (rows, 384), 1) % 128
    return key <= query + (place.lo * 4 + place.y) * 128


def half_mask(s):
    lane = lax.broadcasted_iota(jnp.int32, (1, 128), 1)
    return jnp.where((lane >= 64) == (s == 1), 1.0, 0.0).astype(BF)


def group_peers(place):
    return {
        (c, h, d): place.at(core=c, hi=h, z=d)
        for c in (0, 1) for h in (0, 1) for d in range(4) if (c, h, d) != (0, 0, 0)
    }


def group_index(place, core=0, hi=0, z=0):
    return ((place.hi + hi) % 2 * 2 + (place.core + core) % 2) * 4 + (place.z + z) % 4


class Spread:
    def __init__(self, place, held, sems):
        self.place, self.held, self.sems = place, held, sems
        self.sent, self.waits = [], {}

    def pair(self, c, h, d):
        slot = c * 8 + h * 4 + d
        return (self.sems.at[0, slot], self.sems.at[1, slot])

    def push(self, origin, target, slot):
        c, h, d = target
        index = group_index(self.place, hi=origin[0], z=origin[1])
        block = self.held.at[index]
        copy = send(block, block, self.pair(*slot), self.place.at(core=c, hi=h, z=d))
        self.sent.append(copy)
        self.waits[slot] = copy

    def land(self, slot):
        self.waits[slot].wait_recv()

    def first(self):
        for d in (1, 3, 2):
            self.push((0, 0), (0, 0, d), (0, 0, (4 - d) % 4))
        self.push((0, 0), (0, 1, 0), (0, 1, 0))
        self.push((0, 0), (1, 0, 0), (1, 0, 0))

    def relay_a(self):
        self.land((0, 1, 0))
        for d in (1, 3):
            self.push((1, 0), (0, 0, d), (0, 1, (4 - d) % 4))
        self.push((1, 0), (1, 0, 0), (1, 1, 0))

    def relay_b(self):
        self.land((0, 0, 2))
        self.push((0, 2), (0, 1, 0), (0, 1, 2))
        self.push((0, 2), (1, 0, 0), (1, 0, 2))
        for d in (1, 3):
            self.land((0, 0, d))
            self.push((0, d), (1, 0, 0), (1, 0, d))

    def finish_near(self):
        for d in range(4):
            self.land((1, 0, d))

    def relay_far(self):
        for d in (1, 3, 2):
            self.land((0, 1, d))
            self.push((1, d), (1, 0, 0), (1, 1, d))

    def finish_far(self):
        for d in range(4):
            self.land((1, 1, d))

    def drain(self):
        for copy in self.sent:
            copy.wait_send()


def add_rows(out, terms):
    def body(i, carry):
        part = pl.ds(pl.multiple_of(i * 16, 16), 16)
        total = terms[0][part].astype(F32)
        for term in terms[1:]:
            total = total + term[part].astype(F32)
        out[part] = total.astype(out.dtype)
        return carry

    lax.fori_loop(0, 8, body, 0)


class Gather:
    def __init__(self, place, parts, pool, landing, sems, own=None):
        self.place, self.parts, self.pool, self.landing, self.sems = place, parts, pool, landing, sems
        self.own = own
        self.sent = []

    def pair(self, slot):
        return (self.sems.at[0, slot], self.sems.at[1, slot])

    def push(self, src, dst, slot, device):
        copy = send(src, dst, self.pair(slot), device)
        self.sent.append(copy)
        return copy

    def swap(self, hi):
        half = (self.place.hi + hi) % 2
        start = group_index(self.place, core=1, hi=hi) - self.place.z
        return self.push(
            self.parts.at[pl.ds(start, 4)], self.pool.at[pl.ds(half * 4, 4)], hi, self.place.at(core=1)
        )

    def chunk(self, hi, z):
        return self.pool.at[(self.place.hi + hi) % 2 * 4 + (self.place.z + z) % 4]

    def mine(self, hi, z):
        if self.own is not None:
            return self.own.at[(self.place.hi + hi) % 2 * 4 + (self.place.z + z) % 4]
        return self.parts.at[group_index(self.place, hi=hi, z=z)]

    def join(self, hi, z, more=()):
        block = self.chunk(hi, z)
        add_rows(block, [block, self.mine(hi, z), *more])
        return block

    def first(self):
        place, land = self.place, self.landing
        self.cross, self.direct = [], []
        for i, d in enumerate((1, 3)):
            self.cross.append(self.push(self.join(1, d), land.at[i], 2 + i, place.at(z=d)))
        self.far = self.push(self.join(1, 2), land.at[2], 4, place.at(hi=1))
        for i, d in enumerate((1, 3)):
            self.direct.append(self.push(self.join(0, d), land.at[3 + i], 5 + i, place.at(z=d)))

    def second(self):
        place, land = self.place, self.landing
        for copy in self.cross:
            copy.wait_recv()
        block = self.join(1, 0, [land.at[0], land.at[1]])
        self.last = [self.push(block, land.at[5], 7, place.at(hi=1))]
        self.far.wait_recv()
        block = self.join(0, 2, [land.at[2]])
        self.last.append(self.push(block, land.at[6], 8, place.at(z=2)))

    def finish(self, out):
        for copy in self.direct + self.last:
            copy.wait_recv()
        land = self.landing
        add_rows(out, [self.chunk(0, 0), self.mine(0, 0), land.at[3], land.at[4], land.at[5], land.at[6]])

    def drain(self):
        for copy in self.sent:
            copy.wait_send()


def contract(left, right, dims):
    return lax.dot_general(left, right, (dims, ((), ())), preferred_element_type=F32)


def expert_kernel(
    n2, cots_far, table, wg, wu, wd,
    dn2, dgate, eo, eg, eu, ed,
    rows, cots, tables, table_sems, rows_sems, cots_sem,
    x_rows, c_rows, pick, gate, dhg, dhu, gact, dg, drow,
    pool, landing, gather_sems, dgate_out, dgate_sems, stage, stage_sems, eo_pool, eo_sems,
):
    place = Place()
    peers = group_peers(place)
    greet(list(peers.values()))
    me = group_index(place)

    small = []
    tables[me] = table[me]
    for (c, h, d), device in peers.items():
        slot = c * 8 + h * 4 + d
        pair = (table_sems.at[0, slot], table_sems.at[1, c * 8 + h * 4 + (4 - d) % 4])
        small.append(send(table.at[group_index(place, c, h, d)], tables.at[me], pair, device))
    rows[me] = n2[...]
    spread_rows = Spread(place, rows, rows_sems)
    spread_rows.first()
    cots_load = pltpu.make_async_copy(cots_far, cots, cots_sem)
    cots_load.start()
    for copy in small:
        copy.wait_recv()

    slots = lax.broadcasted_iota(jnp.int32, (80, 256), 0).astype(F32)
    second = lax.broadcasted_iota(jnp.int32, (1, 256), 1) >= 128

    def select(pair_index):
        parts = []
        for e in range(2):
            here = jnp.concatenate(
                [tables[pair_index * 2, e : e + 1, :], tables[pair_index * 2 + 1, e : e + 1, :]], axis=1
            )
            here = jnp.where(here < 0.0, -1000.0, here + jnp.where(second, 40.0, 0.0))
            weight = jnp.concatenate(
                [tables[pair_index * 2, 2 + e : 3 + e, :], tables[pair_index * 2 + 1, 2 + e : 3 + e, :]],
                axis=1,
            )
            hit = slots == here
            parts.append(jnp.where(hit, 1.0, 0.0).astype(BF))
            place_rows = pl.ds(pl.multiple_of(pair_index * 80, 80), 80)
            gate[e, place_rows, :] = jnp.sum(jnp.where(hit, weight, 0.0), axis=1, keepdims=True)
        pick[pair_index] = jnp.concatenate(parts, axis=0)

    def pull(pair_index, held, out):
        both = jnp.concatenate([held[pair_index * 2], held[pair_index * 2 + 1]], axis=0)
        picked = contract(pick[pair_index], both, ((1,), (0,))).astype(BF)
        place_rows = pl.ds(pl.multiple_of(pair_index * 80, 80), 80)
        out[0, place_rows, :] = picked[0:80]
        out[1, place_rows, :] = picked[80:160]

    def all_pairs(body):
        def step(i, carry):
            body(i)
            return carry
        lax.fori_loop(0, 8, step, 0)

    all_pairs(select)
    spread_rows.relay_a()
    spread_rows.relay_b()
    cots_load.wait()
    all_pairs(lambda p: pull(p, cots, c_rows))

    def pull_side(c, h, held, out):
        start = group_index(place, core=c, hi=h) - place.z
        base = start // 2

        def step(i, carry):
            pull(base + i, held, out)
            return carry

        lax.fori_loop(0, 2, step, 0)

    spread_rows.finish_near()
    pull_side(0, 0, rows, x_rows)
    pull_side(1, 0, rows, x_rows)
    spread_rows.relay_far()
    pull_side(0, 1, rows, x_rows)
    spread_rows.finish_far()
    pull_side(1, 1, rows, x_rows)

    def work(i, carry):
        e, m = i // 2, i % 2
        part = pl.ds(pl.multiple_of(m * 320, 320), 320)
        x = x_rows[e, part, :]
        hg = contract(x, wg[e], ((1,), (0,)))
        hu = contract(x, wu[e], ((1,), (0,)))
        back = contract(c_rows[e, part, :], wd[e], ((1,), (1,)))
        weight = gate[e, part, :]
        sig = 1.0 / (1.0 + jnp.exp(-hg))
        silu = hg * sig
        act = silu * hu
        dg[e, part, :] = jnp.sum(act * back, axis=1, keepdims=True)
        gact[e, part, :] = (weight * act).astype(BF)
        dact = weight * back
        low_hg = (dact * hu * (sig + silu * (1.0 - sig))).astype(BF)
        low_hu = (dact * silu).astype(BF)
        dhg[e, part, :] = low_hg
        dhu[e, part, :] = low_hu
        back_rows = (
            contract(low_hg, wg[e], ((1,), (1,))) + contract(low_hu, wu[e], ((1,), (1,)))
        ).astype(BF)
        for j in range(4):
            drow[m * 4 + j, pl.ds(pl.multiple_of(e * 80, 80), 80), :] = back_rows[j * 80 : (j + 1) * 80]
        return carry

    lax.fori_loop(0, 4, work, 0)
    spread_rows.drain()

    def put_back(pair_index, out):
        both = contract(pick[pair_index], drow[pair_index], ((0,), (0,))).astype(BF)
        out[pair_index * 2] = both[0:128]
        out[pair_index * 2 + 1] = both[128:256]

    def put_side(c, h, out):
        base = (group_index(place, core=c, hi=h) - place.z) // 2

        def step(i, carry):
            put_back(base + i, out)
            return carry

        lax.fori_loop(0, 2, step, 0)

    home = Gather(place, rows, pool, landing, gather_sems)
    put_side(1, 1, rows)
    swaps = [home.swap(1)]
    put_side(1, 0, rows)
    swaps.append(home.swap(0))

    def gate_grads(pair_index):
        chosen = pick[pair_index].astype(F32)
        for e in range(2):
            column = dg[e, pl.ds(pl.multiple_of(pair_index * 80, 80), 80), :]
            line = jnp.sum(chosen[e * 80 : (e + 1) * 80] * column, axis=0, keepdims=True)
            dgate_out[pair_index * 2, e : e + 1, :] = line[:, 0:128]
            dgate_out[pair_index * 2 + 1, e : e + 1, :] = line[:, 128:256]

    dgate_out[...] = jnp.zeros_like(dgate_out)
    all_pairs(gate_grads)
    small_back = []
    dgate[me] = dgate_out[me]
    for (c, h, d), device in peers.items():
        slot = c * 8 + h * 4 + d
        pair = (dgate_sems.at[0, slot], dgate_sems.at[1, c * 8 + h * 4 + (4 - d) % 4])
        small_back.append(send(dgate_out.at[group_index(place, c, h, d)], dgate.at[me], pair, device))
    put_side(0, 1, rows)
    swaps[0].wait_recv()
    put_side(0, 0, rows)
    swaps[1].wait_recv()
    home.first()

    def outputs(i, carry):
        e, m = i // 2, i % 2
        part = pl.ds(pl.multiple_of(m * 320, 320), 320)
        made = contract(gact[e, part, :], wd[e], ((1,), (0,))).astype(BF)
        for j in range(4):
            drow[m * 4 + j, pl.ds(pl.multiple_of(e * 80, 80), 80), :] = made[j * 80 : (j + 1) * 80]
        return carry

    lax.fori_loop(0, 4, outputs, 0)
    all_pairs(lambda p: put_back(p, cots))
    outward = Gather(place, cots, eo_pool, landing, eo_sems)
    out_swaps = [outward.swap(0), outward.swap(1)]
    home.second()
    copies = {}
    step = 0
    for e in range(2):
        for left, right, out in ((x_rows, dhg, eg), (x_rows, dhu, eu), (c_rows, gact, ed)):
            slot = step % 2
            if step >= 2:
                copies[step - 2].wait()

            def weight_grad(i, carry):
                tile = pl.ds(pl.multiple_of(i * 256, 256), 256)
                stage[slot, tile, :] = contract(left[e, :, tile], right[e], ((0,), (0,))).astype(BF)
                return carry

            lax.fori_loop(0, 6, weight_grad, 0)
            copies[step] = pltpu.make_async_copy(stage.at[slot], out.at[e], stage_sems.at[slot])
            copies[step].start()
            step += 1
    for copy in out_swaps:
        copy.wait_recv()
    for h in range(2):
        for d in range(4):
            outward.join(h, d)
    eo_copy = pltpu.make_async_copy(eo_pool, eo, stage_sems.at[2])
    eo_copy.start()
    home.finish(dn2)
    for copy in small_back:
        copy.wait_recv()
    for copy in small + small_back:
        copy.wait_send()
    home.drain()
    outward.drain()
    copies[4].wait()
    copies[5].wait()
    eo_copy.wait()


def run_experts(n2, cots, table, wg, wu, wd):
    vmem = pl.BlockSpec(memory_space=pltpu.VMEM)
    hbm = pl.BlockSpec(memory_space=pl.ANY)
    sems = pltpu.SemaphoreType.DMA
    low = lambda *shape: pltpu.VMEM(shape, BF)
    struct = jax.ShapeDtypeStruct
    return pl.pallas_call(
        expert_kernel,
        out_shape=(
            struct((128, 1536), F32), struct((16, 8, 128), F32), struct((8, 128, 1536), BF),
            struct((2, 1536, 512), BF), struct((2, 1536, 512), BF), struct((2, 1536, 512), BF),
        ),
        in_specs=[vmem, hbm, vmem, vmem, vmem, vmem],
        out_specs=[vmem, vmem, hbm, hbm, hbm, hbm],
        scratch_shapes=[
            low(16, 128, 1536), low(16, 128, 1536), pltpu.VMEM((16, 8, 128), F32),
            sems((2, 16)), sems((2, 16)), sems,
            low(2, 640, 1536), low(2, 640, 1536), low(8, 160, 256), pltpu.VMEM((2, 640, 1), F32),
            low(2, 640, 512), low(2, 640, 512), low(2, 640, 512), pltpu.VMEM((2, 640, 1), F32),
            low(8, 160, 1536),
            low(8, 128, 1536), low(7, 128, 1536), sems((2, 9)),
            pltpu.VMEM((16, 8, 128), F32), sems((2, 16)),
            low(2, 1536, 512), sems((3,)), low(8, 128, 1536), sems((2, 2)),
        ],
        compiler_params=pltpu.CompilerParams(
            collective_id=1, has_side_effects=True, vmem_limit_bytes=62 << 20
        ),
    )(n2, cots, table, wg, wu, wd)


def forward_kernel(
    x_ref, ids, cot, gains, wr, wq, wk, wv, wo,
    n1, qp, kv, lse, attn, y1, n2, gates, table, turn, cots,
    wqv, wkv, wov, weight_sems, cots_sems, k_sems, v_sems, own_sem,
):
    place = Place()
    me = group_index(place)
    context = place.lo * 4 + place.y
    loads = [
        pltpu.make_async_copy(wk, wkv.at[:, 0:512], weight_sems.at[0]),
        pltpu.make_async_copy(wv, wkv.at[:, 512:1024], weight_sems.at[1]),
        pltpu.make_async_copy(wq, wqv, weight_sems.at[2]),
        pltpu.make_async_copy(wo, wov, weight_sems.at[3]),
    ]
    for load in loads:
        load.start()
    own_copy = pltpu.make_async_copy(cot, cots.at[me], own_sem)
    own_copy.start()
    y_line, z_line = place.line("y"), place.line("z")
    lo_peer = place.at(lo=1)
    greet(
        [device for line in (y_line, z_line) for _, device in line]
        + [lo_peer, place.at(hi=1), place.at(core=1)]
    )

    x = x_ref[...].astype(F32)
    n1[...] = (x * inverse_root(x) * gains[0:1, :]).astype(BF)
    lane = lax.broadcasted_iota(jnp.int32, (128, 128), 1)
    row = lax.broadcasted_iota(jnp.int32, (128, 128), 0)
    freqs = jnp.exp((lane % 32).astype(F32) * (-math.log(10000.0) / 32))
    angles = (row + context * 128).astype(F32) * freqs
    cosine = jnp.cos(angles)
    sine = jnp.where(lane % 64 < 32, -1.0, 1.0) * jnp.sin(angles)
    turn[0] = cosine
    turn[1] = sine
    own_copy.wait()
    spread = Spread(place, cots, cots_sems)
    spread.first()

    loads[0].wait()
    loads[1].wait()
    for j in range(4):
        raw = contract(n1[...], wkv[:, j * 128 : (j + 1) * 128], ((1,), (0,)))
        kv[0, context, :, j * 128 : (j + 1) * 128] = (raw * cosine + swap_halves(raw) * sine).astype(BF)
    kv[1, context] = contract(n1[...], wkv[:, 512:1024], ((1,), (0,))).astype(BF)

    sent = []
    waits = {}

    def push(which, lo, y, device, slot):
        block = kv.at[which, (place.lo + lo) % 2 * 4 + (place.y + y) % 4]
        sems = (k_sems, v_sems)[which]
        copy = send(block, block, (sems.at[0, slot], sems.at[1, slot]), device)
        sent.append(copy)
        waits[which, slot] = copy

    for which in (0, 1):
        push(which, 0, 0, lo_peer, 4)
        for d in (1, 3, 2):
            push(which, 0, 0, place.at(y=d), (4 - d) % 4)

    loads[2].wait()
    for j in range(4):
        raw = contract(n1[...], wqv[:, j * 384 : (j + 1) * 384], ((1,), (0,)))
        turned = []
        for r in range(3):
            block = raw[:, r * 128 : (r + 1) * 128]
            turned.append((block * cosine + swap_halves(block) * sine) * 0.125)
        for r, block in enumerate(to_pairs(turned)):
            qp[j, r * 128 : (r + 1) * 128, :] = block.astype(BF)
    waits[0, 4].wait_recv()
    for d in (1, 3, 2):
        push(0, 1, 0, place.at(y=d), 4 + (4 - d) % 4)
    spread.relay_a()
    for d in (1, 3, 2):
        waits[1, d].wait_recv()
        push(1, 0, d, lo_peer, 4 + d)

    wide = lax.broadcasted_iota(jnp.int32, (128, 128), 1)
    chosen = jnp.zeros((128, 128), F32)
    for k in range(8):
        chosen = chosen + jnp.where(ids[:, k : k + 1] == wide, 1.0, 0.0)
    earlier = jnp.where(lane < row, 1.0, 0.0).astype(BF)
    before = contract(earlier, chosen.astype(BF), ((1,), (0,)))
    slots = jnp.where(chosen > 0.0, before, -1.0).T
    table[...] = jnp.zeros_like(table)
    for g in range(16):
        table[g, 0:2, :] = slots[2 * g : 2 * g + 2, :]

    for d in (1, 3, 2):
        waits[0, d].wait_recv()
        waits[0, 4 + d].wait_recv()
        waits[1, 4 + d].wait_recv()
    waits[1, 4].wait_recv()
    spread.relay_b()

    def attend(j, carry):
        lanes = pl.ds(pl.multiple_of(j * 128, 128), 128)
        keys = kv[0, :, :, lanes].reshape(1024, 128)
        values = kv[1, :, :, lanes].reshape(1024, 128)
        halves = []
        for s in range(2):
            scores = contract(keys, qp[j] * half_mask(s), ((1,), (1,)))
            scores = jnp.where(visible(place, 0, 1024), scores, floor_score)
            top = jnp.max(scores, axis=0, keepdims=True)
            probs = jnp.exp(scores - top)
            total = jnp.sum(probs, axis=0, keepdims=True)
            lse[j * 2 + s] = top + jnp.log(total)
            out = contract(values, probs.astype(BF), ((0,), (0,))) * (1.0 / total)
            halves.append(out[s * 64 : (s + 1) * 64])
        joined = jnp.concatenate(halves, axis=0).T
        for r, block in enumerate(from_pairs([joined[r * 128 : (r + 1) * 128] for r in range(3)])):
            attn[:, pl.ds(pl.multiple_of(j * 384 + r * 128, 128), 128)] = block.astype(BF)
        return carry

    lax.fori_loop(0, 4, attend, 0)
    spread.relay_far()

    loads[3].wait()
    for j in range(4):
        part = slice(j * 384, (j + 1) * 384)
        y1[:, part] = x_ref[:, part].astype(F32) + contract(attn[...], wov[:, part], ((1,), (0,)))
    y = y1[...]
    n2[...] = (y * inverse_root(y) * gains[1:2, :]).astype(BF)
    logits = contract(n2[...], wr[...], ((1,), (0,)))
    logits = jnp.where(chosen > 0.0, logits, -jnp.inf)
    weights = jnp.exp(logits - jnp.max(logits, axis=1, keepdims=True))
    weights = weights / jnp.sum(weights, axis=1, keepdims=True)
    gates[...] = weights
    turned = weights.T
    for g in range(16):
        table[g, 2:4, :] = turned[2 * g : 2 * g + 2, :]
    spread.finish_near()
    spread.finish_far()
    spread.drain()
    for copy in sent:
        copy.wait_send()


def run_forward(x, ids, cot, gains, wr, wq, wk, wv, wo):
    vmem = pl.BlockSpec(memory_space=pltpu.VMEM)
    hbm = pl.BlockSpec(memory_space=pl.ANY)
    sems = pltpu.SemaphoreType.DMA
    low = lambda *shape: pltpu.VMEM(shape, BF)
    struct = jax.ShapeDtypeStruct
    return pl.pallas_call(
        forward_kernel,
        out_shape=(
            struct((128, 1536), BF), struct((4, 384, 128), BF), struct((2, 8, 128, 512), BF),
            struct((8, 1, 384), F32), struct((128, 1536), BF), struct((128, 1536), F32),
            struct((128, 1536), BF), struct((128, 128), F32), struct((16, 8, 128), F32),
            struct((2, 128, 128), F32), struct((16, 128, 1536), BF),
        ),
        in_specs=[vmem] * 5 + [hbm] * 4,
        out_specs=[vmem] * 10 + [hbm],
        scratch_shapes=[
            low(1536, 1536), low(1536, 1024), low(1536, 1536), sems((4,)),
            sems((2, 16)), sems((2, 8)), sems((2, 8)), sems,
        ],
        compiler_params=pltpu.CompilerParams(
            collective_id=2, has_side_effects=True, vmem_limit_bytes=60 << 20
        ),
    )(x, ids, cot, gains, wr, wq, wk, wv, wo)


WIDTH = {"o": 512, "q": 384, "s": 256}
ORDERS = {"o": "xyz", "q": "zyx", "s": "yzx"}


def stream_index(order, block, half):
    at = {"x": half * 2 + block // 16, "y": block // 4 % 4, "z": block % 4}
    return tuple(at[axis] for axis in order)


def fill_stream(out, order, left, right, width):
    for half in range(2):
        columns = right[:, half * width : (half + 1) * width]
        for tile in range(4):
            grads = contract(left[:, tile * 384 : (tile + 1) * 384], columns, ((0,), (0,))).astype(BF)
            for j in range(8):
                index = stream_index(order, tile * 8 + j, half)
                out[(*index, slice(None), slice(0, width))] = grads[j * 48 : (j + 1) * 48]


class Homeward:
    def __init__(self, place, pool, near, landing, sems, near_sems):
        self.place, self.pool, self.near, self.landing, self.sems = place, pool, near, landing, sems
        self.loads = []
        for i, (h, d) in enumerate(((1, 0), (0, 2), (0, 0))):
            self.loads.append(pltpu.make_async_copy(self.chunk(h, d), near.at[i], near_sems.at[i]))
            self.loads[-1].start()
        self.sent = []

    def chunk(self, hi, z):
        return self.pool.at[(self.place.hi + hi) % 2 * 4 + (self.place.z + z) % 4]

    def push(self, src, slot, device):
        pair = (self.sems.at[0, slot], self.sems.at[1, slot])
        self.sent.append(send(src, self.landing.at[slot], pair, device))

    def first(self):
        place = self.place
        self.push(self.chunk(1, 1), 0, place.at(z=1))
        self.push(self.chunk(1, 3), 1, place.at(z=3))
        self.push(self.chunk(1, 2), 2, place.at(hi=1))
        self.push(self.chunk(0, 1), 3, place.at(z=1))
        self.push(self.chunk(0, 3), 4, place.at(z=3))

    def second(self):
        for load in self.loads:
            load.wait()
        near, land = self.near, self.landing
        for copy in self.sent[:3]:
            copy.wait_recv()
        add_rows(near.at[0], [near.at[0], land.at[0], land.at[1]])
        self.push(near.at[0], 5, self.place.at(hi=1))
        add_rows(near.at[1], [near.at[1], land.at[2]])
        self.push(near.at[1], 6, self.place.at(z=2))

    def finish(self, out, base):
        for copy in self.sent[3:]:
            copy.wait_recv()
        add_rows(out, [base, self.near.at[2]] + [self.landing.at[i] for i in (3, 4, 5, 6)])

    def drain(self):
        for copy in self.sent:
            copy.wait_send()


def backward_kernel(
    dn2r, dgate, gates, n2, y1, cot, x_ref, n1, attn, qp, kv, lse, turn, gains, wr,
    wo, wq, wk, wv, eo, eg, eu, ed,
    mixed, gt, gq, gk, gv, go, gs, og, ou, od, far_p, far_q,
    w_big, w_kv, weight_sems,
    n1c, attnc, dqc, dkvc, dbrc, pair_sems,
    dgt, dbr, dap, delta, dq, dk, dv, dy1, dkv, land_a, land_b, land_c, land_d, kv_sems,
    send_o, send_q, send_s, land1_o, land1_q, land1_s, mid_o, mid_q, mid_s,
    land2_o, land2_q, land2_s, last_o, last_q, last_s, land3_o, land3_q, land3_s, dense_sems,
    mine, quarters, quarter_sems,
    near, home_landing, home_sems, near_sems,
    stage, stage_sems, sum_p, sum_q, land_p2, land_q2, expert_sems,
):
    place = Place()
    context = place.lo * 4 + place.y
    y_line, z_line, x_line = (place.line(axis) for axis in "yzx")
    sibling, cross, lo_device = place.at(core=1), place.at(hi=1, core=1), place.at(lo=1)
    other_lo = (place.lo + 1) % 2
    load_o = pltpu.make_async_copy(wo, w_big, weight_sems.at[0])
    load_o.start()
    load_kv = [
        pltpu.make_async_copy(wk, w_kv.at[:, 0:512], weight_sems.at[1]),
        pltpu.make_async_copy(wv, w_kv.at[:, 512:1024], weight_sems.at[2]),
    ]
    for load in load_kv:
        load.start()
    greet([device for line in (y_line, z_line, x_line) for _, device in line] + [sibling, cross])
    pending = []

    mats = (eg, eu, ed)
    stage_p, stage_q = [], []
    at = 0
    for m, mat in enumerate(mats):
        for d, (index, device) in enumerate(y_line):
            pair = (expert_sems.at[0, at], expert_sems.at[1, at])
            stage_p.append(send(mat.at[0, :, index], far_p.at[d, m], pair, device))
            at += 1
        pair = (expert_sems.at[0, at], expert_sems.at[1, at])
        stage_q.append(send(mat.at[1, other_lo], far_q.at[m], pair, lo_device))
        at += 1
    home = Homeward(place, eo, near, home_landing, home_sems, near_sems)
    home.first()

    def share(i, rows, both, half):
        source = rows if half is None else rows.at[1 - place.core]
        pair = (pair_sems.at[0, i], pair_sems.at[1, i])
        copy = send(source, both.at[pl.ds(128, 128)], pair, sibling)
        both[0:128, :] = rows[...] if half is None else rows[place.core]
        pending.append(copy)
        return copy

    share_attn = share(0, attn, attnc, None)
    share_n1 = share(1, n1, n1c, None)

    dgt[...] = jnp.zeros_like(dgt)
    for g in range(16):
        dgt[2 * g : 2 * g + 2, :] = dgate[g, 0:2, :]
    weights = gates[...]
    dgates = dgt[...].T
    dlogits = weights * (dgates - jnp.sum(weights * dgates, axis=1, keepdims=True))
    dlogits = dlogits.astype(BF)
    dn2 = dn2r[...] + contract(dlogits, wr[...], ((1,), (1,)))
    y = y1[...]
    root = inverse_root(y)
    scaled = dn2 * gains[1:2, :]
    inner = jnp.mean(scaled * y, axis=-1, keepdims=True)
    dy = cot[...].astype(F32) + root * scaled - y * (root * root * root * inner)
    dy1[...] = dy
    low = dy.astype(BF)
    dbr[0] = low[:, 0:768]
    dbr[1] = low[:, 768:1536]
    share_dbr = share(2, dbr, dbrc, 1)
    gain_rows = (dn2 * y * root).astype(BF)
    column = jnp.where(lax.broadcasted_iota(jnp.int32, (128, 128), 1) == 32, 1.0, 0.0).astype(BF)
    narrow_left = jnp.concatenate([n2[...], gain_rows], axis=0)
    narrow_right = jnp.concatenate([dlogits, column], axis=0)
    for tile in range(4):
        part = contract(
            narrow_left[:, tile * 384 : (tile + 1) * 384], narrow_right, ((0,), (0,))
        ).astype(BF)
        for j in range(8):
            for half in range(2):
                index = stream_index(ORDERS["o"], tile * 8 + j, half)
                send_o[(*index, slice(None), slice(384, 512))] = part[j * 48 : (j + 1) * 48]

    load_o.wait()
    for j in range(4):
        back = contract(low, w_big[j * 384 : (j + 1) * 384, :], ((1,), (1,)))
        grads = to_pairs([back[:, r * 128 : (r + 1) * 128] for r in range(3)])
        outs = to_pairs(
            [attn[:, j * 384 + r * 128 : j * 384 + (r + 1) * 128].astype(F32) for r in range(3)]
        )
        grads = jnp.concatenate(grads, axis=0).astype(BF)
        dap[j] = grads
        product = (grads.astype(F32) * jnp.concatenate(outs, axis=0)).T
        for s in range(2):
            delta[j * 2 + s] = jnp.sum(product[s * 64 : (s + 1) * 64], axis=0, keepdims=True)
    load_q = pltpu.make_async_copy(wq, w_big, weight_sems.at[0])
    load_q.start()

    sends = {"o": send_o, "q": send_q, "s": send_s}
    lands = {
        "o": (land1_o, land2_o, land3_o), "q": (land1_q, land2_q, land3_q),
        "s": (land1_s, land2_s, land3_s),
    }
    mids = {"o": (mid_o, last_o), "q": (mid_q, last_q), "s": (mid_s, last_s)}
    begin = {"o": 0, "q": 9, "s": 18}
    flight = {}

    def launch(name, phase):
        source = sends[name] if phase == 0 else mids[name][phase - 1]
        flight[name] = scatter_start(
            place, ORDERS[name][phase], source, lands[name][phase], dense_sems,
            begin[name] + 3 * phase,
        )

    def land(name, phase):
        for copy in flight[name]:
            copy.wait_recv()
        pending.extend(flight[name])
        source = sends[name] if phase == 0 else mids[name][phase - 1]
        own = source.at[place.own(ORDERS[name][phase])]
        landing = lands[name][phase]
        if phase == 0:
            out = mids[name][0]

            def body(i, carry):
                a, b = i // 4, i % 4
                total = own[a, b].astype(F32)
                for d in range(3):
                    total = total + landing[d, a, b].astype(F32)
                out[a, b] = total.astype(BF)
                return carry

            lax.fori_loop(0, 16, body, 0)
        elif phase == 1:
            add_up(mids[name][1], own, landing, 4)
        else:
            total = own[...].astype(F32)
            for d in range(3):
                total = total + landing[d].astype(F32)
            mine["oqs".index(name), :, 0 : WIDTH[name]] = total.astype(BF)

    share_attn.wait_recv()
    share_dbr.wait_recv()
    fill_stream(send_o, ORDERS["o"], attnc, dbrc, 384)
    launch("o", 0)

    cosine, sine = turn[0], turn[1]

    def attend(j, carry):
        lanes = pl.ds(pl.multiple_of(j * 128, 128), 128)
        turned = [jnp.zeros((128, 384), F32) for _ in range(2)]
        for block in range(2):
            part = slice(block * 4, (block + 1) * 4)
            keys = kv[0, part, :, lanes].reshape(512, 128)
            values = kv[1, part, :, lanes].reshape(512, 128)
            grad_keys = jnp.zeros((512, 128), F32)
            grad_values = jnp.zeros((512, 128), F32)
            seen = visible(place, block * 512, 512)
            for s in range(2):
                queries = qp[j] * half_mask(s)
                grads = dap[j] * half_mask(s)
                scores = contract(keys, queries, ((1,), (1,)))
                probs = jnp.exp(jnp.where(seen, scores, floor_score) - lse[j * 2 + s])
                back = contract(values, grads, ((1,), (1,)))
                grad_scores = (probs * (back - delta[j * 2 + s])).astype(BF)
                grad_values = grad_values + contract(probs.astype(BF), grads, ((1,), (0,)))
                grad_keys = grad_keys + contract(grad_scores, queries, ((1,), (0,)))
                turned[s] = turned[s] + contract(keys, grad_scores, ((0,), (0,)))
            dkv[part, j, 0] = grad_keys.astype(BF).reshape(4, 128, 128)
            dkv[part, j, 1] = grad_values.astype(BF).reshape(4, 128, 128)
        joined = jnp.concatenate([turned[0][0:64], turned[1][64:128]], axis=0).T * 0.125
        blocks = from_pairs([joined[r * 128 : (r + 1) * 128] for r in range(3)])
        for r, part in enumerate(blocks):
            raw = part * cosine - swap_halves(part) * sine
            lanes = pl.ds(pl.multiple_of((j % 2) * 384 + r * 128, 128), 128)
            dq[j // 2, :, lanes] = raw.astype(BF)
        return carry

    kv_sent = []

    def kv_push(src, dst, slot, device):
        copy = send(src, dst, (kv_sems.at[0, slot], kv_sems.at[1, slot]), device)
        kv_sent.append(copy)
        return copy

    def kv_add(out, count, terms):
        def body(i, carry):
            a, b, c = i // 4, i // 2 % 2, i % 2
            block = out(a)
            total = block[b, c].astype(F32)
            for term in terms:
                total = total + term(a)[b, c].astype(F32)
            block[b, c] = total.astype(BF)
            return carry

        lax.fori_loop(0, count * 4, body, 0)

    first, later = pl.ds(0, 2), pl.ds(2, 2)
    lax.fori_loop(0, 2, attend, 0)
    lead = kv_push(dkv.at[pl.ds(other_lo * 4, 4), first], land_a, 0, lo_device)
    lax.fori_loop(2, 4, attend, 0)
    legs = []
    for d, (index, device) in enumerate(y_line):
        for lo in range(2):
            legs.append(
                kv_push(dkv.at[lo * 4 + index, later], land_c.at[d, lo], 4 + d * 2 + lo, device)
            )
    share_dq = share(3, dq, dqc, 1)
    lead.wait_recv()
    kv_add(lambda a: dkv.at[place.lo * 4 + a, first], 4, [lambda a: land_a.at[a]])
    legs_b = [
        kv_push(dkv.at[place.lo * 4 + index, first], land_b.at[d], 1 + d, device)
        for d, (index, device) in enumerate(y_line)
    ]
    share_n1.wait_recv()
    share_dq.wait_recv()
    fill_stream(send_q, ORDERS["q"], n1c, dqc, 384)
    launch("q", 0)
    for copy in legs:
        copy.wait_recv()
    kv_add(
        lambda a: dkv.at[a * 4 + place.y, later], 2,
        [lambda a, d=d: land_c.at[d, a] for d in range(3)],
    )
    leg_d = kv_push(dkv.at[other_lo * 4 + place.y, later], land_d, 10, lo_device)
    for copy in legs_b:
        copy.wait_recv()

    def key_grads(j, terms):
        total_k = dkv[context, j, 0].astype(F32)
        total_v = dkv[context, j, 1].astype(F32)
        for term in terms:
            total_k = total_k + term[0].astype(F32)
            total_v = total_v + term[1].astype(F32)
        raw = total_k * cosine - swap_halves(total_k) * sine
        lanes = (j % 2) * 256
        dk[j // 2, :, lanes : lanes + 128] = raw.astype(BF)
        dk[j // 2, :, lanes + 128 : lanes + 256] = total_v.astype(BF)

    for j in range(2):
        key_grads(j, [land_b.at[d, j] for d in range(3)])
    leg_d.wait_recv()
    for j in range(2):
        key_grads(2 + j, [land_d.at[j]])
    share_dkv = share(4, dk, dkvc, 1)
    share_dkv.wait_recv()
    fill_stream(send_s, ORDERS["s"], n1c, dkvc, 256)
    launch("s", 0)
    pending.extend(kv_sent)

    for load in load_kv:
        load.wait()
    load_q.wait()
    x = x_ref[...].astype(F32)
    root = inverse_root(x)
    keys = jnp.concatenate([dk[j // 2, :, j % 2 * 256 : j % 2 * 256 + 128] for j in range(4)], axis=1)
    values = jnp.concatenate(
        [dk[j // 2, :, j % 2 * 256 + 128 : j % 2 * 256 + 256] for j in range(4)], axis=1
    )
    both = jnp.concatenate([keys, values], axis=1)
    queries = jnp.concatenate([dq[0], dq[1]], axis=1)
    for j in range(4):
        part = slice(j * 384, (j + 1) * 384)
        gt[:, part] = contract(queries, w_big[part, :], ((1,), (1,))) + contract(
            both, w_kv[part, :], ((1,), (1,))
        )
    scaled = gt[...] * gains[0:1, :]
    inner = jnp.mean(scaled * x, axis=-1, keepdims=True)
    gt[...] = dy1[...] + root * scaled - x * (root * root * root * inner)

    home.second()
    land("o", 0)
    launch("o", 1)
    land("o", 1)
    launch("o", 2)
    land("q", 0)
    launch("q", 1)
    land("s", 0)
    launch("s", 1)
    land("q", 1)
    launch("q", 2)
    land("s", 1)
    launch("s", 2)
    land("o", 2)
    land("q", 2)
    land("s", 2)
    own_quarter = place.core * 2 + place.hi
    gathered = []
    for i, (a, b) in enumerate(((0, 1), (1, 0), (1, 1))):
        pair = (quarter_sems.at[0, i], quarter_sems.at[1, i])
        gathered.append(send(mine, quarters.at[own_quarter], pair, place.at(hi=a, core=b)))
    quarters[own_quarter] = mine[...]

    for copy in stage_p + stage_q:
        copy.wait_recv()
    pending.extend(stage_p + stage_q)
    steps = []
    for m, mat in enumerate(mats):
        for lo in range(2):
            terms = [mat.at[0, lo, place.y]] + [far_p.at[d, m, lo] for d in range(3)]
            steps.append((terms, sum_p.at[lo, m]))
    for m, mat in enumerate(mats):
        for pair_y in range(2):
            for i in range(2):
                y_at = pair_y * 2 + i
                steps.append(([mat.at[1, place.lo, y_at], far_q.at[m, y_at]], sum_q.at[y_at, m]))

    def fetch(step):
        loads = []
        for i, term in enumerate(steps[step][0]):
            loads.append(
                pltpu.make_async_copy(term, stage.at[step % 2, i], stage_sems.at[step % 2, i])
            )
            loads[-1].start()
        return loads

    second = []
    ready = fetch(0)
    for step, (terms, out) in enumerate(steps):
        following = fetch(step + 1) if step + 1 < len(steps) else None
        for load in ready:
            load.wait()

        def fold(i, carry):
            part = pl.ds(pl.multiple_of(i * 48, 16), 48)
            total = stage[step % 2, 0, part].astype(F32)
            for term in range(1, len(terms)):
                total = total + stage[step % 2, term, part].astype(F32)
            out[part] = total.astype(BF)
            return carry

        lax.fori_loop(0, 4, fold, 0)
        ready = following
        if step == 5:
            pair = (expert_sems.at[0, 12], expert_sems.at[1, 12])
            second.append(send(sum_p.at[other_lo], land_p2, pair, lo_device))
    for d, (index, device) in enumerate(y_line):
        pair = (expert_sems.at[0, 13 + d], expert_sems.at[1, 13 + d])
        second.append(send(sum_q.at[index], land_q2.at[d], pair, device))

    home.finish(mixed, y1)
    home.drain()
    for copy in gathered:
        copy.wait_recv()
    pending.extend(gathered)
    for q in range(4):
        go[:, q * 384 : (q + 1) * 384] = quarters[q, 0, :, 0:384].astype(F32)
        gq[:, q * 384 : (q + 1) * 384] = quarters[q, 1, :, 0:384].astype(F32)
        gk[:, q * 128 : (q + 1) * 128] = quarters[q, 2, :, 0:128].astype(F32)
        gv[:, q * 128 : (q + 1) * 128] = quarters[q, 2, :, 128:256].astype(F32)
    narrow = quarters[0, 0, :, 384:512].astype(F32) + quarters[2, 0, :, 384:512].astype(F32)
    rows = pl.ds(pl.multiple_of((context * 4 + place.z) * 48, 16), 48)
    line = jnp.sum(gq[...] * w_big[rows, :].astype(F32), axis=1, keepdims=True)
    line = line + jnp.sum(gk[...] * w_kv[rows, 0:512].astype(F32), axis=1, keepdims=True)
    line = line + jnp.sum(gv[...] * w_kv[rows, 512:1024].astype(F32), axis=1, keepdims=True)
    gs[...] = jnp.where(lax.broadcasted_iota(jnp.int32, (48, 128), 1) == 33, line, narrow)

    for copy in second:
        copy.wait_recv()
    pending.extend(second)
    for m, out in enumerate((og, ou, od)):
        def finish(i, carry):
            part = pl.ds(pl.multiple_of(i * 48, 16), 48)
            out[0, part] = sum_p[place.lo, m, part].astype(F32) + land_p2[m, part].astype(F32)
            total = sum_q[place.y, m, part].astype(F32)
            for d in range(3):
                total = total + land_q2[d, m, part].astype(F32)
            out[1, part] = total
            return carry

        lax.fori_loop(0, 4, finish, 0)
    for copy in pending:
        copy.wait_send()


def run_backward(*operands):
    vmem = pl.BlockSpec(memory_space=pltpu.VMEM)
    hbm = pl.BlockSpec(memory_space=pl.ANY)
    sems = pltpu.SemaphoreType.DMA
    struct = jax.ShapeDtypeStruct
    f32 = lambda *shape: struct(shape, F32)
    low = lambda *shape: pltpu.VMEM(shape, BF)
    high = lambda *shape: pltpu.VMEM(shape, F32)
    wide = [WIDTH[name] for name in "oqs"]
    return pl.pallas_call(
        backward_kernel,
        out_shape=(
            struct((128, 1536), BF), f32(128, 1536),
            f32(48, 1536), f32(48, 512), f32(48, 512), f32(48, 1536), f32(48, 128),
            f32(2, 192, 512), f32(2, 192, 512), f32(2, 192, 512),
            struct((3, 3, 2, 192, 512), BF), struct((3, 4, 192, 512), BF),
        ),
        in_specs=[vmem] * 15 + [hbm] * 8,
        out_specs=[vmem] * 10 + [hbm] * 2,
        scratch_shapes=[
            low(1536, 1536), low(1536, 1024), sems((3,)),
            low(256, 1536), low(256, 1536), low(256, 768), low(256, 512), low(256, 768),
            sems((2, 5)),
            high(128, 128), low(2, 128, 768), low(4, 384, 128), high(8, 1, 384),
            low(2, 128, 768), low(2, 128, 512), low(16, 128), high(128, 1536),
            low(8, 4, 2, 128, 128), low(4, 2, 2, 128, 128), low(3, 2, 2, 128, 128),
            low(3, 2, 2, 2, 128, 128), low(2, 2, 128, 128), sems((2, 11)),
            *[low(4, 4, 4, 48, w) for w in wide],
            *[low(3, 4, 4, 48, w) for w in wide],
            *[low(4, 4, 48, w) for w in wide],
            *[low(3, 4, 48, w) for w in wide],
            *[low(4, 48, w) for w in wide],
            *[low(3, 48, w) for w in wide],
            sems((2, 27)),
            low(3, 48, 512), low(4, 3, 48, 512), sems((2, 3)),
            low(3, 128, 1536), low(7, 128, 1536), sems((2, 7)), sems((3,)),
            low(2, 4, 192, 512), sems((2, 4)),
            low(2, 3, 192, 512), low(4, 3, 192, 512), low(3, 192, 512), low(3, 3, 192, 512),
            sems((2, 16)),
        ],
        compiler_params=pltpu.CompilerParams(
            collective_id=3, has_side_effects=True, vmem_limit_bytes=63 << 20
        ),
    )(*operands)


def shards(
    tokens, expert_ids, w_query, w_key, w_value, w_out, gain_attn, gain_moe, w_router,
    w_gate, w_up, w_down, cotangent,
):
    gains = jnp.stack([gain_attn, gain_moe])
    router = jnp.pad(w_router, ((0, 0), (0, 96)))
    x, cot = tokens[0], cotangent[0]
    n1, qp, kv, lse, attn, y1, n2, gates, table, turn, cots = run_forward(
        x, expert_ids[0], cot, gains, router, w_query, w_key, w_value, w_out
    )
    dn2, dgate, eo, eg, eu, ed = run_experts(n2, cots, table, w_gate, w_up, w_down)
    blocks = lambda grads: grads.reshape(2, 2, 4, 192, 512)
    mixed, gt, gq, gk, gv, go, gs, og, ou, od, _, _ = run_backward(
        dn2, dgate, gates, n2, y1, cot, x, n1, attn, qp, kv, lse, turn, gains, router,
        w_out, w_query, w_key, w_value, eo, blocks(eg), blocks(eu), blocks(ed),
    )
    own = lax.axis_index("context") * 4 + lax.axis_index("dp")
    own_gain = lax.dynamic_slice(gain_attn, (own * 48,), (48,))
    return (
        mixed[None], gt[None], gq, gk, gv, go, gs[:, 33] / own_gain, gs[:, 32], gs[:, :32],
        og, ou, od.transpose(0, 2, 1),
    )


def solution(mesh):
    in_specs = (
        P(("expert", "dp"), "context", None),
        P(("expert", "dp"), "context", None),
        P(),
        P(),
        P(),
        P(),
        P(),
        P(),
        P(),
        P(("expert", "dp"), None, None),
        P(("expert", "dp"), None, None),
        P(("expert", "dp"), None, None),
        P(("expert", "dp"), "context", None),
    )
    out_specs = (
        P(("expert", "dp"), "context", None),
        P(("expert", "dp"), "context", None),
        P(("context", "dp"), None),
        P(("context", "dp"), None),
        P(("context", "dp"), None),
        P(("context", "dp"), None),
        P(("context", "dp")),
        P(("context", "dp")),
        P(("context", "dp"), None),
        P(("expert", "dp"), "context", None),
        P(("expert", "dp"), "context", None),
        P(("expert", "dp"), None, "context"),
    )
    return jax.shard_map(shards, mesh=mesh, in_specs=in_specs, out_specs=out_specs, check_vma=False)
```

```python
import math

import jax
import jax.numpy as jnp
from jax import lax
from jax.experimental import pallas as pl
from jax.experimental.pallas import tpu as pltpu
from jax.sharding import PartitionSpec as P

epsilon = 1e-06
floor_score = -1e30
MESH = pl.DeviceIdType.MESH
BF = jnp.bfloat16
F32 = jnp.float32


def low(*shape):
    return pltpu.VMEM(shape, BF)


def high(*shape):
    return pltpu.VMEM(shape, F32)


class Place:
    def __init__(self):
        e, c = lax.axis_index("expert"), lax.axis_index("context")
        self.hi, self.core = e // 2, e % 2
        self.lo, self.y = c // 4, c % 4
        self.z = lax.axis_index("dp")

    def at(self, hi=0, core=0, lo=0, y=0, z=0):
        e = (self.hi + hi) % 2 * 2 + (self.core + core) % 2
        c = (self.lo + lo) % 2 * 4 + (self.y + y) % 4
        return (e, c, (self.z + z) % 4)

    def line(self, axis):
        if axis == "y":
            return [((self.y + d) % 4, self.at(y=d)) for d in (1, 2, 3)]
        if axis == "z":
            return [((self.z + d) % 4, self.at(z=d)) for d in (1, 2, 3)]
        return [
            ((self.hi + a) % 2 * 2 + (self.lo + b) % 2, self.at(hi=a, lo=b))
            for a, b in ((0, 1), (1, 0), (1, 1))
        ]

    def own(self, axis):
        return {"y": self.y, "z": self.z, "x": self.hi * 2 + self.lo}[axis]


def greet(devices):
    barrier = pltpu.get_barrier_semaphore()
    for device in devices:
        pl.semaphore_signal(barrier, inc=1, device_id=device, device_id_type=MESH)
    pl.semaphore_wait(barrier, len(devices))


def send(src, dst, sems, device):
    copy = pltpu.make_async_remote_copy(
        src_ref=src, dst_ref=dst, send_sem=sems[0], recv_sem=sems[1],
        device_id=device, device_id_type=MESH,
    )
    copy.start()
    return copy


def scatter_start(place, axis, src, landing, sems, begin):
    copies = []
    for d, (index, device) in enumerate(place.line(axis)):
        pair = (sems.at[0, begin + d], sems.at[1, begin + d])
        copies.append(send(src.at[index], landing.at[d], pair, device))
    return copies


def add_up(out, own, landing, lead):
    count = landing.shape[0]

    def body(i, carry):
        total = own[i].astype(F32)
        for d in range(count):
            total = total + landing[d, i].astype(F32)
        out[i] = total.astype(out.dtype)
        return carry

    lax.fori_loop(0, lead, body, 0)


def roll_lanes(u, shift):
    return pltpu.roll(u, shift, 1)


def swap_halves(u):
    lane = lax.broadcasted_iota(jnp.int32, u.shape, 1)
    return jnp.where(lane % 64 < 32, roll_lanes(u, 96), roll_lanes(u, 32))


def to_pairs(blocks):
    a, b, c = blocks
    low = lax.broadcasted_iota(jnp.int32, a.shape, 1) < 64
    return [
        jnp.where(low, a, b), jnp.where(low, roll_lanes(a, 64), roll_lanes(c, 64)), jnp.where(low, b, c)
    ]


def from_pairs(blocks):
    a, b, c = blocks
    low = lax.broadcasted_iota(jnp.int32, a.shape, 1) < 64
    turned = roll_lanes(b, 64)
    return [jnp.where(low, a, turned), jnp.where(low, c, a), jnp.where(low, turned, c)]


def inverse_root(values):
    return lax.rsqrt(jnp.mean(values * values, axis=-1, keepdims=True) + epsilon)


def visible(place, start, rows):
    key = lax.broadcasted_iota(jnp.int32, (rows, 384), 0) + start
    query = lax.broadcasted_iota(jnp.int32, (rows, 384), 1) % 128
    return key <= query + (place.lo * 4 + place.y) * 128


def half_mask(s):
    lane = lax.broadcasted_iota(jnp.int32, (1, 128), 1)
    return jnp.where((lane >= 64) == (s == 1), 1.0, 0.0).astype(BF)


def group_peers(place):
    return {
        (c, h, d): place.at(core=c, hi=h, z=d)
        for c in (0, 1) for h in (0, 1) for d in range(4) if (c, h, d) != (0, 0, 0)
    }


def group_index(place, core=0, hi=0, z=0):
    return ((place.hi + hi) % 2 * 2 + (place.core + core) % 2) * 4 + (place.z + z) % 4


class Spread:
    def __init__(self, place, held, sems):
        self.place, self.held, self.sems = place, held, sems
        self.sent, self.waits = [], {}

    def push(self, origin, device, slot, rows=None):
        block = self.held.at[group_index(self.place, hi=origin[0], z=origin[1])]
        if rows is not None:
            block = block.at[pl.ds(rows, 64)]
        pair = (self.sems.at[0, len(self.sent)], self.sems.at[1, slot])
        copy = send(block, block, pair, device)
        self.sent.append(copy)
        self.waits[slot] = copy

    def land(self, slot):
        self.waits[slot].wait_recv()

    def around(self, h):
        self.push((h, 0), self.place.at(z=1), h * 4 + 3)
        self.push((h, 0), self.place.at(z=3), h * 4 + 1)

    def first(self):
        self.push((0, 0), self.place.at(hi=1), 4)
        self.around(0)
        self.push((0, 0), self.place.at(core=1), 8)

    def relay_hi(self):
        self.land(4)
        self.around(1)
        self.push((1, 0), self.place.at(core=1), 12)

    def relay(self, h):
        sibling = self.place.at(core=1)
        self.land(h * 4 + 3)
        self.push((h, 3), self.place.at(z=1), h * 4 + 2, 0)
        self.push((h, 3), sibling, 8 + h * 4 + 3)
        self.land(h * 4 + 1)
        self.push((h, 1), self.place.at(z=3), 16 + h, 64)
        self.push((h, 1), sibling, 8 + h * 4 + 1)

    def last(self, h):
        self.land(h * 4 + 2)
        self.land(16 + h)
        self.push((h, 2), self.place.at(core=1), 8 + h * 4 + 2)

    def finish(self, h):
        for d in range(4):
            self.land(8 + h * 4 + d)

    def drain(self):
        for copy in self.sent:
            copy.wait_send()


def add_rows(out, terms):
    def body(i, carry):
        part = pl.ds(pl.multiple_of(i * 16, 16), 16)
        total = terms[0][part].astype(F32)
        for term in terms[1:]:
            total = total + term[part].astype(F32)
        out[part] = total.astype(out.dtype)
        return carry

    lax.fori_loop(0, out.shape[0] // 16, body, 0)


class Gather:
    def __init__(self, place, parts, pool, halves, wholes, sems):
        self.place, self.parts, self.pool, self.sems = place, parts, pool, sems
        self.halves, self.wholes = halves, wholes
        self.sent, self.waits = [], {}

    def push(self, src, dst, slot, device):
        copy = send(src, dst, (self.sems.at[0, slot], self.sems.at[1, slot]), device)
        self.sent.append(copy)
        self.waits[slot] = copy
        return copy

    def swap(self, hi):
        half = (self.place.hi + hi) % 2
        start = group_index(self.place, core=1, hi=hi) - self.place.z
        return self.push(
            self.parts.at[pl.ds(start, 4)], self.pool.at[pl.ds(half * 4, 4)], hi, self.place.at(core=1)
        )

    def chunk(self, hi, z):
        return self.pool.at[(self.place.hi + hi) % 2 * 4 + (self.place.z + z) % 4]

    def terms(self, hi, z):
        if self.parts is None:
            return [self.chunk(hi, z)]
        return [self.chunk(hi, z), self.parts.at[group_index(self.place, hi=hi, z=z)]]

    def join(self, hi, z, more=()):
        block = self.chunk(hi, z)
        if self.parts is not None or more:
            add_rows(block, [*self.terms(hi, z), *more])
        return block

    def first(self, h):
        block = self.join(h, 2)
        upper, lower = pl.ds(0, 64), pl.ds(64, 64)
        self.push(block.at[upper], self.halves.at[h, 0], 2 + h * 4, self.place.at(z=1))
        self.push(block.at[lower], self.halves.at[h, 1], 3 + h * 4, self.place.at(z=3))
        self.join(h, 1)
        self.join(h, 3)

    def second(self, h):
        for side, d in ((0, 1), (1, 3)):
            part = pl.ds(side * 64, 64)
            self.waits[2 + h * 4 + side].wait_recv()
            block = self.chunk(h, d)
            add_rows(block.at[part], [block.at[part], self.halves.at[h, side]])
            self.push(block, self.wholes.at[h * 2 + side], 4 + h * 4 + side, self.place.at(z=d))

    def third(self):
        for side in range(2):
            self.waits[8 + side].wait_recv()
        block = self.join(1, 0, [self.wholes.at[2], self.wholes.at[3]])
        self.push(block, self.wholes.at[4], 10, self.place.at(hi=1))

    def finish(self, out, more=()):
        for slot in (4, 5, 10):
            self.waits[slot].wait_recv()
        add_rows(out, [*more, *self.terms(0, 0)] + [self.wholes.at[i] for i in (0, 1, 4)])

    def drain(self):
        for copy in self.sent:
            copy.wait_send()


class SpreadShort:
    def __init__(self, place, held, sems):
        self.place, self.held, self.sems = place, held, sems
        self.sent, self.waits = [], {}

    def pair(self, c, h, d):
        slot = c * 8 + h * 4 + d
        return (self.sems.at[0, slot], self.sems.at[1, slot])

    def push(self, origin, target, slot):
        c, h, d = target
        index = group_index(self.place, hi=origin[0], z=origin[1])
        block = self.held.at[index]
        copy = send(block, block, self.pair(*slot), self.place.at(core=c, hi=h, z=d))
        self.sent.append(copy)
        self.waits[slot] = copy

    def land(self, slot):
        self.waits[slot].wait_recv()

    def first(self):
        for d in (1, 3, 2):
            self.push((0, 0), (0, 0, d), (0, 0, (4 - d) % 4))
        self.push((0, 0), (0, 1, 0), (0, 1, 0))
        self.push((0, 0), (1, 0, 0), (1, 0, 0))

    def relay_a(self):
        self.land((0, 1, 0))
        for d in (1, 3):
            self.push((1, 0), (0, 0, d), (0, 1, (4 - d) % 4))
        self.push((1, 0), (1, 0, 0), (1, 1, 0))

    def relay_b(self):
        self.land((0, 0, 2))
        self.push((0, 2), (0, 1, 0), (0, 1, 2))
        self.push((0, 2), (1, 0, 0), (1, 0, 2))
        for d in (1, 3):
            self.land((0, 0, d))
            self.push((0, d), (1, 0, 0), (1, 0, d))

    def finish_near(self):
        for d in range(4):
            self.land((1, 0, d))

    def relay_far(self):
        for d in (1, 3, 2):
            self.land((0, 1, d))
            self.push((1, d), (1, 0, 0), (1, 1, d))

    def finish_far(self):
        for d in range(4):
            self.land((1, 1, d))

    def drain(self):
        for copy in self.sent:
            copy.wait_send()


class GatherShort:
    def __init__(self, place, parts, pool, landing, sems):
        self.place, self.parts, self.pool, self.landing, self.sems = place, parts, pool, landing, sems
        self.sent = []

    def pair(self, slot):
        return (self.sems.at[0, slot], self.sems.at[1, slot])

    def push(self, src, dst, slot, device):
        copy = send(src, dst, self.pair(slot), device)
        self.sent.append(copy)
        return copy

    def swap(self, hi):
        half = (self.place.hi + hi) % 2
        start = group_index(self.place, core=1, hi=hi) - self.place.z
        return self.push(
            self.parts.at[pl.ds(start, 4)], self.pool.at[pl.ds(half * 4, 4)], hi, self.place.at(core=1)
        )

    def chunk(self, hi, z):
        return self.pool.at[(self.place.hi + hi) % 2 * 4 + (self.place.z + z) % 4]

    def mine(self, hi, z):
        return self.parts.at[group_index(self.place, hi=hi, z=z)]

    def join(self, hi, z, more=()):
        block = self.chunk(hi, z)
        add_rows(block, [block, self.mine(hi, z), *more])
        return block

    def near(self):
        place, land = self.place, self.landing
        self.direct = []
        for i, d in enumerate((1, 3)):
            self.direct.append(self.push(self.join(0, d), land.at[3 + i], 5 + i, place.at(z=d)))

    def first(self):
        place, land = self.place, self.landing
        self.cross = []
        for i, d in enumerate((1, 3)):
            self.cross.append(self.push(self.join(1, d), land.at[i], 2 + i, place.at(z=d)))
        self.far = self.push(self.join(1, 2), land.at[2], 4, place.at(hi=1))

    def second(self):
        place, land = self.place, self.landing
        for copy in self.cross:
            copy.wait_recv()
        block = self.join(1, 0, [land.at[0], land.at[1]])
        self.last = [self.push(block, land.at[5], 7, place.at(hi=1))]
        self.far.wait_recv()
        block = self.join(0, 2, [land.at[2]])
        self.last.append(self.push(block, land.at[6], 8, place.at(z=2)))

    def finish(self, out):
        for copy in self.direct + self.last:
            copy.wait_recv()
        land = self.landing
        add_rows(out, [self.chunk(0, 0), self.mine(0, 0), land.at[3], land.at[4], land.at[5], land.at[6]])

    def drain(self):
        for copy in self.sent:
            copy.wait_send()


class Columns:
    def __init__(self, place, own, held, sems, own_sem):
        self.place, self.own, self.held, self.sems = place, own, held, sems
        self.sent, self.waits = [], {}
        self.local = pltpu.make_async_copy(own, held.at[0, self.context()], own_sem)
        self.local.start()

    def context(self, lo=0, y=0):
        return (self.place.lo + lo) % 2 * 4 + (self.place.y + y) % 4

    def push(self, src, side, lo, y, device, slot):
        pair = (self.sems.at[0, len(self.sent)], self.sems.at[1, slot])
        copy = send(src, self.held.at[side, self.context(lo, y)], pair, device)
        self.sent.append(copy)
        self.waits[slot] = copy

    def first(self):
        place = self.place
        self.push(self.own, 0, 0, 0, place.at(lo=1), 4)
        for d in (1, 3, 2):
            self.push(self.own, 0, 0, 0, place.at(y=d), (4 - d) % 4)
        self.push(self.own, 1, 0, 0, place.at(core=1), 8)

    def cross(self, lo, y):
        self.waits[lo * 4 + y].wait_recv()
        block = self.held.at[0, self.context(lo, y)]
        self.push(block, 1, lo, y, self.place.at(core=1), 8 + lo * 4 + y)
        return block

    def second(self):
        block = self.cross(1, 0)
        for d in (1, 3, 2):
            self.push(block, 0, 1, 0, self.place.at(y=d), 4 + (4 - d) % 4)
        for d in (1, 3, 2):
            self.cross(0, d)

    def third(self):
        for d in (1, 3, 2):
            self.cross(1, d)

    def finish(self):
        for slot in range(8):
            self.waits[8 + slot].wait_recv()
        self.local.wait()
        for copy in self.sent:
            copy.wait_send()


def contract(left, right, dims):
    return lax.dot_general(left, right, (dims, ((), ())), preferred_element_type=F32)


STREAMS = {
    "o1": ("zxy", 256, 0), "o2": ("zyx", 256, 256), "q1": ("zxy", 256, 512),
    "q2": ("yxz", 128, 768), "s1": ("xzy", 128, 896), "s2": ("zyx", 128, 1024),
}
ALL_WIDE = 1152


def stream_index(order, block, half):
    at = {"x": half * 2 + block // 16, "y": block // 4 % 4, "z": block % 4}
    return tuple(at[axis] for axis in order)


class Streams:
    def __init__(self, place, buffers, sems, mine):
        self.place, self.buffers, self.sems, self.mine = place, buffers, sems, mine
        self.flight, self.sent = {}, []

    def put(self, name, tile, half, grads, begin=0):
        order = STREAMS[name][0]
        width = grads.shape[1]
        for j in range(8):
            index = stream_index(order, tile * 8 + j, half)
            self.buffers[name][0][(*index, slice(None), slice(begin, begin + width))] = (
                grads[j * 48 : (j + 1) * 48]
            )

    def source(self, name, phase):
        return self.buffers[name][2 * phase]

    def launch(self, name, phase):
        begin = list(STREAMS).index(name) * 9 + 3 * phase
        copies = scatter_start(
            self.place, STREAMS[name][0][phase], self.source(name, phase),
            self.buffers[name][2 * phase + 1], self.sems, begin,
        )
        self.flight[name] = copies
        self.sent.extend(copies)

    def land(self, name, phase):
        for copy in self.flight[name]:
            copy.wait_recv()
        order, width, begin = STREAMS[name]
        own = self.source(name, phase).at[self.place.own(order[phase])]
        landing = self.buffers[name][2 * phase + 1]
        if phase == 2:
            total = own[...].astype(F32)
            for d in range(3):
                total = total + landing[d].astype(F32)
            self.mine[:, begin : begin + width] = total.astype(BF)
            return
        out = self.source(name, phase + 1)
        if phase == 1:
            add_up(out, own, landing, 4)
            return

        def body(i, carry):
            a, b = i // 4, i % 4
            total = own[a, b].astype(F32)
            for d in range(3):
                total = total + landing[d, a, b].astype(F32)
            out[a, b] = total.astype(BF)
            return carry

        lax.fori_loop(0, 16, body, 0)

    def step(self, name, phase):
        self.land(name, phase)
        if phase < 2:
            self.launch(name, phase + 1)


def layer_kernel(
    x_far, ids, cot_far, gain_attn, gain_moe, wr, wq, wk, wv, wo, wg_far, wu_far, wd_far,
    mixed_far, gt_far, quarters, experts_far, eg, eu, ed, far_p, far_q, n1t_all,
    kv, qp, lse, attn, y1, n2, gates, turn, dn2r, dgate, eo_pool, home_halves, home_wholes,
    ready, weight_sems, expert_load_sems, own_sem, cots_sems, k_sems, v_sems,
    table_sems, rows_sems, gather_sems, dgate_sems, stage_sems, eo_sems, column_sems, column_sem, far_sems,
    column_load_sems, pair_sems, kv_sems, dense_sems, quarter_sems, home_sems, fold_sems, expert_sems,
    out_sems,
):
    def early(cots, rows, tables, table, pool, landing, n1t, wg, wu, wd):
        expert_loads = [
            pltpu.make_async_copy(far, near, expert_load_sems.at[i])
            for i, (far, near) in enumerate(((wg_far, wg), (wu_far, wu), (wd_far, wd)))
        ]

        def forward(n1, x_ref, wqv, wkv, wov):
            place = Place()
            me = group_index(place)
            context = place.lo * 4 + place.y
            own_copy = pltpu.make_async_copy(cot_far, cots.at[me], own_sem)
            own_copy.start()
            loads = [
                pltpu.make_async_copy(x_far, x_ref, weight_sems.at[4]),
                pltpu.make_async_copy(wk, wkv.at[:, 0:512], weight_sems.at[0]),
                pltpu.make_async_copy(wv, wkv.at[:, 512:1024], weight_sems.at[1]),
                pltpu.make_async_copy(wq, wqv, weight_sems.at[2]),
                pltpu.make_async_copy(wo, wov, weight_sems.at[3]),
            ]
            for load in loads:
                load.start()
            for load in expert_loads:
                load.start()
            greet(
                list(group_peers(place).values())
                + [place.at(y=d) for d in (1, 2, 3)] + [place.at(lo=1), place.at(hi=1, lo=1)]
            )
            lo_peer = place.at(lo=1)
            spread = Spread(place, cots, cots_sems)
            own_copy.wait()
            spread.first()
            loads.pop(0).wait()
            x = x_ref[...].astype(F32)
            n1[...] = (x * inverse_root(x) * gain_attn[...].reshape(1, 1536)).astype(BF)
            lane = lax.broadcasted_iota(jnp.int32, (128, 128), 1)
            row = lax.broadcasted_iota(jnp.int32, (128, 128), 0)
            freqs = jnp.exp((lane % 32).astype(F32) * (-math.log(10000.0) / 32))
            angles = (row + context * 128).astype(F32) * freqs
            cosine = jnp.cos(angles)
            sine = jnp.where(lane % 64 < 32, -1.0, 1.0) * jnp.sin(angles)
            turn[0] = cosine
            turn[1] = sine

            loads[0].wait()
            loads[1].wait()
            for j in range(4):
                raw = contract(n1[...], wkv[:, j * 128 : (j + 1) * 128], ((1,), (0,)))
                kv[0, context, :, j * 128 : (j + 1) * 128] = (raw * cosine + swap_halves(raw) * sine).astype(BF)
            kv[1, context] = contract(n1[...], wkv[:, 512:1024], ((1,), (0,))).astype(BF)

            sent = []
            waits = {}

            def push(which, lo, y, device, slot):
                block = kv.at[which, (place.lo + lo) % 2 * 4 + (place.y + y) % 4]
                sems = (k_sems, v_sems)[which]
                copy = send(block, block, (sems.at[0, slot], sems.at[1, slot]), device)
                sent.append(copy)
                waits[which, slot] = copy

            for which in (0, 1):
                push(which, 0, 0, lo_peer, 4)
                for d in (1, 3, 2):
                    push(which, 0, 0, place.at(y=d), (4 - d) % 4)

            loads[2].wait()
            for j in range(4):
                raw = contract(n1[...], wqv[:, j * 384 : (j + 1) * 384], ((1,), (0,)))
                turned = []
                for r in range(3):
                    block = raw[:, r * 128 : (r + 1) * 128]
                    turned.append((block * cosine + swap_halves(block) * sine) * 0.125)
                for r, block in enumerate(to_pairs(turned)):
                    qp[j, r * 128 : (r + 1) * 128, :] = block.astype(BF)
            waits[0, 4].wait_recv()
            for d in (1, 3, 2):
                push(0, 1, 0, place.at(y=d), 4 + (4 - d) % 4)
            spread.relay_hi()
            for d in (1, 3, 2):
                waits[1, d].wait_recv()
                push(1, 0, d, lo_peer, 4 + d)

            spread.relay(0)
            for j in range(12):
                part = slice(j * 128, (j + 1) * 128)
                n1t[part, :] = n1[:, part].astype(F32).T.astype(BF)

            picked = jnp.zeros((128, 128), F32)
            for k in range(8):
                picked = picked + jnp.where(ids[k : k + 1, :] == row, 1.0, 0.0)
            chosen = picked.T
            earlier = jnp.where(lane < row, 1.0, 0.0).astype(BF)
            before = contract(earlier, chosen.astype(BF), ((1,), (0,)))
            slots = jnp.where(chosen > 0.0, before, -1.0).T
            table[...] = jnp.zeros_like(table)
            for g in range(16):
                table[g, 0:2, :] = slots[2 * g : 2 * g + 2, :]

            for d in (1, 3, 2):
                waits[0, d].wait_recv()
                waits[0, 4 + d].wait_recv()
                waits[1, 4 + d].wait_recv()
            waits[1, 4].wait_recv()
            spread.relay(1)

            def attend(j, carry):
                lanes = pl.ds(pl.multiple_of(j * 128, 128), 128)
                keys = kv[0, :, :, lanes].reshape(1024, 128)
                values = kv[1, :, :, lanes].reshape(1024, 128)
                halves = []
                for s in range(2):
                    scores = contract(keys, qp[j] * half_mask(s), ((1,), (1,)))
                    scores = jnp.where(visible(place, 0, 1024), scores, floor_score)
                    top = jnp.max(scores, axis=0, keepdims=True)
                    probs = jnp.exp(scores - top)
                    total = jnp.sum(probs, axis=0, keepdims=True)
                    lse[j * 2 + s] = top + jnp.log(total)
                    out = contract(values, probs.astype(BF), ((0,), (0,))) * (1.0 / total)
                    halves.append(out[s * 64 : (s + 1) * 64])
                joined = jnp.concatenate(halves, axis=0).T
                for r, block in enumerate(from_pairs([joined[r * 128 : (r + 1) * 128] for r in range(3)])):
                    attn[:, pl.ds(pl.multiple_of(j * 384 + r * 128, 128), 128)] = block.astype(BF)
                return carry

            lax.fori_loop(0, 4, attend, 0)
            spread.last(0)

            loads[3].wait()
            for j in range(4):
                part = slice(j * 384, (j + 1) * 384)
                y1[:, part] = x_ref[:, part].astype(F32) + contract(attn[...], wov[:, part], ((1,), (0,)))
            y = y1[...]
            n2[...] = (y * inverse_root(y) * gain_moe[...].reshape(1, 1536)).astype(BF)
            logits = jnp.concatenate(
                [contract(n2[...], wr[...], ((1,), (1,))), jnp.zeros((128, 96), F32)], axis=1
            )
            logits = jnp.where(chosen > 0.0, logits, -jnp.inf)
            weights = jnp.exp(logits - jnp.max(logits, axis=1, keepdims=True))
            weights = weights / jnp.sum(weights, axis=1, keepdims=True)
            gates[...] = weights
            turned = weights.T
            for g in range(16):
                table[g, 2:4, :] = turned[2 * g : 2 * g + 2, :]
            spread.last(1)
            spread.finish(0)
            spread.finish(1)
            spread.drain()
            for copy in sent:
                copy.wait_send()

        def experts(
            x_rows, c_rows, pick, gate, dg, dhg, dhu, gact, drow, back, dgate_out,
        ):
            place = Place()
            peers = group_peers(place)
            me = group_index(place)
            y_line, lo_device = place.line("y"), place.at(lo=1)

            small = []
            tables[me] = table[me]
            for (c, h, d), device in peers.items():
                slot = c * 8 + h * 4 + d
                pair = (table_sems.at[0, slot], table_sems.at[1, c * 8 + h * 4 + (4 - d) % 4])
                small.append(send(table.at[group_index(place, c, h, d)], tables.at[me], pair, device))
            rows[me] = n2[...]
            spread_rows = SpreadShort(place, rows, rows_sems)
            spread_rows.first()
            columns = Columns(place, n1t, n1t_all, column_sems, column_sem)
            columns.first()
            for copy in small:
                copy.wait_recv()

            slots = lax.broadcasted_iota(jnp.int32, (80, 256), 0).astype(F32)
            second = lax.broadcasted_iota(jnp.int32, (1, 256), 1) >= 128

            def select(pair_index):
                parts = []
                for e in range(2):
                    here = jnp.concatenate(
                        [tables[pair_index * 2, e : e + 1, :], tables[pair_index * 2 + 1, e : e + 1, :]], axis=1
                    )
                    here = jnp.where(here < 0.0, -1000.0, here + jnp.where(second, 40.0, 0.0))
                    weight = jnp.concatenate(
                        [tables[pair_index * 2, 2 + e : 3 + e, :], tables[pair_index * 2 + 1, 2 + e : 3 + e, :]],
                        axis=1,
                    )
                    hit = slots == here
                    parts.append(jnp.where(hit, 1.0, 0.0).astype(BF))
                    place_rows = pl.ds(pl.multiple_of(pair_index * 80, 80), 80)
                    gate[e, place_rows, :] = jnp.sum(jnp.where(hit, weight, 0.0), axis=1, keepdims=True)
                pick[pair_index] = jnp.concatenate(parts, axis=0)

            def pull(pair_index, held, out):
                both = jnp.concatenate([held[pair_index * 2], held[pair_index * 2 + 1]], axis=0)
                picked = contract(pick[pair_index], both, ((1,), (0,))).astype(BF)
                place_rows = pl.ds(pl.multiple_of(pair_index * 80, 80), 80)
                out[0, place_rows, :] = picked[0:80]
                out[1, place_rows, :] = picked[80:160]

            def all_pairs(body):
                def step(i, carry):
                    body(i)
                    return carry
                lax.fori_loop(0, 8, step, 0)

            def side_pairs(c, h, body):
                base = (group_index(place, core=c, hi=h) - place.z) // 2

                def step(i, carry):
                    body(base + i)
                    return carry

                lax.fori_loop(0, 2, step, 0)

            all_pairs(select)
            all_pairs(lambda p: pull(p, cots, c_rows))
            expert_loads[2].wait()

            def back_rows(i, carry):
                e, m = i // 2, i % 2
                part = pl.ds(pl.multiple_of(m * 320, 320), 320)
                back[e, part, :] = contract(c_rows[e, part, :], wd[e], ((1,), (1,)))
                return carry

            lax.fori_loop(0, 4, back_rows, 0)

            def work(h):
                m = (place.hi + h) % 2
                part = pl.ds(pl.multiple_of(m * 320, 320), 320)

                def step(e, carry):
                    x = x_rows[e, part, :]
                    hg = contract(x, wg[e].reshape(1536, 512), ((1,), (0,)))
                    hu = contract(x, wu[e], ((1,), (0,)))
                    turned = back[e, part, :]
                    weight = gate[e, part, :]
                    sig = 1.0 / (1.0 + jnp.exp(-hg))
                    silu = hg * sig
                    act = silu * hu
                    dg[e, part, :] = jnp.sum(act * turned, axis=1, keepdims=True)
                    gact[e, part, :] = (weight * act).astype(BF)
                    dact = weight * turned
                    low_hg = (dact * hu * (sig + silu * (1.0 - sig))).astype(BF)
                    low_hu = (dact * silu).astype(BF)
                    dhg[e, part, :] = low_hg
                    dhu[e, part, :] = low_hu
                    made = (
                        contract(low_hg, wg[e].reshape(1536, 512), ((1,), (1,))) + contract(low_hu, wu[e], ((1,), (1,)))
                    ).astype(BF)
                    for j in range(4):
                        drow[m * 4 + j, pl.ds(pl.multiple_of(e * 80, 80), 80), :] = made[j * 80 : (j + 1) * 80]
                    return carry

                lax.fori_loop(0, 2, step, 0)

            def put_back(pair_index, out):
                both = contract(pick[pair_index], drow[pair_index], ((0,), (0,))).astype(BF)
                out[pair_index * 2] = both[0:128]
                out[pair_index * 2 + 1] = both[128:256]

            def gate_grads(pair_index):
                chosen = pick[pair_index].astype(F32)
                for e in range(2):
                    column = dg[e, pl.ds(pl.multiple_of(pair_index * 80, 80), 80), :]
                    line = jnp.sum(chosen[e * 80 : (e + 1) * 80] * column, axis=0, keepdims=True)
                    dgate_out[pair_index * 2, e : e + 1, :] = line[:, 0:128]
                    dgate_out[pair_index * 2 + 1, e : e + 1, :] = line[:, 128:256]

            home = GatherShort(place, cots, pool, landing, gather_sems)
            spread_rows.relay_a()
            spread_rows.relay_b()
            spread_rows.finish_near()
            side_pairs(0, 0, lambda p: pull(p, rows, x_rows))
            side_pairs(1, 0, lambda p: pull(p, rows, x_rows))
            expert_loads[0].wait()
            expert_loads[1].wait()
            work(0)
            side_pairs(1, 0, lambda p: put_back(p, cots))
            near_swap = home.swap(0)
            spread_rows.relay_far()
            side_pairs(0, 0, lambda p: put_back(p, cots))
            columns.second()
            spread_rows.finish_far()
            side_pairs(0, 1, lambda p: pull(p, rows, x_rows))
            side_pairs(1, 1, lambda p: pull(p, rows, x_rows))
            near_swap.wait_recv()
            home.near()
            work(1)
            side_pairs(1, 1, lambda p: put_back(p, cots))
            far_swap = home.swap(1)
            side_pairs(0, 1, lambda p: put_back(p, cots))
            dgate_out[...] = jnp.zeros_like(dgate_out)
            all_pairs(gate_grads)
            small_back = []
            dgate[me] = dgate_out[me]
            for (c, h, d), device in peers.items():
                slot = c * 8 + h * 4 + d
                pair = (dgate_sems.at[0, slot], dgate_sems.at[1, c * 8 + h * 4 + (4 - d) % 4])
                small_back.append(send(dgate_out.at[group_index(place, c, h, d)], dgate.at[me], pair, device))
            far_swap.wait_recv()
            home.first()
            spread_rows.drain()
            columns.third()

            def outputs(i, carry):
                e, m = i // 2, i % 2
                part = pl.ds(pl.multiple_of(m * 320, 320), 320)
                made = contract(gact[e, part, :], wd[e], ((1,), (0,))).astype(BF)
                for j in range(4):
                    drow[m * 4 + j, pl.ds(pl.multiple_of(e * 80, 80), 80), :] = made[j * 80 : (j + 1) * 80]
                return carry

            lax.fori_loop(0, 4, outputs, 0)
            home.second()
            all_pairs(lambda p: put_back(p, rows))
            outward = Gather(place, rows, eo_pool, None, None, eo_sems)
            out_swaps = [outward.swap(0), outward.swap(1)]
            copies, far = {}, []
            other_lo = (place.lo + 1) % 2
            order = [
                (e, left, right, out, m)
                for left, right, out, m in ((x_rows, dhg, eg, 0), (x_rows, dhu, eu, 1), (c_rows, gact, ed, 2))
                for e in range(2)
            ]

            def forward(step):
                copies[step].wait()
                e, _, _, out, m = order[step]
                if e == 0:
                    for d, (index, device) in enumerate(y_line):
                        pair = (far_sems.at[0, m * 4 + d], far_sems.at[1, m * 4 + d])
                        far.append(send(out.at[0, :, index], far_p.at[d, m], pair, device))
                else:
                    pair = (far_sems.at[0, m * 4 + 3], far_sems.at[1, m * 4 + 3])
                    far.append(send(out.at[1, other_lo], far_q.at[m], pair, lo_device))

            for step, (e, left, right, out, m) in enumerate(order):
                slot = step % 2
                if step >= 2:
                    forward(step - 2)

                def weight_grad(i, carry):
                    tile = pl.ds(pl.multiple_of(i * 384, 128), 384)
                    grads = contract(left[e, :, tile], right[e], ((0,), (0,))).astype(BF)
                    wg[slot, i // 2, pl.ds(i % 2 * 2, 2)] = grads.reshape(2, 192, 512)
                    return carry

                lax.fori_loop(0, 4, weight_grad, 0)
                copies[step] = pltpu.make_async_copy(wg.at[slot], out.at[e], stage_sems.at[slot])
                copies[step].start()
            forward(4)
            forward(5)
            for copy in out_swaps:
                copy.wait_recv()
            for h in range(2):
                for d in range(4):
                    outward.join(h, d)
            home.finish(dn2r)
            for copy in small_back:
                copy.wait_recv()
            for copy in small + small_back:
                copy.wait_send()
            home.drain()
            outward.drain()
            columns.finish()

        pl.run_scoped(
            forward, low(128, 1536), low(128, 1536), low(1536, 1536), low(1536, 1024), low(1536, 1536)
        )
        pl.run_scoped(
            experts, low(2, 640, 1536), low(2, 640, 1536), low(8, 160, 256),
            high(2, 640, 1), high(2, 640, 1), low(2, 640, 512), low(2, 640, 512), low(2, 640, 512),
            low(8, 160, 1536), high(2, 640, 512), high(16, 8, 128),
        )

    def late(
        x_ref, cot, big, w_v, attnc, dqc, dbrc, dkvs, dgt, dbr, dap, delta, dq, dk, dy1, dkv,
        land_a, land_b, land_c, land_d, mine, stage, sum_p, sum_q, land_p2, land_q2, experts, mixed, gt, *rest,
    ):
        buffers = {name: rest[i * 6 : i * 6 + 6] for i, name in enumerate(STREAMS)}
        place = Place()
        context = place.lo * 4 + place.y
        y_line, z_line, x_line = (place.line(axis) for axis in "yzx")
        sibling, cross, lo_device = place.at(core=1), place.at(hi=1, core=1), place.at(lo=1)
        other_lo = (place.lo + 1) % 2
        load_o = pltpu.make_async_copy(wo, big.at[:, 0:1536], weight_sems.at[0])
        load_o.start()
        load_v = pltpu.make_async_copy(wv, w_v, weight_sems.at[1])
        load_v.start()
        load_x = pltpu.make_async_copy(x_far, x_ref, weight_sems.at[3])
        load_x.start()
        load_cot = pltpu.make_async_copy(cot_far, cot, weight_sems.at[4])
        load_cot.start()
        others = [device for line in (y_line, z_line, x_line) for _, device in line] + [sibling, cross]
        for device in others:
            pl.semaphore_signal(ready, inc=1, device_id=device, device_id_type=MESH)
        pl.semaphore_wait(ready, len(others))
        pending = []

        def share(i, source, both):
            pair = (pair_sems.at[0, i], pair_sems.at[1, i])
            copy = send(source, both, pair, sibling)
            pending.append(copy)
            return copy

        lower = pl.ds(128, 128)
        share_attn = share(0, attn, attnc.at[lower])
        attnc[0:128, :] = attn[...]

        home = Gather(place, None, eo_pool, home_halves, home_wholes, home_sems)
        home.first(1)
        home.first(0)

        dgt[...] = jnp.zeros_like(dgt)
        for g in range(16):
            dgt[2 * g : 2 * g + 2, :] = dgate[g, 0:2, :]
        weights = gates[...]
        dgates = dgt[...].T
        dlogits = weights * (dgates - jnp.sum(weights * dgates, axis=1, keepdims=True))
        dlogits = dlogits.astype(BF)
        dn2 = dn2r[...] + contract(dlogits[:, 0:32], wr[...], ((1,), (0,)))
        y = y1[...]
        root = inverse_root(y)
        scaled = dn2 * gain_moe[...].reshape(1, 1536)
        inner = jnp.mean(scaled * y, axis=-1, keepdims=True)
        load_cot.wait()
        dy = cot[...].astype(F32) + root * scaled - y * (root * root * root * inner)
        dy1[...] = dy
        low = dy.astype(BF)
        dbr[0] = low[:, 0:768]
        dbr[1] = low[:, 768:1536]
        share_dbr = share(1, dbr.at[1 - place.core], dbrc.at[lower])
        dbrc[0:128, :] = dbr[place.core]

        load_o.wait()
        for j in range(4):
            back = contract(low, big[j * 384 : (j + 1) * 384, 0:1536], ((1,), (1,)))
            grads = to_pairs([back[:, r * 128 : (r + 1) * 128] for r in range(3)])
            outs = to_pairs(
                [attn[:, j * 384 + r * 128 : j * 384 + (r + 1) * 128].astype(F32) for r in range(3)]
            )
            grads = jnp.concatenate(grads, axis=0).astype(BF)
            dap[j] = grads
            product = (grads.astype(F32) * jnp.concatenate(outs, axis=0)).T
            for s in range(2):
                delta[j * 2 + s] = jnp.sum(product[s * 64 : (s + 1) * 64], axis=0, keepdims=True)
        load_columns = []
        for side in range(2):
            for c in range(8):
                at = side * 8 + c
                load_columns.append(
                    pltpu.make_async_copy(
                        n1t_all.at[side, c], big.at[:, at * 128 : (at + 1) * 128], column_load_sems.at[at]
                    )
                )
                load_columns[-1].start()

        home.second(1)
        home.second(0)
        streams = Streams(place, buffers, dense_sems, mine)
        gain_rows = (dn2 * y * root).astype(BF)
        column = jnp.where(lax.broadcasted_iota(jnp.int32, (128, 128), 1) == 32, 1.0, 0.0).astype(BF)
        narrow_left = jnp.concatenate([n2[...], gain_rows], axis=0)
        narrow_right = jnp.concatenate([dlogits, column], axis=0)
        for tile in range(4):
            part = contract(
                narrow_left[:, tile * 384 : (tile + 1) * 384], narrow_right, ((0,), (0,))
            ).astype(BF)
            for half in range(2):
                streams.put("o2", tile, half, part, 128)
        share_attn.wait_recv()
        share_dbr.wait_recv()
        for tile in range(4):
            for half in range(2):
                grads = contract(
                    attnc[:, tile * 384 : (tile + 1) * 384], dbrc[:, half * 384 : (half + 1) * 384],
                    ((0,), (0,)),
                ).astype(BF)
                streams.put("o1", tile, half, grads[:, 0:256])
                streams.put("o2", tile, half, grads[:, 256:384])
        streams.launch("o1", 0)
        streams.launch("o2", 0)

        cosine, sine = turn[0], turn[1]
        lane = lax.broadcasted_iota(jnp.int32, (1, 128), 1)
        freqs = jnp.exp((lane % 32).astype(F32) * (-math.log(10000.0) / 32))
        sign = jnp.where(lane % 64 < 32, -1.0, 1.0)

        def turn_back(u, cos, sin):
            return u * cos - swap_halves(u) * sin

        def attend(j, carry):
            lanes = pl.ds(pl.multiple_of(j * 128, 128), 128)
            turned = [jnp.zeros((128, 384), F32) for _ in range(2)]
            for block in range(2):
                part = slice(block * 4, (block + 1) * 4)
                keys = kv[0, part, :, lanes].reshape(512, 128)
                values = kv[1, part, :, lanes].reshape(512, 128)
                grad_keys = jnp.zeros((512, 128), F32)
                grad_values = jnp.zeros((512, 128), F32)
                seen = visible(place, block * 512, 512)
                for s in range(2):
                    queries = qp[j] * half_mask(s)
                    grads = dap[j] * half_mask(s)
                    scores = contract(keys, queries, ((1,), (1,)))
                    probs = jnp.exp(jnp.where(seen, scores, floor_score) - lse[j * 2 + s])
                    back = contract(values, grads, ((1,), (1,)))
                    grad_scores = (probs * (back - delta[j * 2 + s])).astype(BF)
                    grad_values = grad_values + contract(probs.astype(BF), grads, ((1,), (0,)))
                    grad_keys = grad_keys + contract(grad_scores, queries, ((1,), (0,)))
                    turned[s] = turned[s] + contract(keys, grad_scores, ((0,), (0,)))
                dkv[part, j, 1] = grad_values.astype(BF).reshape(4, 128, 128)
                for b in range(4):
                    shift = ((block * 4 + b - context) * 128).astype(F32) * freqs
                    cos, sin = jnp.cos(shift), sign * jnp.sin(shift)
                    raw = turn_back(
                        grad_keys[b * 128 : (b + 1) * 128],
                        cosine * cos - sine * sin, sine * cos + cosine * sin,
                    )
                    dkv[block * 4 + b, j, 0] = raw.astype(BF)
            joined = jnp.concatenate([turned[0][0:64], turned[1][64:128]], axis=0).T * 0.125
            blocks = from_pairs([joined[r * 128 : (r + 1) * 128] for r in range(3)])
            for r, part in enumerate(blocks):
                lanes = pl.ds(pl.multiple_of((j % 2) * 384 + r * 128, 128), 128)
                dq[j // 2, :, lanes] = turn_back(part, cosine, sine).astype(BF)
            return carry

        def attend_core(core):
            def step(i, carry):
                return attend(core * 2 + i, carry)

            lax.fori_loop(0, 2, step, 0)

        kv_sent = []

        def kv_push(src, dst, slot, device):
            copy = send(src, dst, (kv_sems.at[0, slot], kv_sems.at[1, slot]), device)
            kv_sent.append(copy)
            return copy

        def kv_add(out, count, terms):
            def body(i, carry):
                a, b, c = i // 4, i // 2 % 2, i % 2
                block = out(a)
                total = block[b, c].astype(F32)
                for term in terms:
                    total = total + term(a)[b, c].astype(F32)
                block[b, c] = total.astype(BF)
                return carry

            lax.fori_loop(0, count * 4, body, 0)

        other = 1 - place.core
        first, later = pl.ds(other * 2, 2), pl.ds(place.core * 2, 2)
        attend_core(other)
        share_dq = share(2, dq.at[other], dqc.at[lower])
        share_dkv = share(3, dkv.at[:, first], dkvs)
        lead = kv_push(dkv.at[pl.ds(other_lo * 4, 4), first], land_a, 0, lo_device)
        streams.step("o1", 0)
        streams.step("o2", 0)
        attend_core(place.core)
        dqc[0:128, :] = dq[place.core]
        share_dq.wait_recv()
        for load in load_columns:
            load.wait()
        own_lanes = pl.ds(pl.multiple_of(context * 128, 128), 128)
        their_lanes = pl.ds(pl.multiple_of(1024 + context * 128, 128), 128)
        for tile in range(4):
            rows = slice(tile * 384, (tile + 1) * 384)
            left = jnp.concatenate([big[rows, own_lanes], big[rows, their_lanes]], axis=1)
            for half in range(2):
                grads = contract(left, dqc[:, half * 384 : (half + 1) * 384], ((1,), (0,))).astype(BF)
                streams.put("q1", tile, half, grads[:, 0:256])
                streams.put("q2", tile, half, grads[:, 256:384])
        streams.launch("q1", 0)
        streams.launch("q2", 0)
        share_dkv.wait_recv()
        own_right = jnp.concatenate(
            [dkv[:, place.core * 2 + h, which].reshape(1024, 128) for h in range(2) for which in range(2)],
            axis=1,
        )
        their_right = jnp.concatenate(
            [dkvs[:, h, which].reshape(1024, 128) for h in range(2) for which in range(2)], axis=1
        )
        for tile in range(4):
            rows = slice(tile * 384, (tile + 1) * 384)
            grads = contract(big[rows, 0:1024], own_right, ((1,), (0,))) + contract(
                big[rows, 1024:2048], their_right, ((1,), (0,))
            )
            grads = grads.astype(BF)
            for half in range(2):
                streams.put("s1", tile, half, grads[:, half * 256 : half * 256 + 128])
                streams.put("s2", tile, half, grads[:, half * 256 + 128 : half * 256 + 256])
        streams.launch("s1", 0)
        streams.launch("s2", 0)
        load_q = pltpu.make_async_copy(wq, big.at[:, 0:1536], weight_sems.at[0])
        load_k = pltpu.make_async_copy(wk, big.at[:, 1536:2048], weight_sems.at[2])
        load_q.start()
        load_k.start()

        legs = []
        for d, (index, device) in enumerate(y_line):
            for lo in range(2):
                legs.append(
                    kv_push(dkv.at[lo * 4 + index, later], land_c.at[d, lo], 4 + d * 2 + lo, device)
                )
        lead.wait_recv()
        share_dkv.wait_send()
        pending.pop()
        kv_add(lambda a: dkv.at[place.lo * 4 + a, first], 4, [lambda a: land_a.at[a]])
        legs_b = [
            kv_push(dkv.at[place.lo * 4 + index, first], land_b.at[d], 1 + d, device)
            for d, (index, device) in enumerate(y_line)
        ]
        home.third()

        mats = (eg, eu, ed)
        second = []

        def fold_expert(m):
            mat = mats[m]
            arrived = [far_p.at[0, 0]] * 3 + [far_q.at[0]]
            for i, block in enumerate(arrived):
                sems = (far_sems.at[0, m * 4 + i], far_sems.at[1, m * 4 + i])
                copy = pltpu.make_async_remote_copy(
                    src_ref=block, dst_ref=block, send_sem=sems[0], recv_sem=sems[1],
                    device_id=sibling, device_id_type=MESH,
                )
                copy.wait()
            steps = []
            for lo in range(2):
                terms = [mat.at[0, lo, place.y]]
                for d in range(3):
                    terms.append(far_p.at[d, m, lo])
                steps.append((terms, sum_p.at[lo, m]))
            for y_at in range(4):
                steps.append(([mat.at[1, place.lo, y_at], far_q.at[m, y_at]], sum_q.at[y_at, m]))

            def fetch(step):
                loads = []
                for i, term in enumerate(steps[step][0]):
                    loads.append(
                        pltpu.make_async_copy(term, stage.at[step % 2, i], fold_sems.at[step % 2, i])
                    )
                    loads[-1].start()
                return loads

            ready = fetch(0)
            for step, (terms, out) in enumerate(steps):
                following = fetch(step + 1) if step + 1 < len(steps) else None
                for load in ready:
                    load.wait()

                def fold(i, carry):
                    part = pl.ds(pl.multiple_of(i * 48, 16), 48)
                    total = stage[step % 2, 0, part].astype(F32)
                    for term in range(1, len(terms)):
                        total = total + stage[step % 2, term, part].astype(F32)
                    out[part] = total.astype(BF)
                    return carry

                lax.fori_loop(0, 4, fold, 0)
                ready = following
            pair = (expert_sems.at[0, 4 + m * 4], expert_sems.at[1, 4 + m * 4])
            second.append(send(sum_p.at[other_lo, m], land_p2.at[m], pair, lo_device))
            for d, (index, device) in enumerate(y_line):
                pair = (expert_sems.at[0, 5 + m * 4 + d], expert_sems.at[1, 5 + m * 4 + d])
                second.append(send(sum_q.at[index, m], land_q2.at[d, m], pair, device))

        fold_expert(0)
        fold_expert(1)
        streams.step("o1", 1)
        streams.step("o2", 1)
        streams.step("q2", 0)
        streams.step("s1", 0)
        streams.step("s2", 0)
        streams.step("q1", 0)
        for copy in legs:
            copy.wait_recv()
        kv_add(
            lambda a: dkv.at[a * 4 + place.y, later], 2,
            [lambda a, d=d: land_c.at[d, a] for d in range(3)],
        )
        leg_d = kv_push(dkv.at[other_lo * 4 + place.y, later], land_d, 10, lo_device)
        streams.step("q2", 1)
        streams.step("s1", 1)
        streams.step("s2", 1)
        streams.step("q1", 1)
        for name in STREAMS:
            streams.land(name, 2)
        own_quarter = place.core * 2 + place.hi
        gathered = []
        for i, (a, b) in enumerate(((0, 1), (1, 0), (1, 1))):
            pair = (quarter_sems.at[0, i], quarter_sems.at[1, i])
            gathered.append(send(mine, quarters.at[own_quarter], pair, place.at(hi=a, core=b)))
        own_quarters = pltpu.make_async_copy(mine, quarters.at[own_quarter], weight_sems.at[5])
        own_quarters.start()

        for copy in legs_b:
            copy.wait_recv()

        def key_grads(core, terms):
            for i in range(2):
                for which in range(2):
                    total = dkv[context, core * 2 + i, which].astype(F32)
                    for term in terms:
                        total = total + term(i, which).astype(F32)
                    lanes = pl.ds(pl.multiple_of((which * 4 + core * 2 + i) * 128, 128), 128)
                    dk[:, lanes] = total.astype(BF)

        key_grads(other, [lambda i, w, d=d: land_b[d, i, w] for d in range(3)])
        leg_d.wait_recv()
        key_grads(place.core, [lambda i, w: land_d[i, w]])
        load_q.wait()
        load_k.wait()
        load_v.wait()
        load_x.wait()
        x = x_ref[...].astype(F32)
        root = inverse_root(x)
        queries = jnp.concatenate([dq[0], dq[1]], axis=1)
        for j in range(4):
            part = slice(j * 384, (j + 1) * 384)
            gt[:, part] = (
                contract(queries, big[part, 0:1536], ((1,), (1,)))
                + contract(dk[:, 0:512], big[part, 1536:2048], ((1,), (1,)))
                + contract(dk[:, 512:1024], w_v[part, :], ((1,), (1,)))
            )
        scaled = gt[...] * gain_attn[...].reshape(1, 1536)
        inner = jnp.mean(scaled * x, axis=-1, keepdims=True)
        gt[...] = dy1[...] + root * scaled - x * (root * root * root * inner)

        outs = [pltpu.make_async_copy(gt, gt_far, out_sems.at[0])]
        outs[0].start()
        fold_expert(2)
        home.finish(mixed, [y1])
        outs.append(pltpu.make_async_copy(mixed, mixed_far, out_sems.at[1]))
        outs[1].start()
        home.drain()
        for copy in gathered:
            copy.wait_recv()
        for copy in second:
            copy.wait_recv()
        for m in range(3):
            def finish(i, carry):
                part = pl.ds(pl.multiple_of(i * 48, 16), 48)
                experts[m, 0, part] = sum_p[place.lo, m, part].astype(F32) + land_p2[m, part].astype(F32)
                total = sum_q[place.y, m, part].astype(F32)
                for d in range(3):
                    total = total + land_q2[d, m, part].astype(F32)
                experts[m, 1, part] = total
                return carry

            lax.fori_loop(0, 4, finish, 0)
        outs.append(pltpu.make_async_copy(experts, experts_far, out_sems.at[2]))
        outs[2].start()
        for copy in pending + kv_sent + gathered + second + streams.sent:
            copy.wait_send()
        own_quarters.wait()
        for copy in outs:
            copy.wait()

    pl.run_scoped(
        early, low(16, 128, 1536), low(16, 128, 1536), high(16, 8, 128), high(16, 8, 128),
        low(8, 128, 1536), low(7, 128, 1536), low(1536, 128),
        low(2, 2, 4, 192, 512), low(2, 1536, 512), low(2, 512, 1536),
    )
    buffers = []
    for _, width, _ in STREAMS.values():
        buffers += [
            low(4, 4, 4, 48, width), low(3, 4, 4, 48, width), low(4, 4, 48, width),
            low(3, 4, 48, width), low(4, 48, width), low(3, 48, width),
        ]
    pl.run_scoped(
        late, low(128, 1536), low(128, 1536), low(1536, 2048), low(1536, 512),
        low(256, 1536), low(256, 768), low(256, 768), low(8, 2, 2, 128, 128),
        high(128, 128), low(2, 128, 768), low(4, 384, 128), high(8, 1, 384),
        low(2, 128, 768), low(128, 1024), high(128, 1536), low(8, 4, 2, 128, 128),
        low(4, 2, 2, 128, 128), low(3, 2, 2, 128, 128), low(3, 2, 2, 2, 128, 128), low(2, 2, 128, 128),
        low(48, ALL_WIDE), low(2, 4, 192, 512),
        low(2, 3, 192, 512), low(4, 3, 192, 512), low(3, 192, 512), low(3, 3, 192, 512),
        high(3, 2, 192, 512), low(128, 1536), high(128, 1536), *buffers,
    )


def run_layer(*operands):
    vmem = pl.BlockSpec(memory_space=pltpu.VMEM)
    hbm = pl.BlockSpec(memory_space=pl.ANY)
    sems = pltpu.SemaphoreType.DMA
    struct = jax.ShapeDtypeStruct
    return pl.pallas_call(
        layer_kernel,
        out_shape=(
            struct((128, 1536), BF), struct((128, 1536), F32), struct((4, 48, ALL_WIDE), BF),
            struct((3, 2, 192, 512), F32),
            *[struct((2, 2, 4, 192, 512), BF)] * 3,
            struct((3, 3, 2, 192, 512), BF), struct((3, 4, 192, 512), BF), struct((2, 8, 1536, 128), BF),
        ),
        in_specs=[hbm, vmem, hbm, vmem, vmem, vmem] + [hbm] * 7,
        out_specs=[hbm] * 10,
        scratch_shapes=[
            low(2, 8, 128, 512), low(4, 384, 128), high(8, 1, 384), low(128, 1536), high(128, 1536),
            low(128, 1536), high(128, 128), high(2, 128, 128), high(128, 1536), high(16, 8, 128),
            low(8, 128, 1536), low(2, 2, 64, 1536), low(5, 128, 1536),
            pltpu.SemaphoreType.REGULAR, sems((6,)), sems((3,)), sems, sems((2, 18)), sems((2, 8)),
            sems((2, 8)),
            sems((2, 16)), sems((2, 16)), sems((2, 9)), sems((2, 16)), sems((2,)), sems((2, 2)),
            sems((2, 16)), sems, sems((2, 12)),
            sems((16,)), sems((2, 4)), sems((2, 11)), sems((2, 9 * len(STREAMS))), sems((2, 3)),
            sems((2, 11)), sems((2, 4)), sems((2, 16)), sems((3,)),
        ],
        compiler_params=pltpu.CompilerParams(
            collective_id=0, has_side_effects=True, vmem_limit_bytes=63 << 20
        ),
    )(*operands)


def finish_kernel(
    mixed, gt, quarters, experts, gain, wq, wk, wv,
    mixed_out, gt_out, gq, gk, gv, go, ga, gm, gr, og, ou, od,
    rows_q, rows_kv, sems,
):
    place = Place()
    start = ((place.lo * 4 + place.y) * 4 + place.z) * 48
    rows = pl.ds(pl.multiple_of(start, 16), 48)
    loads = [
        pltpu.make_async_copy(wq.at[rows, :], rows_q, sems.at[0]),
        pltpu.make_async_copy(wk.at[rows, :], rows_kv.at[0], sems.at[1]),
        pltpu.make_async_copy(wv.at[rows, :], rows_kv.at[1], sems.at[2]),
    ]
    for load in loads:
        load.start()
    mixed_out[0] = mixed[...]
    gt_out[0] = gt[...]
    for q in range(4):
        go[:, q * 384 : (q + 1) * 384] = quarters[q, :, 0:384].astype(F32)
        gq[:, q * 384 : (q + 1) * 384] = quarters[q, :, 512:896].astype(F32)
        gk[:, q * 128 : (q + 1) * 128] = quarters[q, :, 896:1024].astype(F32)
        gv[:, q * 128 : (q + 1) * 128] = quarters[q, :, 1024:1152].astype(F32)
    narrow = quarters[0, :, 384:512].astype(F32) + quarters[2, :, 384:512].astype(F32)
    og[...] = experts[0]
    ou[...] = experts[1]
    for e in range(2):
        od[e] = experts[2, e].T
    for load in loads:
        load.wait()
    line = jnp.sum(gq[...] * rows_q[...].astype(F32), axis=1, keepdims=True)
    line = line + jnp.sum(gk[...] * rows_kv[0].astype(F32), axis=1, keepdims=True)
    line = line + jnp.sum(gv[...] * rows_kv[1].astype(F32), axis=1, keepdims=True)
    column = lax.broadcasted_iota(jnp.int32, (48, 1536), 1) - lax.broadcasted_iota(jnp.int32, (48, 1536), 0)
    own_gain = jnp.sum(jnp.where(column == start, gain[...].reshape(1, 1536), 0.0), axis=1, keepdims=True)
    both = jnp.where(
        lax.broadcasted_iota(jnp.int32, (48, 128), 1) == 33, line / own_gain, narrow
    )
    flat = jnp.concatenate([both, jnp.zeros((80, 128), F32)], axis=0).T
    gr[...] = flat[0:32, 0:48]
    gm[...] = flat[32:33, 0:48]
    ga[...] = flat[33:34, 0:48]


def run_finish(*operands):
    vmem = pl.BlockSpec(memory_space=pltpu.VMEM)
    hbm = pl.BlockSpec(memory_space=pl.ANY)
    f32 = lambda *shape: jax.ShapeDtypeStruct(shape, F32)
    return pl.pallas_call(
        finish_kernel,
        out_shape=(
            jax.ShapeDtypeStruct((1, 128, 1536), BF), f32(1, 128, 1536),
            f32(48, 1536), f32(48, 512), f32(48, 512), f32(48, 1536), f32(1, 48), f32(1, 48), f32(32, 48),
            f32(2, 192, 512), f32(2, 192, 512), f32(2, 512, 192),
        ),
        in_specs=[vmem] * 5 + [hbm] * 3,
        out_specs=[vmem] * 12,
        scratch_shapes=[low(48, 1536), low(2, 48, 512), pltpu.SemaphoreType.DMA((3,))],
        compiler_params=pltpu.CompilerParams(vmem_limit_bytes=63 << 20),
    )(*operands)


def shards(
    tokens, expert_ids, w_query, w_key, w_value, w_out, gain_attn, gain_moe, w_router,
    w_gate, w_up, w_down, cotangent,
):
    mixed, gt, quarters, experts, *_ = run_layer(
        tokens[0], expert_ids[0].T, cotangent[0], gain_attn, gain_moe, w_router.T,
        w_query, w_key, w_value, w_out, w_gate.reshape(2, 2, 4, 192, 512), w_up, w_down,
    )
    mixed, gt, gq, gk, gv, go, ga, gm, gr, og, ou, od = run_finish(
        mixed, gt, quarters, experts, gain_attn, w_query, w_key, w_value
    )
    return (mixed, gt, gq, gk, gv, go, ga.reshape(48), gm.reshape(48), gr.T, og, ou, od)


def solution(mesh):
    in_specs = (
        P(("expert", "dp"), "context", None),
        P(("expert", "dp"), "context", None),
        P(),
        P(),
        P(),
        P(),
        P(),
        P(),
        P(),
        P(("expert", "dp"), None, None),
        P(("expert", "dp"), None, None),
        P(("expert", "dp"), None, None),
        P(("expert", "dp"), "context", None),
    )
    out_specs = (
        P(("expert", "dp"), "context", None),
        P(("expert", "dp"), "context", None),
        P(("context", "dp"), None),
        P(("context", "dp"), None),
        P(("context", "dp"), None),
        P(("context", "dp"), None),
        P(("context", "dp")),
        P(("context", "dp")),
        P(("context", "dp"), None),
        P(("expert", "dp"), "context", None),
        P(("expert", "dp"), "context", None),
        P(("expert", "dp"), None, "context"),
    )
    return jax.shard_map(shards, mesh=mesh, in_specs=in_specs, out_specs=out_specs, check_vma=False)
```

```python
import math

import jax
import jax.numpy as jnp
from jax import lax
from jax.experimental import pallas as pl
from jax.experimental.pallas import tpu as pltpu
from jax.sharding import PartitionSpec as P

epsilon = 1e-06
floor_score = -1e30
MESH = pl.DeviceIdType.MESH
BF = jnp.bfloat16
F32 = jnp.float32


def low(*shape):
    return pltpu.VMEM(shape, BF)


def high(*shape):
    return pltpu.VMEM(shape, F32)


class Place:
    def __init__(self):
        e, c = lax.axis_index("expert"), lax.axis_index("context")
        self.hi, self.core = e // 2, e % 2
        self.lo, self.y = c // 4, c % 4
        self.z = lax.axis_index("dp")

    def at(self, hi=0, core=0, lo=0, y=0, z=0):
        e = (self.hi + hi) % 2 * 2 + (self.core + core) % 2
        c = (self.lo + lo) % 2 * 4 + (self.y + y) % 4
        return (e, c, (self.z + z) % 4)

    def line(self, axis):
        if axis == "y":
            return [((self.y + d) % 4, self.at(y=d)) for d in (1, 2, 3)]
        if axis == "z":
            return [((self.z + d) % 4, self.at(z=d)) for d in (1, 2, 3)]
        return [
            ((self.hi + a) % 2 * 2 + (self.lo + b) % 2, self.at(hi=a, lo=b))
            for a, b in ((0, 1), (1, 0), (1, 1))
        ]

    def own(self, axis):
        return {"y": self.y, "z": self.z, "x": self.hi * 2 + self.lo}[axis]


def greet(devices):
    barrier = pltpu.get_barrier_semaphore()
    for device in devices:
        pl.semaphore_signal(barrier, inc=1, device_id=device, device_id_type=MESH)
    pl.semaphore_wait(barrier, len(devices))


def send(src, dst, sems, device):
    copy = pltpu.make_async_remote_copy(
        src_ref=src, dst_ref=dst, send_sem=sems[0], recv_sem=sems[1],
        device_id=device, device_id_type=MESH,
    )
    copy.start()
    return copy


def scatter_start(place, axis, src, landing, sems, begin):
    copies = []
    for d, (index, device) in enumerate(place.line(axis)):
        pair = (sems.at[0, begin + d], sems.at[1, begin + d])
        copies.append(send(src.at[index], landing.at[d], pair, device))
    return copies


def add_up(out, own, landing, lead):
    count = landing.shape[0]

    def body(i, carry):
        total = own[i].astype(F32)
        for d in range(count):
            total = total + landing[d, i].astype(F32)
        out[i] = total.astype(out.dtype)
        return carry

    lax.fori_loop(0, lead, body, 0)


def roll_lanes(u, shift):
    return pltpu.roll(u, shift, 1)


def swap_halves(u):
    lane = lax.broadcasted_iota(jnp.int32, u.shape, 1)
    return jnp.where(lane % 64 < 32, roll_lanes(u, 96), roll_lanes(u, 32))


def to_pairs(blocks):
    a, b, c = blocks
    low = lax.broadcasted_iota(jnp.int32, a.shape, 1) < 64
    return [
        jnp.where(low, a, b), jnp.where(low, roll_lanes(a, 64), roll_lanes(c, 64)), jnp.where(low, b, c)
    ]


def from_pairs(blocks):
    a, b, c = blocks
    low = lax.broadcasted_iota(jnp.int32, a.shape, 1) < 64
    turned = roll_lanes(b, 64)
    return [jnp.where(low, a, turned), jnp.where(low, c, a), jnp.where(low, turned, c)]


def inverse_root(values):
    return lax.rsqrt(jnp.mean(values * values, axis=-1, keepdims=True) + epsilon)


def visible(place, start, rows):
    key = lax.broadcasted_iota(jnp.int32, (rows, 384), 0) + start
    query = lax.broadcasted_iota(jnp.int32, (rows, 384), 1) % 128
    return key <= query + (place.lo * 4 + place.y) * 128


def half_mask(s):
    lane = lax.broadcasted_iota(jnp.int32, (1, 128), 1)
    return jnp.where((lane >= 64) == (s == 1), 1.0, 0.0).astype(BF)


def group_peers(place):
    return {
        (c, h, d): place.at(core=c, hi=h, z=d)
        for c in (0, 1) for h in (0, 1) for d in range(4) if (c, h, d) != (0, 0, 0)
    }


def group_index(place, core=0, hi=0, z=0):
    return ((place.hi + hi) % 2 * 2 + (place.core + core) % 2) * 4 + (place.z + z) % 4


class Spread:
    def __init__(self, place, held, sems):
        self.place, self.held, self.sems = place, held, sems
        self.sent, self.waits = [], {}

    def push(self, origin, device, slot, rows=None):
        block = self.held.at[group_index(self.place, hi=origin[0], z=origin[1])]
        if rows is not None:
            block = block.at[pl.ds(rows, 64)]
        pair = (self.sems.at[0, len(self.sent)], self.sems.at[1, slot])
        copy = send(block, block, pair, device)
        self.sent.append(copy)
        self.waits[slot] = copy

    def land(self, slot):
        self.waits[slot].wait_recv()

    def around(self, h):
        self.push((h, 0), self.place.at(z=1), h * 4 + 3)
        self.push((h, 0), self.place.at(z=3), h * 4 + 1)

    def first(self):
        self.push((0, 0), self.place.at(hi=1), 4)
        self.around(0)
        self.push((0, 0), self.place.at(core=1), 8)

    def relay_hi(self):
        self.land(4)
        self.around(1)
        self.push((1, 0), self.place.at(core=1), 12)

    def relay(self, h):
        sibling = self.place.at(core=1)
        self.land(h * 4 + 3)
        self.push((h, 3), self.place.at(z=1), h * 4 + 2, 0)
        self.push((h, 3), sibling, 8 + h * 4 + 3)
        self.land(h * 4 + 1)
        self.push((h, 1), self.place.at(z=3), 16 + h, 64)
        self.push((h, 1), sibling, 8 + h * 4 + 1)

    def last(self, h):
        self.land(h * 4 + 2)
        self.land(16 + h)
        self.push((h, 2), self.place.at(core=1), 8 + h * 4 + 2)

    def finish(self, h):
        for d in range(4):
            self.land(8 + h * 4 + d)

    def drain(self):
        for copy in self.sent:
            copy.wait_send()


def add_rows(out, terms):
    def body(i, carry):
        part = pl.ds(pl.multiple_of(i * 16, 16), 16)
        total = terms[0][part].astype(F32)
        for term in terms[1:]:
            total = total + term[part].astype(F32)
        out[part] = total.astype(out.dtype)
        return carry

    lax.fori_loop(0, out.shape[0] // 16, body, 0)


class Gather:
    def __init__(self, place, parts, pool, halves, wholes, sems):
        self.place, self.parts, self.pool, self.sems = place, parts, pool, sems
        self.halves, self.wholes = halves, wholes
        self.sent, self.waits = [], {}

    def push(self, src, dst, slot, device):
        copy = send(src, dst, (self.sems.at[0, slot], self.sems.at[1, slot]), device)
        self.sent.append(copy)
        self.waits[slot] = copy
        return copy

    def swap(self, hi):
        half = (self.place.hi + hi) % 2
        start = group_index(self.place, core=1, hi=hi) - self.place.z
        return self.push(
            self.parts.at[pl.ds(start, 4)], self.pool.at[pl.ds(half * 4, 4)], hi, self.place.at(core=1)
        )

    def chunk(self, hi, z):
        return self.pool.at[(self.place.hi + hi) % 2 * 4 + (self.place.z + z) % 4]

    def terms(self, hi, z):
        if self.parts is None:
            return [self.chunk(hi, z)]
        return [self.chunk(hi, z), self.parts.at[group_index(self.place, hi=hi, z=z)]]

    def join(self, hi, z, more=()):
        block = self.chunk(hi, z)
        if self.parts is not None or more:
            add_rows(block, [*self.terms(hi, z), *more])
        return block

    def first(self, h):
        block = self.join(h, 2)
        upper, lower = pl.ds(0, 64), pl.ds(64, 64)
        self.push(block.at[upper], self.halves.at[h, 0], 2 + h * 4, self.place.at(z=1))
        self.push(block.at[lower], self.halves.at[h, 1], 3 + h * 4, self.place.at(z=3))
        self.join(h, 1)
        self.join(h, 3)

    def second(self, h):
        for side, d in ((0, 1), (1, 3)):
            part = pl.ds(side * 64, 64)
            self.waits[2 + h * 4 + side].wait_recv()
            block = self.chunk(h, d)
            add_rows(block.at[part], [block.at[part], self.halves.at[h, side]])
            self.push(block, self.wholes.at[h * 2 + side], 4 + h * 4 + side, self.place.at(z=d))

    def third(self):
        for side in range(2):
            self.waits[8 + side].wait_recv()
        block = self.join(1, 0, [self.wholes.at[2], self.wholes.at[3]])
        self.push(block, self.wholes.at[4], 10, self.place.at(hi=1))

    def finish(self, out, more=()):
        for slot in (4, 5, 10):
            self.waits[slot].wait_recv()
        add_rows(out, [*more, *self.terms(0, 0)] + [self.wholes.at[i] for i in (0, 1, 4)])

    def drain(self):
        for copy in self.sent:
            copy.wait_send()


class SpreadShort:
    def __init__(self, place, held, sems):
        self.place, self.held, self.sems = place, held, sems
        self.sent, self.waits = [], {}

    def pair(self, c, h, d):
        slot = c * 8 + h * 4 + d
        return (self.sems.at[0, slot], self.sems.at[1, slot])

    def push(self, origin, target, slot):
        c, h, d = target
        index = group_index(self.place, hi=origin[0], z=origin[1])
        block = self.held.at[index]
        copy = send(block, block, self.pair(*slot), self.place.at(core=c, hi=h, z=d))
        self.sent.append(copy)
        self.waits[slot] = copy

    def land(self, slot):
        self.waits[slot].wait_recv()

    def first(self):
        for d in (1, 3, 2):
            self.push((0, 0), (0, 0, d), (0, 0, (4 - d) % 4))
        self.push((0, 0), (0, 1, 0), (0, 1, 0))
        self.push((0, 0), (1, 0, 0), (1, 0, 0))

    def relay_a(self):
        self.land((0, 1, 0))
        for d in (1, 3):
            self.push((1, 0), (0, 0, d), (0, 1, (4 - d) % 4))
        self.push((1, 0), (1, 0, 0), (1, 1, 0))

    def relay_b(self):
        self.land((0, 0, 2))
        self.push((0, 2), (0, 1, 0), (0, 1, 2))
        self.push((0, 2), (1, 0, 0), (1, 0, 2))
        for d in (1, 3):
            self.land((0, 0, d))
            self.push((0, d), (1, 0, 0), (1, 0, d))

    def finish_near(self):
        for d in range(4):
            self.land((1, 0, d))

    def relay_far(self):
        for d in (1, 3, 2):
            self.land((0, 1, d))
            self.push((1, d), (1, 0, 0), (1, 1, d))

    def finish_far(self):
        for d in range(4):
            self.land((1, 1, d))

    def drain(self):
        for copy in self.sent:
            copy.wait_send()


class GatherShort:
    def __init__(self, place, parts, pool, landing, sems):
        self.place, self.parts, self.pool, self.landing, self.sems = place, parts, pool, landing, sems
        self.sent = []

    def pair(self, slot):
        return (self.sems.at[0, slot], self.sems.at[1, slot])

    def push(self, src, dst, slot, device):
        copy = send(src, dst, self.pair(slot), device)
        self.sent.append(copy)
        return copy

    def swap(self, hi):
        half = (self.place.hi + hi) % 2
        start = group_index(self.place, core=1, hi=hi) - self.place.z
        return self.push(
            self.parts.at[pl.ds(start, 4)], self.pool.at[pl.ds(half * 4, 4)], hi, self.place.at(core=1)
        )

    def chunk(self, hi, z):
        return self.pool.at[(self.place.hi + hi) % 2 * 4 + (self.place.z + z) % 4]

    def mine(self, hi, z):
        return self.parts.at[group_index(self.place, hi=hi, z=z)]

    def join(self, hi, z, more=()):
        block = self.chunk(hi, z)
        add_rows(block, [block, self.mine(hi, z), *more])
        return block

    def near(self):
        place, land = self.place, self.landing
        self.direct = []
        for i, d in enumerate((1, 3)):
            self.direct.append(self.push(self.join(0, d), land.at[3 + i], 5 + i, place.at(z=d)))

    def first(self):
        place, land = self.place, self.landing
        self.cross = []
        for i, d in enumerate((1, 3)):
            self.cross.append(self.push(self.join(1, d), land.at[i], 2 + i, place.at(z=d)))
        self.far = self.push(self.join(1, 2), land.at[2], 4, place.at(hi=1))

    def second(self):
        place, land = self.place, self.landing
        for copy in self.cross:
            copy.wait_recv()
        block = self.join(1, 0, [land.at[0], land.at[1]])
        self.last = [self.push(block, land.at[5], 7, place.at(hi=1))]
        self.far.wait_recv()
        block = self.join(0, 2, [land.at[2]])
        self.last.append(self.push(block, land.at[6], 8, place.at(z=2)))

    def finish(self, out):
        for copy in self.direct + self.last:
            copy.wait_recv()
        land = self.landing
        add_rows(out, [self.chunk(0, 0), self.mine(0, 0), land.at[3], land.at[4], land.at[5], land.at[6]])

    def drain(self):
        for copy in self.sent:
            copy.wait_send()


class Columns:
    def __init__(self, place, own, held, sems, own_sem):
        self.place, self.own, self.held, self.sems = place, own, held, sems
        self.sent, self.waits = [], {}
        self.local = pltpu.make_async_copy(own, held.at[0, self.context()], own_sem)
        self.local.start()

    def context(self, lo=0, y=0):
        return (self.place.lo + lo) % 2 * 4 + (self.place.y + y) % 4

    def push(self, src, side, lo, y, device, slot):
        pair = (self.sems.at[0, len(self.sent)], self.sems.at[1, slot])
        copy = send(src, self.held.at[side, self.context(lo, y)], pair, device)
        self.sent.append(copy)
        self.waits[slot] = copy

    def first(self):
        place = self.place
        self.push(self.own, 0, 0, 0, place.at(lo=1), 4)
        for d in (1, 3, 2):
            self.push(self.own, 0, 0, 0, place.at(y=d), (4 - d) % 4)
        self.push(self.own, 1, 0, 0, place.at(core=1), 8)

    def cross(self, lo, y):
        self.waits[lo * 4 + y].wait_recv()
        block = self.held.at[0, self.context(lo, y)]
        self.push(block, 1, lo, y, self.place.at(core=1), 8 + lo * 4 + y)
        return block

    def second(self):
        block = self.cross(1, 0)
        for d in (1, 3, 2):
            self.push(block, 0, 1, 0, self.place.at(y=d), 4 + (4 - d) % 4)
        for d in (1, 3, 2):
            self.cross(0, d)

    def third(self):
        for d in (1, 3, 2):
            self.cross(1, d)

    def finish(self):
        for slot in range(8):
            self.waits[8 + slot].wait_recv()
        self.local.wait()
        for copy in self.sent:
            copy.wait_send()


def contract(left, right, dims):
    return lax.dot_general(left, right, (dims, ((), ())), preferred_element_type=F32)


STREAMS = {
    "o1": ("yxz", 256, 0), "o2": ("zyx", 256, 256), "q1": ("zxy", 256, 512),
    "q2": ("yxz", 128, 768), "s1": ("xzy", 128, 896), "s2": ("zyx", 128, 1024),
}
ALL_WIDE = 1152


def stream_index(order, block, half):
    at = {"x": half * 2 + block // 16, "y": block // 4 % 4, "z": block % 4}
    return tuple(at[axis] for axis in order)


class Streams:
    def __init__(self, place, buffers, sems, mine):
        self.place, self.buffers, self.sems, self.mine = place, buffers, sems, mine
        self.flight, self.sent = {}, []

    def put(self, name, tile, half, grads, begin=0):
        order = STREAMS[name][0]
        width = grads.shape[1]
        for j in range(8):
            index = stream_index(order, tile * 8 + j, half)
            self.buffers[name][0][(*index, slice(None), slice(begin, begin + width))] = (
                grads[j * 48 : (j + 1) * 48]
            )

    def source(self, name, phase):
        return self.buffers[name][2 * phase]

    def launch(self, name, phase):
        begin = list(STREAMS).index(name) * 9 + 3 * phase
        copies = scatter_start(
            self.place, STREAMS[name][0][phase], self.source(name, phase),
            self.buffers[name][2 * phase + 1], self.sems, begin,
        )
        self.flight[name] = copies
        self.sent.extend(copies)

    def land(self, name, phase):
        for copy in self.flight[name]:
            copy.wait_recv()
        order, width, begin = STREAMS[name]
        own = self.source(name, phase).at[self.place.own(order[phase])]
        landing = self.buffers[name][2 * phase + 1]
        if phase == 2:
            total = own[...].astype(F32)
            for d in range(3):
                total = total + landing[d].astype(F32)
            self.mine[:, begin : begin + width] = total.astype(BF)
            return
        out = self.source(name, phase + 1)
        if phase == 1:
            add_up(out, own, landing, 4)
            return

        def body(i, carry):
            a, b = i // 4, i % 4
            total = own[a, b].astype(F32)
            for d in range(3):
                total = total + landing[d, a, b].astype(F32)
            out[a, b] = total.astype(BF)
            return carry

        lax.fori_loop(0, 16, body, 0)

    def step(self, name, phase):
        self.land(name, phase)
        if phase < 2:
            self.launch(name, phase + 1)


def layer_kernel(
    x_far, ids, cot_far, gain_attn, gain_moe, wr, wq, wk, wv, wo, wg_far, wu_far, wd_far,
    mixed_far, gt_far, quarters, experts_far, eg, eu, ed, far_p, far_q, n1t_all,
    kv, qp, lse, attn, y1, n2, gates, turn, dn2r, dgate, eo_pool, home_halves, home_wholes,
    ready, weight_sems, expert_load_sems, own_sem, cots_sems, k_sems, v_sems,
    table_sems, rows_sems, gather_sems, dgate_sems, stage_sems, eo_sems, column_sems, column_sem, far_sems,
    column_load_sems, pair_sems, kv_sems, dense_sems, quarter_sems, home_sems, fold_sems, expert_sems,
    out_sems,
):
    def early(cots, rows, tables, table, pool, landing, n1t, wg, wu, wd):
        expert_loads = [
            pltpu.make_async_copy(far, near, expert_load_sems.at[i])
            for i, (far, near) in enumerate(((wg_far, wg), (wu_far, wu), (wd_far, wd)))
        ]

        def forward(n1, x_ref, wqv, wkv, wov):
            place = Place()
            me = group_index(place)
            context = place.lo * 4 + place.y
            own_copy = pltpu.make_async_copy(cot_far, cots.at[me], own_sem)
            own_copy.start()
            loads = [
                pltpu.make_async_copy(x_far, x_ref, weight_sems.at[4]),
                pltpu.make_async_copy(wk, wkv.at[:, 0:512], weight_sems.at[0]),
                pltpu.make_async_copy(wv, wkv.at[:, 512:1024], weight_sems.at[1]),
                pltpu.make_async_copy(wq, wqv, weight_sems.at[2]),
                pltpu.make_async_copy(wo, wov, weight_sems.at[3]),
            ]
            for load in loads:
                load.start()
            for load in expert_loads:
                load.start()
            greet(
                list(group_peers(place).values())
                + [place.at(y=d) for d in (1, 2, 3)] + [place.at(lo=1), place.at(hi=1, lo=1)]
            )
            lo_peer = place.at(lo=1)
            spread = Spread(place, cots, cots_sems)
            own_copy.wait()
            spread.first()
            loads.pop(0).wait()
            x = x_ref[...].astype(F32)
            n1[...] = (x * inverse_root(x) * gain_attn[...].reshape(1, 1536)).astype(BF)
            lane = lax.broadcasted_iota(jnp.int32, (128, 128), 1)
            row = lax.broadcasted_iota(jnp.int32, (128, 128), 0)
            freqs = jnp.exp((lane % 32).astype(F32) * (-math.log(10000.0) / 32))
            angles = (row + context * 128).astype(F32) * freqs
            cosine = jnp.cos(angles)
            sine = jnp.where(lane % 64 < 32, -1.0, 1.0) * jnp.sin(angles)
            turn[0] = cosine
            turn[1] = sine

            loads[0].wait()
            loads[1].wait()
            for j in range(4):
                raw = contract(n1[...], wkv[:, j * 128 : (j + 1) * 128], ((1,), (0,)))
                kv[0, context, :, j * 128 : (j + 1) * 128] = (raw * cosine + swap_halves(raw) * sine).astype(BF)
            kv[1, context] = contract(n1[...], wkv[:, 512:1024], ((1,), (0,))).astype(BF)

            sent = []
            waits = {}

            def push(which, lo, y, device, slot):
                block = kv.at[which, (place.lo + lo) % 2 * 4 + (place.y + y) % 4]
                sems = (k_sems, v_sems)[which]
                copy = send(block, block, (sems.at[0, slot], sems.at[1, slot]), device)
                sent.append(copy)
                waits[which, slot] = copy

            for which in (0, 1):
                push(which, 0, 0, lo_peer, 4)
                for d in (1, 3, 2):
                    push(which, 0, 0, place.at(y=d), (4 - d) % 4)

            loads[2].wait()
            for j in range(4):
                raw = contract(n1[...], wqv[:, j * 384 : (j + 1) * 384], ((1,), (0,)))
                turned = []
                for r in range(3):
                    block = raw[:, r * 128 : (r + 1) * 128]
                    turned.append((block * cosine + swap_halves(block) * sine) * 0.125)
                for r, block in enumerate(to_pairs(turned)):
                    qp[j, r * 128 : (r + 1) * 128, :] = block.astype(BF)
            waits[0, 4].wait_recv()
            for d in (1, 3, 2):
                push(0, 1, 0, place.at(y=d), 4 + (4 - d) % 4)
            spread.relay_hi()
            for d in (1, 3, 2):
                waits[1, d].wait_recv()
                push(1, 0, d, lo_peer, 4 + d)

            spread.relay(0)
            for j in range(12):
                part = slice(j * 128, (j + 1) * 128)
                n1t[part, :] = n1[:, part].astype(F32).T.astype(BF)

            picked = jnp.zeros((128, 128), F32)
            for k in range(8):
                picked = picked + jnp.where(ids[k : k + 1, :] == row, 1.0, 0.0)
            chosen = picked.T
            earlier = jnp.where(lane < row, 1.0, 0.0).astype(BF)
            before = contract(earlier, chosen.astype(BF), ((1,), (0,)))
            slots = jnp.where(chosen > 0.0, before, -1.0).T
            table[...] = jnp.zeros_like(table)
            for g in range(16):
                table[g, 0:2, :] = slots[2 * g : 2 * g + 2, :]

            for d in (1, 3, 2):
                waits[0, d].wait_recv()
                waits[0, 4 + d].wait_recv()
                waits[1, 4 + d].wait_recv()
            waits[1, 4].wait_recv()
            spread.relay(1)

            def attend(j, carry):
                lanes = pl.ds(pl.multiple_of(j * 128, 128), 128)
                keys = kv[0, :, :, lanes].reshape(1024, 128)
                values = kv[1, :, :, lanes].reshape(1024, 128)
                halves = []
                for s in range(2):
                    scores = contract(keys, qp[j] * half_mask(s), ((1,), (1,)))
                    scores = jnp.where(visible(place, 0, 1024), scores, floor_score)
                    top = jnp.max(scores, axis=0, keepdims=True)
                    probs = jnp.exp(scores - top)
                    total = jnp.sum(probs, axis=0, keepdims=True)
                    lse[j * 2 + s] = top + jnp.log(total)
                    out = contract(values, probs.astype(BF), ((0,), (0,))) * (1.0 / total)
                    halves.append(out[s * 64 : (s + 1) * 64])
                joined = jnp.concatenate(halves, axis=0).T
                for r, block in enumerate(from_pairs([joined[r * 128 : (r + 1) * 128] for r in range(3)])):
                    attn[:, pl.ds(pl.multiple_of(j * 384 + r * 128, 128), 128)] = block.astype(BF)
                return carry

            lax.fori_loop(0, 4, attend, 0)
            spread.last(0)

            loads[3].wait()
            for j in range(4):
                part = slice(j * 384, (j + 1) * 384)
                y1[:, part] = x_ref[:, part].astype(F32) + contract(attn[...], wov[:, part], ((1,), (0,)))
            y = y1[...]
            n2[...] = (y * inverse_root(y) * gain_moe[...].reshape(1, 1536)).astype(BF)
            logits = jnp.concatenate(
                [contract(n2[...], wr[...], ((1,), (1,))), jnp.zeros((128, 96), F32)], axis=1
            )
            logits = jnp.where(chosen > 0.0, logits, -jnp.inf)
            weights = jnp.exp(logits - jnp.max(logits, axis=1, keepdims=True))
            weights = weights / jnp.sum(weights, axis=1, keepdims=True)
            gates[...] = weights
            turned = weights.T
            for g in range(16):
                table[g, 2:4, :] = turned[2 * g : 2 * g + 2, :]
            spread.last(1)
            spread.finish(0)
            spread.finish(1)
            spread.drain()
            for copy in sent:
                copy.wait_send()

        def experts(
            x_rows, c_rows, pick, gate, dg, dhg, dhu, gact, drow, back, dgate_out,
        ):
            place = Place()
            peers = group_peers(place)
            me = group_index(place)
            y_line, lo_device = place.line("y"), place.at(lo=1)

            small = []
            tables[me] = table[me]
            for (c, h, d), device in peers.items():
                slot = c * 8 + h * 4 + d
                pair = (table_sems.at[0, slot], table_sems.at[1, c * 8 + h * 4 + (4 - d) % 4])
                small.append(send(table.at[group_index(place, c, h, d)], tables.at[me], pair, device))
            rows[me] = n2[...]
            spread_rows = SpreadShort(place, rows, rows_sems)
            spread_rows.first()
            columns = Columns(place, n1t, n1t_all, column_sems, column_sem)
            columns.first()
            for copy in small:
                copy.wait_recv()

            slots = lax.broadcasted_iota(jnp.int32, (80, 256), 0).astype(F32)
            second = lax.broadcasted_iota(jnp.int32, (1, 256), 1) >= 128

            def select(pair_index):
                parts = []
                for e in range(2):
                    here = jnp.concatenate(
                        [tables[pair_index * 2, e : e + 1, :], tables[pair_index * 2 + 1, e : e + 1, :]], axis=1
                    )
                    here = jnp.where(here < 0.0, -1000.0, here + jnp.where(second, 40.0, 0.0))
                    weight = jnp.concatenate(
                        [tables[pair_index * 2, 2 + e : 3 + e, :], tables[pair_index * 2 + 1, 2 + e : 3 + e, :]],
                        axis=1,
                    )
                    hit = slots == here
                    parts.append(jnp.where(hit, 1.0, 0.0).astype(BF))
                    place_rows = pl.ds(pl.multiple_of(pair_index * 80, 80), 80)
                    gate[e, place_rows, :] = jnp.sum(jnp.where(hit, weight, 0.0), axis=1, keepdims=True)
                pick[pair_index] = jnp.concatenate(parts, axis=0)

            def pull(pair_index, held, out):
                both = jnp.concatenate([held[pair_index * 2], held[pair_index * 2 + 1]], axis=0)
                picked = contract(pick[pair_index], both, ((1,), (0,))).astype(BF)
                place_rows = pl.ds(pl.multiple_of(pair_index * 80, 80), 80)
                out[0, place_rows, :] = picked[0:80]
                out[1, place_rows, :] = picked[80:160]

            def all_pairs(body):
                def step(i, carry):
                    body(i)
                    return carry
                lax.fori_loop(0, 8, step, 0)

            def side_pairs(c, h, body):
                base = (group_index(place, core=c, hi=h) - place.z) // 2

                def step(i, carry):
                    body(base + i)
                    return carry

                lax.fori_loop(0, 2, step, 0)

            all_pairs(select)
            all_pairs(lambda p: pull(p, cots, c_rows))
            expert_loads[2].wait()

            def back_rows(i, carry):
                e, m = i // 2, i % 2
                part = pl.ds(pl.multiple_of(m * 320, 320), 320)
                back[e, part, :] = contract(c_rows[e, part, :], wd[e], ((1,), (1,)))
                return carry

            lax.fori_loop(0, 4, back_rows, 0)

            def work(h):
                m = (place.hi + h) % 2
                part = pl.ds(pl.multiple_of(m * 320, 320), 320)

                def step(e, carry):
                    x = x_rows[e, part, :]
                    hg = contract(x, wg[e].reshape(1536, 512), ((1,), (0,)))
                    hu = contract(x, wu[e], ((1,), (0,)))
                    turned = back[e, part, :]
                    weight = gate[e, part, :]
                    sig = 1.0 / (1.0 + jnp.exp(-hg))
                    silu = hg * sig
                    act = silu * hu
                    dg[e, part, :] = jnp.sum(act * turned, axis=1, keepdims=True)
                    gact[e, part, :] = (weight * act).astype(BF)
                    dact = weight * turned
                    low_hg = (dact * hu * (sig + silu * (1.0 - sig))).astype(BF)
                    low_hu = (dact * silu).astype(BF)
                    dhg[e, part, :] = low_hg
                    dhu[e, part, :] = low_hu
                    made = (
                        contract(low_hg, wg[e].reshape(1536, 512), ((1,), (1,))) + contract(low_hu, wu[e], ((1,), (1,)))
                    ).astype(BF)
                    for j in range(4):
                        drow[m * 4 + j, pl.ds(pl.multiple_of(e * 80, 80), 80), :] = made[j * 80 : (j + 1) * 80]
                    return carry

                lax.fori_loop(0, 2, step, 0)

            def put_back(pair_index, out):
                both = contract(pick[pair_index], drow[pair_index], ((0,), (0,))).astype(BF)
                out[pair_index * 2] = both[0:128]
                out[pair_index * 2 + 1] = both[128:256]

            def gate_grads(pair_index):
                chosen = pick[pair_index].astype(F32)
                for e in range(2):
                    column = dg[e, pl.ds(pl.multiple_of(pair_index * 80, 80), 80), :]
                    line = jnp.sum(chosen[e * 80 : (e + 1) * 80] * column, axis=0, keepdims=True)
                    dgate_out[pair_index * 2, e : e + 1, :] = line[:, 0:128]
                    dgate_out[pair_index * 2 + 1, e : e + 1, :] = line[:, 128:256]

            home = GatherShort(place, cots, pool, landing, gather_sems)
            spread_rows.relay_a()
            spread_rows.relay_b()
            spread_rows.finish_near()
            side_pairs(0, 0, lambda p: pull(p, rows, x_rows))
            side_pairs(1, 0, lambda p: pull(p, rows, x_rows))
            expert_loads[0].wait()
            expert_loads[1].wait()
            work(0)
            side_pairs(1, 0, lambda p: put_back(p, cots))
            near_swap = home.swap(0)
            spread_rows.relay_far()
            side_pairs(0, 0, lambda p: put_back(p, cots))
            columns.second()
            spread_rows.finish_far()
            side_pairs(0, 1, lambda p: pull(p, rows, x_rows))
            side_pairs(1, 1, lambda p: pull(p, rows, x_rows))
            near_swap.wait_recv()
            home.near()
            work(1)
            side_pairs(1, 1, lambda p: put_back(p, cots))
            far_swap = home.swap(1)
            side_pairs(0, 1, lambda p: put_back(p, cots))
            dgate_out[...] = jnp.zeros_like(dgate_out)
            all_pairs(gate_grads)
            small_back = []
            dgate[me] = dgate_out[me]
            for (c, h, d), device in peers.items():
                slot = c * 8 + h * 4 + d
                pair = (dgate_sems.at[0, slot], dgate_sems.at[1, c * 8 + h * 4 + (4 - d) % 4])
                small_back.append(send(dgate_out.at[group_index(place, c, h, d)], dgate.at[me], pair, device))
            far_swap.wait_recv()
            home.first()
            spread_rows.drain()
            columns.third()

            copies, far = {}, []
            other_lo = (place.lo + 1) % 2
            order = [
                (e, left, right, out, m)
                for left, right, out, m in ((x_rows, dhg, eg, 0), (x_rows, dhu, eu, 1), (c_rows, gact, ed, 2))
                for e in range(2)
            ]

            def forward(step):
                copies[step].wait()
                e, _, _, out, m = order[step]
                if e == 0:
                    for d, (index, device) in enumerate(y_line):
                        pair = (far_sems.at[0, m * 4 + d], far_sems.at[1, m * 4 + d])
                        far.append(send(out.at[0, :, index], far_p.at[d, m], pair, device))
                else:
                    pair = (far_sems.at[0, m * 4 + 3], far_sems.at[1, m * 4 + 3])
                    far.append(send(out.at[1, other_lo], far_q.at[m], pair, lo_device))

            for step, (e, left, right, out, m) in enumerate(order):
                slot = step % 2
                if step >= 2:
                    forward(step - 2)

                def weight_grad(i, carry):
                    tile = pl.ds(pl.multiple_of(i * 384, 128), 384)
                    grads = contract(left[e, :, tile], right[e], ((0,), (0,))).astype(BF)
                    wg[slot, i // 2, pl.ds(i % 2 * 2, 2)] = grads.reshape(2, 192, 512)
                    return carry

                lax.fori_loop(0, 4, weight_grad, 0)
                copies[step] = pltpu.make_async_copy(wg.at[slot], out.at[e], stage_sems.at[slot])
                copies[step].start()
                if step == 2:
                    home.second()
            forward(4)
            forward(5)

            def outputs(i, carry):
                e, m = i // 2, i % 2
                part = pl.ds(pl.multiple_of(m * 320, 320), 320)
                made = contract(gact[e, part, :], wd[e], ((1,), (0,))).astype(BF)
                for j in range(4):
                    drow[m * 4 + j, pl.ds(pl.multiple_of(e * 80, 80), 80), :] = made[j * 80 : (j + 1) * 80]
                return carry

            lax.fori_loop(0, 4, outputs, 0)
            all_pairs(lambda p: put_back(p, rows))
            outward = Gather(place, rows, eo_pool, None, None, eo_sems)
            out_swaps = [outward.swap(0), outward.swap(1)]
            for copy in out_swaps:
                copy.wait_recv()
            for h in range(2):
                for d in range(4):
                    outward.join(h, d)
            home.finish(dn2r)
            for copy in small_back:
                copy.wait_recv()
            for copy in small + small_back:
                copy.wait_send()
            home.drain()
            outward.drain()
            columns.finish()

        pl.run_scoped(
            forward, low(128, 1536), low(128, 1536), low(1536, 1536), low(1536, 1024), low(1536, 1536)
        )
        pl.run_scoped(
            experts, low(2, 640, 1536), low(2, 640, 1536), low(8, 160, 256),
            high(2, 640, 1), high(2, 640, 1), low(2, 640, 512), low(2, 640, 512), low(2, 640, 512),
            low(8, 160, 1536), high(2, 640, 512), high(16, 8, 128),
        )

    def late(
        x_ref, cot, big, w_v, attnc, dqc, dbrc, dkvs, dgt, dbr, dap, delta, dq, dk, dy1, dkv,
        land_a, land_b, land_c, land_d, mine, stage, sum_p, sum_q, land_p2, land_q2, experts, mixed, gt, *rest,
    ):
        buffers = {name: rest[i * 6 : i * 6 + 6] for i, name in enumerate(STREAMS)}
        place = Place()
        context = place.lo * 4 + place.y
        y_line, z_line, x_line = (place.line(axis) for axis in "yzx")
        sibling, cross, lo_device = place.at(core=1), place.at(hi=1, core=1), place.at(lo=1)
        other_lo = (place.lo + 1) % 2
        load_o = pltpu.make_async_copy(wo, big.at[:, 0:1536], weight_sems.at[0])
        load_o.start()
        load_v = pltpu.make_async_copy(wv, w_v, weight_sems.at[1])
        load_v.start()
        load_x = pltpu.make_async_copy(x_far, x_ref, weight_sems.at[3])
        load_x.start()
        load_cot = pltpu.make_async_copy(cot_far, cot, weight_sems.at[4])
        load_cot.start()
        others = [device for line in (y_line, z_line, x_line) for _, device in line] + [sibling, cross]
        for device in others:
            pl.semaphore_signal(ready, inc=1, device_id=device, device_id_type=MESH)
        pl.semaphore_wait(ready, len(others))
        pending = []

        def share(i, source, both):
            pair = (pair_sems.at[0, i], pair_sems.at[1, i])
            copy = send(source, both, pair, sibling)
            pending.append(copy)
            return copy

        lower = pl.ds(128, 128)
        share_attn = share(0, attn, attnc.at[lower])
        attnc[0:128, :] = attn[...]

        home = Gather(place, None, eo_pool, home_halves, home_wholes, home_sems)
        home.first(1)
        home.first(0)

        dgt[...] = jnp.zeros_like(dgt)
        for g in range(16):
            dgt[2 * g : 2 * g + 2, :] = dgate[g, 0:2, :]
        weights = gates[...]
        dgates = dgt[...].T
        dlogits = weights * (dgates - jnp.sum(weights * dgates, axis=1, keepdims=True))
        dlogits = dlogits.astype(BF)
        dn2 = dn2r[...] + contract(dlogits[:, 0:32], wr[...], ((1,), (0,)))
        y = y1[...]
        root = inverse_root(y)
        scaled = dn2 * gain_moe[...].reshape(1, 1536)
        inner = jnp.mean(scaled * y, axis=-1, keepdims=True)
        load_cot.wait()
        dy = cot[...].astype(F32) + root * scaled - y * (root * root * root * inner)
        dy1[...] = dy
        low = dy.astype(BF)
        dbr[0] = low[:, 0:768]
        dbr[1] = low[:, 768:1536]
        share_dbr = share(1, dbr.at[1 - place.core], dbrc.at[lower])
        dbrc[0:128, :] = dbr[place.core]

        load_o.wait()
        for j in range(4):
            back = contract(low, big[j * 384 : (j + 1) * 384, 0:1536], ((1,), (1,)))
            grads = to_pairs([back[:, r * 128 : (r + 1) * 128] for r in range(3)])
            outs = to_pairs(
                [attn[:, j * 384 + r * 128 : j * 384 + (r + 1) * 128].astype(F32) for r in range(3)]
            )
            grads = jnp.concatenate(grads, axis=0).astype(BF)
            dap[j] = grads
            product = (grads.astype(F32) * jnp.concatenate(outs, axis=0)).T
            for s in range(2):
                delta[j * 2 + s] = jnp.sum(product[s * 64 : (s + 1) * 64], axis=0, keepdims=True)
        load_columns = []
        for side in range(2):
            for c in range(8):
                at = side * 8 + c
                load_columns.append(
                    pltpu.make_async_copy(
                        n1t_all.at[side, c], big.at[:, at * 128 : (at + 1) * 128], column_load_sems.at[at]
                    )
                )
                load_columns[-1].start()

        home.second(1)
        home.second(0)
        streams = Streams(place, buffers, dense_sems, mine)
        gain_rows = (dn2 * y * root).astype(BF)
        column = jnp.where(lax.broadcasted_iota(jnp.int32, (128, 128), 1) == 32, 1.0, 0.0).astype(BF)
        narrow_left = jnp.concatenate([n2[...], gain_rows], axis=0)
        narrow_right = jnp.concatenate([dlogits, column], axis=0)
        for tile in range(4):
            part = contract(
                narrow_left[:, tile * 384 : (tile + 1) * 384], narrow_right, ((0,), (0,))
            ).astype(BF)
            for half in range(2):
                streams.put("o2", tile, half, part, 128)
        share_attn.wait_recv()
        share_dbr.wait_recv()
        for tile in range(4):
            for half in range(2):
                grads = contract(
                    attnc[:, tile * 384 : (tile + 1) * 384], dbrc[:, half * 384 : (half + 1) * 384],
                    ((0,), (0,)),
                ).astype(BF)
                streams.put("o1", tile, half, grads[:, 0:256])
                streams.put("o2", tile, half, grads[:, 256:384])
        streams.launch("o1", 0)
        streams.launch("o2", 0)

        cosine, sine = turn[0], turn[1]
        lane = lax.broadcasted_iota(jnp.int32, (1, 128), 1)
        freqs = jnp.exp((lane % 32).astype(F32) * (-math.log(10000.0) / 32))
        sign = jnp.where(lane % 64 < 32, -1.0, 1.0)

        def turn_back(u, cos, sin):
            return u * cos - swap_halves(u) * sin

        def attend(j, carry):
            lanes = pl.ds(pl.multiple_of(j * 128, 128), 128)
            turned = [jnp.zeros((128, 384), F32) for _ in range(2)]
            for block in range(2):
                part = slice(block * 4, (block + 1) * 4)
                keys = kv[0, part, :, lanes].reshape(512, 128)
                values = kv[1, part, :, lanes].reshape(512, 128)
                grad_keys = jnp.zeros((512, 128), F32)
                grad_values = jnp.zeros((512, 128), F32)
                seen = visible(place, block * 512, 512)
                for s in range(2):
                    queries = qp[j] * half_mask(s)
                    grads = dap[j] * half_mask(s)
                    scores = contract(keys, queries, ((1,), (1,)))
                    probs = jnp.exp(jnp.where(seen, scores, floor_score) - lse[j * 2 + s])
                    back = contract(values, grads, ((1,), (1,)))
                    grad_scores = (probs * (back - delta[j * 2 + s])).astype(BF)
                    grad_values = grad_values + contract(probs.astype(BF), grads, ((1,), (0,)))
                    grad_keys = grad_keys + contract(grad_scores, queries, ((1,), (0,)))
                    turned[s] = turned[s] + contract(keys, grad_scores, ((0,), (0,)))
                dkv[part, j, 1] = grad_values.astype(BF).reshape(4, 128, 128)
                for b in range(4):
                    shift = ((block * 4 + b - context) * 128).astype(F32) * freqs
                    cos, sin = jnp.cos(shift), sign * jnp.sin(shift)
                    raw = turn_back(
                        grad_keys[b * 128 : (b + 1) * 128],
                        cosine * cos - sine * sin, sine * cos + cosine * sin,
                    )
                    dkv[block * 4 + b, j, 0] = raw.astype(BF)
            joined = jnp.concatenate([turned[0][0:64], turned[1][64:128]], axis=0).T * 0.125
            blocks = from_pairs([joined[r * 128 : (r + 1) * 128] for r in range(3)])
            for r, part in enumerate(blocks):
                lanes = pl.ds(pl.multiple_of((j % 2) * 384 + r * 128, 128), 128)
                dq[j // 2, :, lanes] = turn_back(part, cosine, sine).astype(BF)
            return carry

        def attend_core(core):
            def step(i, carry):
                return attend(core * 2 + i, carry)

            lax.fori_loop(0, 2, step, 0)

        kv_sent = []

        def kv_push(src, dst, slot, device):
            copy = send(src, dst, (kv_sems.at[0, slot], kv_sems.at[1, slot]), device)
            kv_sent.append(copy)
            return copy

        def kv_add(out, count, terms):
            def body(i, carry):
                a, b, c = i // 4, i // 2 % 2, i % 2
                block = out(a)
                total = block[b, c].astype(F32)
                for term in terms:
                    total = total + term(a)[b, c].astype(F32)
                block[b, c] = total.astype(BF)
                return carry

            lax.fori_loop(0, count * 4, body, 0)

        other = 1 - place.core
        first, later = pl.ds(other * 2, 2), pl.ds(place.core * 2, 2)
        attend_core(other)
        share_dq = share(2, dq.at[other], dqc.at[lower])
        share_dkv = share(3, dkv.at[:, first], dkvs)
        lead = kv_push(dkv.at[pl.ds(other_lo * 4, 4), first], land_a, 0, lo_device)
        streams.step("o1", 0)
        streams.step("o2", 0)
        attend_core(place.core)
        dqc[0:128, :] = dq[place.core]
        share_dq.wait_recv()
        for load in load_columns:
            load.wait()
        own_lanes = pl.ds(pl.multiple_of(context * 128, 128), 128)
        their_lanes = pl.ds(pl.multiple_of(1024 + context * 128, 128), 128)
        for tile in range(4):
            rows = slice(tile * 384, (tile + 1) * 384)
            left = jnp.concatenate([big[rows, own_lanes], big[rows, their_lanes]], axis=1)
            for half in range(2):
                grads = contract(left, dqc[:, half * 384 : (half + 1) * 384], ((1,), (0,))).astype(BF)
                streams.put("q1", tile, half, grads[:, 0:256])
                streams.put("q2", tile, half, grads[:, 256:384])
        streams.launch("q1", 0)
        streams.launch("q2", 0)
        share_dkv.wait_recv()
        own_right = jnp.concatenate(
            [dkv[:, place.core * 2 + h, which].reshape(1024, 128) for h in range(2) for which in range(2)],
            axis=1,
        )
        their_right = jnp.concatenate(
            [dkvs[:, h, which].reshape(1024, 128) for h in range(2) for which in range(2)], axis=1
        )
        for tile in range(4):
            rows = slice(tile * 384, (tile + 1) * 384)
            grads = contract(big[rows, 0:1024], own_right, ((1,), (0,))) + contract(
                big[rows, 1024:2048], their_right, ((1,), (0,))
            )
            grads = grads.astype(BF)
            for half in range(2):
                streams.put("s1", tile, half, grads[:, half * 256 : half * 256 + 128])
                streams.put("s2", tile, half, grads[:, half * 256 + 128 : half * 256 + 256])
        streams.launch("s1", 0)
        streams.launch("s2", 0)
        load_q = pltpu.make_async_copy(wq, big.at[:, 0:1536], weight_sems.at[0])
        load_k = pltpu.make_async_copy(wk, big.at[:, 1536:2048], weight_sems.at[2])
        load_q.start()
        load_k.start()

        legs = []
        for d, (index, device) in enumerate(y_line):
            for lo in range(2):
                legs.append(
                    kv_push(dkv.at[lo * 4 + index, later], land_c.at[d, lo], 4 + d * 2 + lo, device)
                )
        lead.wait_recv()
        share_dkv.wait_send()
        pending.pop()
        kv_add(lambda a: dkv.at[place.lo * 4 + a, first], 4, [lambda a: land_a.at[a]])
        legs_b = [
            kv_push(dkv.at[place.lo * 4 + index, first], land_b.at[d], 1 + d, device)
            for d, (index, device) in enumerate(y_line)
        ]
        home.third()

        mats = (eg, eu, ed)
        second = []

        def fold_expert(m):
            mat = mats[m]
            arrived = [far_p.at[0, 0]] * 3 + [far_q.at[0]]
            for i, block in enumerate(arrived):
                sems = (far_sems.at[0, m * 4 + i], far_sems.at[1, m * 4 + i])
                copy = pltpu.make_async_remote_copy(
                    src_ref=block, dst_ref=block, send_sem=sems[0], recv_sem=sems[1],
                    device_id=sibling, device_id_type=MESH,
                )
                copy.wait()
            steps = []
            for lo in range(2):
                terms = [mat.at[0, lo, place.y]]
                for d in range(3):
                    terms.append(far_p.at[d, m, lo])
                steps.append((terms, sum_p.at[lo, m]))
            for y_at in range(4):
                steps.append(([mat.at[1, place.lo, y_at], far_q.at[m, y_at]], sum_q.at[y_at, m]))

            def fetch(step):
                loads = []
                for i, term in enumerate(steps[step][0]):
                    loads.append(
                        pltpu.make_async_copy(term, stage.at[step % 2, i], fold_sems.at[step % 2, i])
                    )
                    loads[-1].start()
                return loads

            ready = fetch(0)
            for step, (terms, out) in enumerate(steps):
                following = fetch(step + 1) if step + 1 < len(steps) else None
                for load in ready:
                    load.wait()

                def fold(i, carry):
                    part = pl.ds(pl.multiple_of(i * 48, 16), 48)
                    total = stage[step % 2, 0, part].astype(F32)
                    for term in range(1, len(terms)):
                        total = total + stage[step % 2, term, part].astype(F32)
                    out[part] = total.astype(BF)
                    return carry

                lax.fori_loop(0, 4, fold, 0)
                ready = following
            pair = (expert_sems.at[0, 4 + m * 4], expert_sems.at[1, 4 + m * 4])
            second.append(send(sum_p.at[other_lo, m], land_p2.at[m], pair, lo_device))
            for d, (index, device) in enumerate(y_line):
                pair = (expert_sems.at[0, 5 + m * 4 + d], expert_sems.at[1, 5 + m * 4 + d])
                second.append(send(sum_q.at[index, m], land_q2.at[d, m], pair, device))

        fold_expert(0)
        fold_expert(1)
        streams.step("o1", 1)
        streams.step("o2", 1)
        streams.step("q2", 0)
        streams.step("s1", 0)
        streams.step("s2", 0)
        streams.step("q1", 0)
        fold_expert(2)
        for copy in legs:
            copy.wait_recv()
        kv_add(
            lambda a: dkv.at[a * 4 + place.y, later], 2,
            [lambda a, d=d: land_c.at[d, a] for d in range(3)],
        )
        leg_d = kv_push(dkv.at[other_lo * 4 + place.y, later], land_d, 10, lo_device)
        streams.step("q2", 1)
        streams.step("s1", 1)
        streams.step("s2", 1)
        streams.step("q1", 1)
        for name in STREAMS:
            streams.land(name, 2)
        own_quarter = place.core * 2 + place.hi
        gathered = []
        for i, (a, b) in enumerate(((0, 1), (1, 0), (1, 1))):
            pair = (quarter_sems.at[0, i], quarter_sems.at[1, i])
            gathered.append(send(mine, quarters.at[own_quarter], pair, place.at(hi=a, core=b)))
        own_quarters = pltpu.make_async_copy(mine, quarters.at[own_quarter], weight_sems.at[5])
        own_quarters.start()

        for copy in legs_b:
            copy.wait_recv()

        def key_grads(core, terms):
            for i in range(2):
                for which in range(2):
                    total = dkv[context, core * 2 + i, which].astype(F32)
                    for term in terms:
                        total = total + term(i, which).astype(F32)
                    lanes = pl.ds(pl.multiple_of((which * 4 + core * 2 + i) * 128, 128), 128)
                    dk[:, lanes] = total.astype(BF)

        key_grads(other, [lambda i, w, d=d: land_b[d, i, w] for d in range(3)])
        leg_d.wait_recv()
        key_grads(place.core, [lambda i, w: land_d[i, w]])
        load_q.wait()
        load_k.wait()
        load_v.wait()
        load_x.wait()
        x = x_ref[...].astype(F32)
        root = inverse_root(x)
        queries = jnp.concatenate([dq[0], dq[1]], axis=1)
        for j in range(4):
            part = slice(j * 384, (j + 1) * 384)
            gt[:, part] = (
                contract(queries, big[part, 0:1536], ((1,), (1,)))
                + contract(dk[:, 0:512], big[part, 1536:2048], ((1,), (1,)))
                + contract(dk[:, 512:1024], w_v[part, :], ((1,), (1,)))
            )
        scaled = gt[...] * gain_attn[...].reshape(1, 1536)
        inner = jnp.mean(scaled * x, axis=-1, keepdims=True)
        gt[...] = dy1[...] + root * scaled - x * (root * root * root * inner)

        outs = [pltpu.make_async_copy(gt, gt_far, out_sems.at[0])]
        outs[0].start()
        home.finish(mixed, [y1])
        outs.append(pltpu.make_async_copy(mixed, mixed_far, out_sems.at[1]))
        outs[1].start()
        home.drain()
        for copy in gathered:
            copy.wait_recv()
        for m in range(3):
            for copy in second[m * 4 : m * 4 + 4]:
                copy.wait_recv()

            def finish(i, carry):
                part = pl.ds(pl.multiple_of(i * 48, 16), 48)
                experts[m, 0, part] = sum_p[place.lo, m, part].astype(F32) + land_p2[m, part].astype(F32)
                total = sum_q[place.y, m, part].astype(F32)
                for d in range(3):
                    total = total + land_q2[d, m, part].astype(F32)
                experts[m, 1, part] = total
                return carry

            lax.fori_loop(0, 4, finish, 0)
            outs.append(pltpu.make_async_copy(experts.at[m], experts_far.at[m], out_sems.at[2 + m]))
            outs[-1].start()
        for copy in pending + kv_sent + gathered + second + streams.sent:
            copy.wait_send()
        own_quarters.wait()
        for copy in outs:
            copy.wait()

    pl.run_scoped(
        early, low(16, 128, 1536), low(16, 128, 1536), high(16, 8, 128), high(16, 8, 128),
        low(8, 128, 1536), low(7, 128, 1536), low(1536, 128),
        low(2, 2, 4, 192, 512), low(2, 1536, 512), low(2, 512, 1536),
    )
    buffers = []
    for _, width, _ in STREAMS.values():
        buffers += [
            low(4, 4, 4, 48, width), low(3, 4, 4, 48, width), low(4, 4, 48, width),
            low(3, 4, 48, width), low(4, 48, width), low(3, 48, width),
        ]
    pl.run_scoped(
        late, low(128, 1536), low(128, 1536), low(1536, 2048), low(1536, 512),
        low(256, 1536), low(256, 768), low(256, 768), low(8, 2, 2, 128, 128),
        high(128, 128), low(2, 128, 768), low(4, 384, 128), high(8, 1, 384),
        low(2, 128, 768), low(128, 1024), high(128, 1536), low(8, 4, 2, 128, 128),
        low(4, 2, 2, 128, 128), low(3, 2, 2, 128, 128), low(3, 2, 2, 2, 128, 128), low(2, 2, 128, 128),
        low(48, ALL_WIDE), low(2, 4, 192, 512),
        low(2, 3, 192, 512), low(4, 3, 192, 512), low(3, 192, 512), low(3, 3, 192, 512),
        high(3, 2, 192, 512), low(128, 1536), high(128, 1536), *buffers,
    )


def run_layer(*operands):
    vmem = pl.BlockSpec(memory_space=pltpu.VMEM)
    hbm = pl.BlockSpec(memory_space=pl.ANY)
    sems = pltpu.SemaphoreType.DMA
    struct = jax.ShapeDtypeStruct
    return pl.pallas_call(
        layer_kernel,
        out_shape=(
            struct((128, 1536), BF), struct((128, 1536), F32), struct((4, 48, ALL_WIDE), BF),
            struct((3, 2, 192, 512), F32),
            *[struct((2, 2, 4, 192, 512), BF)] * 3,
            struct((3, 3, 2, 192, 512), BF), struct((3, 4, 192, 512), BF), struct((2, 8, 1536, 128), BF),
        ),
        in_specs=[hbm, vmem, hbm, vmem, vmem, vmem] + [hbm] * 7,
        out_specs=[hbm] * 10,
        scratch_shapes=[
            low(2, 8, 128, 512), low(4, 384, 128), high(8, 1, 384), low(128, 1536), high(128, 1536),
            low(128, 1536), high(128, 128), high(2, 128, 128), high(128, 1536), high(16, 8, 128),
            low(8, 128, 1536), low(2, 2, 64, 1536), low(5, 128, 1536),
            pltpu.SemaphoreType.REGULAR, sems((6,)), sems((3,)), sems, sems((2, 18)), sems((2, 8)),
            sems((2, 8)),
            sems((2, 16)), sems((2, 16)), sems((2, 9)), sems((2, 16)), sems((2,)), sems((2, 2)),
            sems((2, 16)), sems, sems((2, 12)),
            sems((16,)), sems((2, 4)), sems((2, 11)), sems((2, 9 * len(STREAMS))), sems((2, 3)),
            sems((2, 11)), sems((2, 4)), sems((2, 16)), sems((5,)),
        ],
        compiler_params=pltpu.CompilerParams(
            collective_id=0, has_side_effects=True, vmem_limit_bytes=63 << 20
        ),
    )(*operands)


def finish_kernel(
    mixed, gt, quarters, experts, gain, wq, wk, wv,
    mixed_out, gt_out, gq, gk, gv, go, ga, gm, gr, og, ou, od,
    rows_q, rows_kv, sems,
):
    place = Place()
    start = ((place.lo * 4 + place.y) * 4 + place.z) * 48
    rows = pl.ds(pl.multiple_of(start, 16), 48)
    loads = [
        pltpu.make_async_copy(wq.at[rows, :], rows_q, sems.at[0]),
        pltpu.make_async_copy(wk.at[rows, :], rows_kv.at[0], sems.at[1]),
        pltpu.make_async_copy(wv.at[rows, :], rows_kv.at[1], sems.at[2]),
    ]
    for load in loads:
        load.start()
    mixed_out[0] = mixed[...]
    gt_out[0] = gt[...]
    for q in range(4):
        go[:, q * 384 : (q + 1) * 384] = quarters[q, :, 0:384].astype(F32)
        gq[:, q * 384 : (q + 1) * 384] = quarters[q, :, 512:896].astype(F32)
        gk[:, q * 128 : (q + 1) * 128] = quarters[q, :, 896:1024].astype(F32)
        gv[:, q * 128 : (q + 1) * 128] = quarters[q, :, 1024:1152].astype(F32)
    narrow = quarters[0, :, 384:512].astype(F32) + quarters[2, :, 384:512].astype(F32)
    og[...] = experts[0]
    ou[...] = experts[1]
    od[...] = experts[2]
    for load in loads:
        load.wait()
    line = jnp.sum(gq[...] * rows_q[...].astype(F32), axis=1, keepdims=True)
    line = line + jnp.sum(gk[...] * rows_kv[0].astype(F32), axis=1, keepdims=True)
    line = line + jnp.sum(gv[...] * rows_kv[1].astype(F32), axis=1, keepdims=True)
    column = lax.broadcasted_iota(jnp.int32, (48, 1536), 1) - lax.broadcasted_iota(jnp.int32, (48, 1536), 0)
    own_gain = jnp.sum(jnp.where(column == start, gain[...].reshape(1, 1536), 0.0), axis=1, keepdims=True)
    both = jnp.where(
        lax.broadcasted_iota(jnp.int32, (48, 128), 1) == 33, line / own_gain, narrow
    )
    flat = jnp.concatenate([both, jnp.zeros((80, 128), F32)], axis=0).T
    gr[...] = flat[0:32, 0:48]
    gm[...] = flat[32:33, 0:48]
    ga[...] = flat[33:34, 0:48]


def run_finish(*operands):
    vmem = pl.BlockSpec(memory_space=pltpu.VMEM)
    hbm = pl.BlockSpec(memory_space=pl.ANY)
    f32 = lambda *shape: jax.ShapeDtypeStruct(shape, F32)
    return pl.pallas_call(
        finish_kernel,
        out_shape=(
            jax.ShapeDtypeStruct((1, 128, 1536), BF), f32(1, 128, 1536),
            f32(48, 1536), f32(48, 512), f32(48, 512), f32(48, 1536), f32(1, 48), f32(1, 48), f32(32, 48),
            f32(2, 192, 512), f32(2, 192, 512), f32(2, 192, 512),
        ),
        in_specs=[vmem] * 5 + [hbm] * 3,
        out_specs=[vmem] * 12,
        scratch_shapes=[low(48, 1536), low(2, 48, 512), pltpu.SemaphoreType.DMA((3,))],
        compiler_params=pltpu.CompilerParams(vmem_limit_bytes=63 << 20),
    )(*operands)


def shards(
    tokens, expert_ids, w_query, w_key, w_value, w_out, gain_attn, gain_moe, w_router,
    w_gate, w_up, w_down, cotangent,
):
    mixed, gt, quarters, experts, *_ = run_layer(
        tokens[0], expert_ids[0].T, cotangent[0], gain_attn, gain_moe, w_router.T,
        w_query, w_key, w_value, w_out, w_gate.reshape(2, 2, 4, 192, 512), w_up, w_down,
    )
    mixed, gt, gq, gk, gv, go, ga, gm, gr, og, ou, od = run_finish(
        mixed, gt, quarters, experts, gain_attn, w_query, w_key, w_value
    )
    return (mixed, gt, gq, gk, gv, go, ga.reshape(48), gm.reshape(48), gr.T, og, ou, od.transpose(0, 2, 1))


def solution(mesh):
    in_specs = (
        P(("expert", "dp"), "context", None),
        P(("expert", "dp"), "context", None),
        P(),
        P(),
        P(),
        P(),
        P(),
        P(),
        P(),
        P(("expert", "dp"), None, None),
        P(("expert", "dp"), None, None),
        P(("expert", "dp"), None, None),
        P(("expert", "dp"), "context", None),
    )
    out_specs = (
        P(("expert", "dp"), "context", None),
        P(("expert", "dp"), "context", None),
        P(("context", "dp"), None),
        P(("context", "dp"), None),
        P(("context", "dp"), None),
        P(("context", "dp"), None),
        P(("context", "dp")),
        P(("context", "dp")),
        P(("context", "dp"), None),
        P(("expert", "dp"), "context", None),
        P(("expert", "dp"), "context", None),
        P(("expert", "dp"), None, "context"),
    )
    return jax.shard_map(shards, mesh=mesh, in_specs=in_specs, out_specs=out_specs, check_vma=False)
```

```python
import math

import jax
import jax.numpy as jnp
from jax import lax
from jax.experimental import pallas as pl
from jax.experimental.pallas import tpu as pltpu
from jax.sharding import PartitionSpec as P

epsilon = 1e-06
floor_score = -1e30
MESH = pl.DeviceIdType.MESH
BF = jnp.bfloat16
F32 = jnp.float32


def low(*shape):
    return pltpu.VMEM(shape, BF)


def high(*shape):
    return pltpu.VMEM(shape, F32)


class Place:
    def __init__(self):
        e, c = lax.axis_index("expert"), lax.axis_index("context")
        self.hi, self.core = e // 2, e % 2
        self.lo, self.y = c // 4, c % 4
        self.z = lax.axis_index("dp")

    def at(self, hi=0, core=0, lo=0, y=0, z=0):
        e = (self.hi + hi) % 2 * 2 + (self.core + core) % 2
        c = (self.lo + lo) % 2 * 4 + (self.y + y) % 4
        return (e, c, (self.z + z) % 4)

    def line(self, axis):
        if axis == "y":
            return [((self.y + d) % 4, self.at(y=d)) for d in (1, 2, 3)]
        if axis == "z":
            return [((self.z + d) % 4, self.at(z=d)) for d in (1, 2, 3)]
        return [
            ((self.hi + a) % 2 * 2 + (self.lo + b) % 2, self.at(hi=a, lo=b))
            for a, b in ((0, 1), (1, 0), (1, 1))
        ]

    def own(self, axis):
        return {"y": self.y, "z": self.z, "x": self.hi * 2 + self.lo}[axis]


def greet(devices):
    barrier = pltpu.get_barrier_semaphore()
    for device in devices:
        pl.semaphore_signal(barrier, inc=1, device_id=device, device_id_type=MESH)
    pl.semaphore_wait(barrier, len(devices))


def send(src, dst, sems, device):
    copy = pltpu.make_async_remote_copy(
        src_ref=src, dst_ref=dst, send_sem=sems[0], recv_sem=sems[1],
        device_id=device, device_id_type=MESH,
    )
    copy.start()
    return copy


def scatter_start(place, axis, src, landing, sems, begin):
    copies = []
    for d, (index, device) in enumerate(place.line(axis)):
        pair = (sems.at[0, begin + d], sems.at[1, begin + d])
        copies.append(send(src.at[index], landing.at[d], pair, device))
    return copies


def add_up(out, own, landing, lead):
    count = landing.shape[0]

    def body(i, carry):
        total = own[i].astype(F32)
        for d in range(count):
            total = total + landing[d, i].astype(F32)
        out[i] = total.astype(out.dtype)
        return carry

    lax.fori_loop(0, lead, body, 0)


def roll_lanes(u, shift):
    return pltpu.roll(u, shift, 1)


def swap_halves(u):
    lane = lax.broadcasted_iota(jnp.int32, u.shape, 1)
    return jnp.where(lane % 64 < 32, roll_lanes(u, 96), roll_lanes(u, 32))


def to_pairs(blocks):
    a, b, c = blocks
    low = lax.broadcasted_iota(jnp.int32, a.shape, 1) < 64
    return [
        jnp.where(low, a, b), jnp.where(low, roll_lanes(a, 64), roll_lanes(c, 64)), jnp.where(low, b, c)
    ]


def from_pairs(blocks):
    a, b, c = blocks
    low = lax.broadcasted_iota(jnp.int32, a.shape, 1) < 64
    turned = roll_lanes(b, 64)
    return [jnp.where(low, a, turned), jnp.where(low, c, a), jnp.where(low, turned, c)]


def inverse_root(values):
    return lax.rsqrt(jnp.mean(values * values, axis=-1, keepdims=True) + epsilon)


def visible(place, start, rows):
    key = lax.broadcasted_iota(jnp.int32, (rows, 384), 0) + start
    query = lax.broadcasted_iota(jnp.int32, (rows, 384), 1) % 128
    return key <= query + (place.lo * 4 + place.y) * 128


def half_mask(s):
    lane = lax.broadcasted_iota(jnp.int32, (1, 128), 1)
    return jnp.where((lane >= 64) == (s == 1), 1.0, 0.0).astype(BF)


def group_peers(place):
    return {
        (c, h, d): place.at(core=c, hi=h, z=d)
        for c in (0, 1) for h in (0, 1) for d in range(4) if (c, h, d) != (0, 0, 0)
    }


def group_index(place, core=0, hi=0, z=0):
    return ((place.hi + hi) % 2 * 2 + (place.core + core) % 2) * 4 + (place.z + z) % 4


class Spread:
    def __init__(self, place, held, sems):
        self.place, self.held, self.sems = place, held, sems
        self.sent, self.waits = [], {}

    def push(self, origin, device, slot, rows=None):
        block = self.held.at[group_index(self.place, hi=origin[0], z=origin[1])]
        if rows is not None:
            block = block.at[pl.ds(rows, 64)]
        pair = (self.sems.at[0, len(self.sent)], self.sems.at[1, slot])
        copy = send(block, block, pair, device)
        self.sent.append(copy)
        self.waits[slot] = copy

    def land(self, slot):
        self.waits[slot].wait_recv()

    def around(self, h):
        self.push((h, 0), self.place.at(z=1), h * 4 + 3)
        self.push((h, 0), self.place.at(z=3), h * 4 + 1)

    def first(self):
        self.push((0, 0), self.place.at(hi=1), 4)
        self.around(0)
        self.push((0, 0), self.place.at(core=1), 8)

    def relay_hi(self):
        self.land(4)
        self.around(1)
        self.push((1, 0), self.place.at(core=1), 12)

    def relay(self, h):
        sibling = self.place.at(core=1)
        self.land(h * 4 + 3)
        self.push((h, 3), self.place.at(z=1), h * 4 + 2, 0)
        self.push((h, 3), sibling, 8 + h * 4 + 3)
        self.land(h * 4 + 1)
        self.push((h, 1), self.place.at(z=3), 16 + h, 64)
        self.push((h, 1), sibling, 8 + h * 4 + 1)

    def last(self, h):
        self.land(h * 4 + 2)
        self.land(16 + h)
        self.push((h, 2), self.place.at(core=1), 8 + h * 4 + 2)

    def finish(self, h):
        for d in range(4):
            self.land(8 + h * 4 + d)

    def drain(self):
        for copy in self.sent:
            copy.wait_send()


def add_rows(out, terms):
    def body(i, carry):
        part = pl.ds(pl.multiple_of(i * 16, 16), 16)
        total = terms[0][part].astype(F32)
        for term in terms[1:]:
            total = total + term[part].astype(F32)
        out[part] = total.astype(out.dtype)
        return carry

    lax.fori_loop(0, out.shape[0] // 16, body, 0)


class Gather:
    def __init__(self, place, parts, pool, halves, wholes, sems):
        self.place, self.parts, self.pool, self.sems = place, parts, pool, sems
        self.halves, self.wholes = halves, wholes
        self.sent, self.waits = [], {}

    def push(self, src, dst, slot, device):
        copy = send(src, dst, (self.sems.at[0, slot], self.sems.at[1, slot]), device)
        self.sent.append(copy)
        self.waits[slot] = copy
        return copy

    def swap(self, hi):
        half = (self.place.hi + hi) % 2
        start = group_index(self.place, core=1, hi=hi) - self.place.z
        return self.push(
            self.parts.at[pl.ds(start, 4)], self.pool.at[pl.ds(half * 4, 4)], hi, self.place.at(core=1)
        )

    def chunk(self, hi, z):
        return self.pool.at[(self.place.hi + hi) % 2 * 4 + (self.place.z + z) % 4]

    def terms(self, hi, z):
        if self.parts is None:
            return [self.chunk(hi, z)]
        return [self.chunk(hi, z), self.parts.at[group_index(self.place, hi=hi, z=z)]]

    def join(self, hi, z, more=()):
        block = self.chunk(hi, z)
        if self.parts is not None or more:
            add_rows(block, [*self.terms(hi, z), *more])
        return block

    def first(self, h):
        block = self.join(h, 2)
        upper, lower = pl.ds(0, 64), pl.ds(64, 64)
        self.push(block.at[upper], self.halves.at[h, 0], 2 + h * 4, self.place.at(z=1))
        self.push(block.at[lower], self.halves.at[h, 1], 3 + h * 4, self.place.at(z=3))
        self.join(h, 1)
        self.join(h, 3)

    def second(self, h):
        for side, d in ((0, 1), (1, 3)):
            part = pl.ds(side * 64, 64)
            self.waits[2 + h * 4 + side].wait_recv()
            block = self.chunk(h, d)
            add_rows(block.at[part], [block.at[part], self.halves.at[h, side]])
            self.push(block, self.wholes.at[h * 2 + side], 4 + h * 4 + side, self.place.at(z=d))

    def third(self):
        for side in range(2):
            self.waits[8 + side].wait_recv()
        block = self.join(1, 0, [self.wholes.at[2], self.wholes.at[3]])
        self.push(block, self.wholes.at[4], 10, self.place.at(hi=1))

    def finish(self, out, more=()):
        for slot in (4, 5, 10):
            self.waits[slot].wait_recv()
        add_rows(out, [*more, *self.terms(0, 0)] + [self.wholes.at[i] for i in (0, 1, 4)])

    def drain(self):
        for copy in self.sent:
            copy.wait_send()


class SpreadShort:
    def __init__(self, place, held, sems):
        self.place, self.held, self.sems = place, held, sems
        self.sent, self.waits = [], {}

    def pair(self, c, h, d):
        slot = c * 8 + h * 4 + d
        return (self.sems.at[0, slot], self.sems.at[1, slot])

    def push(self, origin, target, slot):
        c, h, d = target
        index = group_index(self.place, hi=origin[0], z=origin[1])
        block = self.held.at[index]
        copy = send(block, block, self.pair(*slot), self.place.at(core=c, hi=h, z=d))
        self.sent.append(copy)
        self.waits[slot] = copy

    def land(self, slot):
        self.waits[slot].wait_recv()

    def first(self):
        for d in (1, 3, 2):
            self.push((0, 0), (0, 0, d), (0, 0, (4 - d) % 4))
        self.push((0, 0), (0, 1, 0), (0, 1, 0))
        self.push((0, 0), (1, 0, 0), (1, 0, 0))

    def relay_a(self):
        self.land((0, 1, 0))
        for d in (1, 3):
            self.push((1, 0), (0, 0, d), (0, 1, (4 - d) % 4))
        self.push((1, 0), (1, 0, 0), (1, 1, 0))

    def relay_b(self):
        self.land((0, 0, 2))
        self.push((0, 2), (0, 1, 0), (0, 1, 2))
        self.push((0, 2), (1, 0, 0), (1, 0, 2))
        for d in (1, 3):
            self.land((0, 0, d))
            self.push((0, d), (1, 0, 0), (1, 0, d))

    def finish_near(self):
        for d in range(4):
            self.land((1, 0, d))

    def relay_far(self):
        for d in (1, 3, 2):
            self.land((0, 1, d))
            self.push((1, d), (1, 0, 0), (1, 1, d))

    def finish_far(self):
        for d in range(4):
            self.land((1, 1, d))

    def drain(self):
        for copy in self.sent:
            copy.wait_send()


class GatherShort:
    def __init__(self, place, parts, pool, landing, sems):
        self.place, self.parts, self.pool, self.landing, self.sems = place, parts, pool, landing, sems
        self.sent = []

    def pair(self, slot):
        return (self.sems.at[0, slot], self.sems.at[1, slot])

    def push(self, src, dst, slot, device):
        copy = send(src, dst, self.pair(slot), device)
        self.sent.append(copy)
        return copy

    def swap(self, hi):
        half = (self.place.hi + hi) % 2
        start = group_index(self.place, core=1, hi=hi) - self.place.z
        return self.push(
            self.parts.at[pl.ds(start, 4)], self.pool.at[pl.ds(half * 4, 4)], hi, self.place.at(core=1)
        )

    def chunk(self, hi, z):
        return self.pool.at[(self.place.hi + hi) % 2 * 4 + (self.place.z + z) % 4]

    def mine(self, hi, z):
        return self.parts.at[group_index(self.place, hi=hi, z=z)]

    def join(self, hi, z, more=()):
        block = self.chunk(hi, z)
        add_rows(block, [block, self.mine(hi, z), *more])
        return block

    def near(self):
        place, land = self.place, self.landing
        self.direct = []
        for i, d in enumerate((1, 3)):
            self.direct.append(self.push(self.join(0, d), land.at[3 + i], 5 + i, place.at(z=d)))

    def first(self):
        place, land = self.place, self.landing
        self.cross = []
        for i, d in enumerate((1, 3)):
            self.cross.append(self.push(self.join(1, d), land.at[i], 2 + i, place.at(z=d)))
        self.far = self.push(self.join(1, 2), land.at[2], 4, place.at(hi=1))

    def second(self):
        place, land = self.place, self.landing
        for copy in self.cross:
            copy.wait_recv()
        block = self.join(1, 0, [land.at[0], land.at[1]])
        self.last = [self.push(block, land.at[5], 7, place.at(hi=1))]
        self.far.wait_recv()
        block = self.join(0, 2, [land.at[2]])
        self.last.append(self.push(block, land.at[6], 8, place.at(z=2)))

    def finish(self, out):
        for copy in self.direct + self.last:
            copy.wait_recv()
        land = self.landing
        add_rows(out, [self.chunk(0, 0), self.mine(0, 0), land.at[3], land.at[4], land.at[5], land.at[6]])

    def drain(self):
        for copy in self.sent:
            copy.wait_send()


class Columns:
    def __init__(self, place, own, held, sems, own_sem):
        self.place, self.own, self.held, self.sems = place, own, held, sems
        self.sent, self.waits = [], {}
        self.local = pltpu.make_async_copy(own, held.at[0, self.context()], own_sem)
        self.local.start()

    def context(self, lo=0, y=0):
        return (self.place.lo + lo) % 2 * 4 + (self.place.y + y) % 4

    def push(self, src, side, lo, y, device, slot):
        pair = (self.sems.at[0, len(self.sent)], self.sems.at[1, slot])
        copy = send(src, self.held.at[side, self.context(lo, y)], pair, device)
        self.sent.append(copy)
        self.waits[slot] = copy

    def first(self):
        place = self.place
        self.push(self.own, 0, 0, 0, place.at(lo=1), 4)
        for d in (1, 3, 2):
            self.push(self.own, 0, 0, 0, place.at(y=d), (4 - d) % 4)
        self.push(self.own, 1, 0, 0, place.at(core=1), 8)

    def cross(self, lo, y):
        self.waits[lo * 4 + y].wait_recv()
        block = self.held.at[0, self.context(lo, y)]
        self.push(block, 1, lo, y, self.place.at(core=1), 8 + lo * 4 + y)
        return block

    def second(self):
        block = self.cross(1, 0)
        for d in (1, 3, 2):
            self.push(block, 0, 1, 0, self.place.at(y=d), 4 + (4 - d) % 4)
        for d in (1, 3, 2):
            self.cross(0, d)

    def third(self):
        for d in (1, 3, 2):
            self.cross(1, d)

    def finish(self):
        for slot in range(8):
            self.waits[8 + slot].wait_recv()
        self.local.wait()
        for copy in self.sent:
            copy.wait_send()


def contract(left, right, dims):
    return lax.dot_general(left, right, (dims, ((), ())), preferred_element_type=F32)


STREAMS = {
    "o1": ("yxz", 256, 0), "o2": ("zyx", 256, 256), "q1": ("zxy", 256, 512),
    "q2": ("zyx", 128, 768), "s1": ("xzy", 128, 896), "s2": ("zyx", 128, 1024),
}
ALL_WIDE = 1152


def stream_index(order, block, half):
    at = {"x": half * 2 + block // 16, "y": block // 4 % 4, "z": block % 4}
    return tuple(at[axis] for axis in order)


class Streams:
    def __init__(self, place, buffers, sems, mine):
        self.place, self.buffers, self.sems, self.mine = place, buffers, sems, mine
        self.flight, self.sent = {}, []

    def put(self, name, tile, half, grads, begin=0):
        order = STREAMS[name][0]
        width = grads.shape[1]
        for j in range(8):
            index = stream_index(order, tile * 8 + j, half)
            self.buffers[name][0][(*index, slice(None), slice(begin, begin + width))] = (
                grads[j * 48 : (j + 1) * 48]
            )

    def source(self, name, phase):
        return self.buffers[name][2 * phase]

    def launch(self, name, phase):
        begin = list(STREAMS).index(name) * 9 + 3 * phase
        copies = scatter_start(
            self.place, STREAMS[name][0][phase], self.source(name, phase),
            self.buffers[name][2 * phase + 1], self.sems, begin,
        )
        self.flight[name] = copies
        self.sent.extend(copies)

    def land(self, name, phase):
        for copy in self.flight[name]:
            copy.wait_recv()
        order, width, begin = STREAMS[name]
        own = self.source(name, phase).at[self.place.own(order[phase])]
        landing = self.buffers[name][2 * phase + 1]
        if phase == 2:
            total = own[...].astype(F32)
            for d in range(3):
                total = total + landing[d].astype(F32)
            self.mine[:, begin : begin + width] = total.astype(BF)
            return
        out = self.source(name, phase + 1)
        if phase == 1:
            add_up(out, own, landing, 4)
            return

        def body(i, carry):
            a, b = i // 4, i % 4
            total = own[a, b].astype(F32)
            for d in range(3):
                total = total + landing[d, a, b].astype(F32)
            out[a, b] = total.astype(BF)
            return carry

        lax.fori_loop(0, 16, body, 0)

    def step(self, name, phase):
        self.land(name, phase)
        if phase < 2:
            self.launch(name, phase + 1)


def layer_kernel(
    x_far, ids, cot_far, gain_attn, gain_moe, wr, wq, wk, wv, wo, wg_far, wu_far, wd_far,
    mixed_far, gt_far, quarters, experts_far, eg, eu, ed, far_p, far_q, n1t_all,
    kv, qp, lse, attn, y1, n2, gates, turn, dn2r, dgate, eo_pool, home_halves, home_wholes,
    ready, weight_sems, expert_load_sems, own_sem, cots_sems, k_sems, v_sems,
    table_sems, rows_sems, gather_sems, dgate_sems, stage_sems, eo_sems, column_sems, column_sem, far_sems,
    column_load_sems, pair_sems, kv_sems, dense_sems, quarter_sems, home_sems, fold_sems, expert_sems,
    out_sems,
):
    def early(cots, rows, tables, table, pool, landing, n1t, wg, wu, wd):
        expert_loads = [
            pltpu.make_async_copy(far, near, expert_load_sems.at[i])
            for i, (far, near) in enumerate(((wg_far, wg), (wu_far, wu), (wd_far, wd)))
        ]

        def forward(n1, x_ref, wqv, wkv, wov):
            place = Place()
            me = group_index(place)
            context = place.lo * 4 + place.y
            own_copy = pltpu.make_async_copy(cot_far, cots.at[me], own_sem)
            own_copy.start()
            loads = [
                pltpu.make_async_copy(x_far, x_ref, weight_sems.at[4]),
                pltpu.make_async_copy(wk, wkv.at[:, 0:512], weight_sems.at[0]),
                pltpu.make_async_copy(wv, wkv.at[:, 512:1024], weight_sems.at[1]),
                pltpu.make_async_copy(wq, wqv, weight_sems.at[2]),
                pltpu.make_async_copy(wo, wov, weight_sems.at[3]),
            ]
            for load in loads:
                load.start()
            for load in expert_loads:
                load.start()
            greet(
                list(group_peers(place).values())
                + [place.at(y=d) for d in (1, 2, 3)] + [place.at(lo=1), place.at(hi=1, lo=1)]
            )
            lo_peer = place.at(lo=1)
            spread = Spread(place, cots, cots_sems)
            own_copy.wait()
            spread.first()
            loads.pop(0).wait()
            x = x_ref[...].astype(F32)
            n1[...] = (x * inverse_root(x) * gain_attn[...].reshape(1, 1536)).astype(BF)
            lane = lax.broadcasted_iota(jnp.int32, (128, 128), 1)
            row = lax.broadcasted_iota(jnp.int32, (128, 128), 0)
            freqs = jnp.exp((lane % 32).astype(F32) * (-math.log(10000.0) / 32))
            angles = (row + context * 128).astype(F32) * freqs
            cosine = jnp.cos(angles)
            sine = jnp.where(lane % 64 < 32, -1.0, 1.0) * jnp.sin(angles)
            turn[0] = cosine
            turn[1] = sine

            loads[0].wait()
            loads[1].wait()
            for j in range(4):
                raw = contract(n1[...], wkv[:, j * 128 : (j + 1) * 128], ((1,), (0,)))
                kv[0, context, :, j * 128 : (j + 1) * 128] = (raw * cosine + swap_halves(raw) * sine).astype(BF)
            kv[1, context] = contract(n1[...], wkv[:, 512:1024], ((1,), (0,))).astype(BF)

            sent = []
            waits = {}

            def push(which, lo, y, device, slot):
                block = kv.at[which, (place.lo + lo) % 2 * 4 + (place.y + y) % 4]
                sems = (k_sems, v_sems)[which]
                copy = send(block, block, (sems.at[0, slot], sems.at[1, slot]), device)
                sent.append(copy)
                waits[which, slot] = copy

            for which in (0, 1):
                push(which, 0, 0, lo_peer, 4)
                for d in (1, 3, 2):
                    push(which, 0, 0, place.at(y=d), (4 - d) % 4)

            loads[2].wait()
            for j in range(4):
                raw = contract(n1[...], wqv[:, j * 384 : (j + 1) * 384], ((1,), (0,)))
                turned = []
                for r in range(3):
                    block = raw[:, r * 128 : (r + 1) * 128]
                    turned.append((block * cosine + swap_halves(block) * sine) * 0.125)
                for r, block in enumerate(to_pairs(turned)):
                    qp[j, r * 128 : (r + 1) * 128, :] = block.astype(BF)
            waits[0, 4].wait_recv()
            for d in (1, 3, 2):
                push(0, 1, 0, place.at(y=d), 4 + (4 - d) % 4)
            spread.relay_hi()
            for d in (1, 3, 2):
                waits[1, d].wait_recv()
                push(1, 0, d, lo_peer, 4 + d)

            spread.relay(0)
            for j in range(12):
                part = slice(j * 128, (j + 1) * 128)
                n1t[part, :] = n1[:, part].astype(F32).T.astype(BF)

            picked = jnp.zeros((128, 128), F32)
            for k in range(8):
                picked = picked + jnp.where(ids[k : k + 1, :] == row, 1.0, 0.0)
            chosen = picked.T
            earlier = jnp.where(lane < row, 1.0, 0.0).astype(BF)
            before = contract(earlier, chosen.astype(BF), ((1,), (0,)))
            slots = jnp.where(chosen > 0.0, before, -1.0).T
            table[...] = jnp.zeros_like(table)
            for g in range(16):
                table[g, 0:2, :] = slots[2 * g : 2 * g + 2, :]

            for d in (1, 3, 2):
                waits[0, d].wait_recv()
                waits[0, 4 + d].wait_recv()
                waits[1, 4 + d].wait_recv()
            waits[1, 4].wait_recv()
            spread.relay(1)

            def attend(j, carry):
                lanes = pl.ds(pl.multiple_of(j * 128, 128), 128)
                keys = kv[0, :, :, lanes].reshape(1024, 128)
                values = kv[1, :, :, lanes].reshape(1024, 128)
                halves = []
                for s in range(2):
                    scores = contract(keys, qp[j] * half_mask(s), ((1,), (1,)))
                    scores = jnp.where(visible(place, 0, 1024), scores, floor_score)
                    top = jnp.max(scores, axis=0, keepdims=True)
                    probs = jnp.exp(scores - top)
                    total = jnp.sum(probs, axis=0, keepdims=True)
                    lse[j * 2 + s] = top + jnp.log(total)
                    out = contract(values, probs.astype(BF), ((0,), (0,))) * (1.0 / total)
                    halves.append(out[s * 64 : (s + 1) * 64])
                joined = jnp.concatenate(halves, axis=0).T
                for r, block in enumerate(from_pairs([joined[r * 128 : (r + 1) * 128] for r in range(3)])):
                    attn[:, pl.ds(pl.multiple_of(j * 384 + r * 128, 128), 128)] = block.astype(BF)
                return carry

            lax.fori_loop(0, 4, attend, 0)
            spread.last(0)

            loads[3].wait()
            for j in range(4):
                part = slice(j * 384, (j + 1) * 384)
                y1[:, part] = x_ref[:, part].astype(F32) + contract(attn[...], wov[:, part], ((1,), (0,)))
            y = y1[...]
            n2[...] = (y * inverse_root(y) * gain_moe[...].reshape(1, 1536)).astype(BF)
            logits = jnp.concatenate(
                [contract(n2[...], wr[...], ((1,), (1,))), jnp.zeros((128, 96), F32)], axis=1
            )
            logits = jnp.where(chosen > 0.0, logits, -jnp.inf)
            weights = jnp.exp(logits - jnp.max(logits, axis=1, keepdims=True))
            weights = weights / jnp.sum(weights, axis=1, keepdims=True)
            gates[...] = weights
            turned = weights.T
            for g in range(16):
                table[g, 2:4, :] = turned[2 * g : 2 * g + 2, :]
            spread.last(1)
            spread.finish(0)
            spread.finish(1)
            spread.drain()
            for copy in sent:
                copy.wait_send()

        def experts(
            x_rows, c_rows, pick, gate, dg, dhg, dhu, gact, drow, back, dgate_out,
        ):
            place = Place()
            peers = group_peers(place)
            me = group_index(place)
            y_line, lo_device = place.line("y"), place.at(lo=1)

            small = []
            tables[me] = table[me]
            for (c, h, d), device in peers.items():
                slot = c * 8 + h * 4 + d
                pair = (table_sems.at[0, slot], table_sems.at[1, c * 8 + h * 4 + (4 - d) % 4])
                small.append(send(table.at[group_index(place, c, h, d)], tables.at[me], pair, device))
            rows[me] = n2[...]
            spread_rows = SpreadShort(place, rows, rows_sems)
            spread_rows.first()
            columns = Columns(place, n1t, n1t_all, column_sems, column_sem)
            columns.first()
            for copy in small:
                copy.wait_recv()

            slots = lax.broadcasted_iota(jnp.int32, (80, 256), 0).astype(F32)
            second = lax.broadcasted_iota(jnp.int32, (1, 256), 1) >= 128

            def select(pair_index):
                parts = []
                for e in range(2):
                    here = jnp.concatenate(
                        [tables[pair_index * 2, e : e + 1, :], tables[pair_index * 2 + 1, e : e + 1, :]], axis=1
                    )
                    here = jnp.where(here < 0.0, -1000.0, here + jnp.where(second, 40.0, 0.0))
                    weight = jnp.concatenate(
                        [tables[pair_index * 2, 2 + e : 3 + e, :], tables[pair_index * 2 + 1, 2 + e : 3 + e, :]],
                        axis=1,
                    )
                    hit = slots == here
                    parts.append(jnp.where(hit, 1.0, 0.0).astype(BF))
                    place_rows = pl.ds(pl.multiple_of(pair_index * 80, 80), 80)
                    gate[e, place_rows, :] = jnp.sum(jnp.where(hit, weight, 0.0), axis=1, keepdims=True)
                pick[pair_index] = jnp.concatenate(parts, axis=0)

            def pull(pair_index, held, out):
                both = jnp.concatenate([held[pair_index * 2], held[pair_index * 2 + 1]], axis=0)
                picked = contract(pick[pair_index], both, ((1,), (0,))).astype(BF)
                place_rows = pl.ds(pl.multiple_of(pair_index * 80, 80), 80)
                out[0, place_rows, :] = picked[0:80]
                out[1, place_rows, :] = picked[80:160]

            def all_pairs(body):
                def step(i, carry):
                    body(i)
                    return carry
                lax.fori_loop(0, 8, step, 0)

            def side_pairs(c, h, body):
                base = (group_index(place, core=c, hi=h) - place.z) // 2

                def step(i, carry):
                    body(base + i)
                    return carry

                lax.fori_loop(0, 2, step, 0)

            all_pairs(select)
            all_pairs(lambda p: pull(p, cots, c_rows))
            expert_loads[2].wait()

            def back_rows(i, carry):
                e, m = i // 2, i % 2
                part = pl.ds(pl.multiple_of(m * 320, 320), 320)
                back[e, part, :] = contract(c_rows[e, part, :], wd[e], ((1,), (1,)))
                return carry

            lax.fori_loop(0, 4, back_rows, 0)

            def work(h):
                m = (place.hi + h) % 2
                part = pl.ds(pl.multiple_of(m * 320, 320), 320)

                def step(e, carry):
                    x = x_rows[e, part, :]
                    hg = contract(x, wg[e].reshape(1536, 512), ((1,), (0,)))
                    hu = contract(x, wu[e], ((1,), (0,)))
                    turned = back[e, part, :]
                    weight = gate[e, part, :]
                    sig = 1.0 / (1.0 + jnp.exp(-hg))
                    silu = hg * sig
                    act = silu * hu
                    dg[e, part, :] = jnp.sum(act * turned, axis=1, keepdims=True)
                    gact[e, part, :] = (weight * act).astype(BF)
                    dact = weight * turned
                    low_hg = (dact * hu * (sig + silu * (1.0 - sig))).astype(BF)
                    low_hu = (dact * silu).astype(BF)
                    dhg[e, part, :] = low_hg
                    dhu[e, part, :] = low_hu
                    made = (
                        contract(low_hg, wg[e].reshape(1536, 512), ((1,), (1,))) + contract(low_hu, wu[e], ((1,), (1,)))
                    ).astype(BF)
                    for j in range(4):
                        drow[m * 4 + j, pl.ds(pl.multiple_of(e * 80, 80), 80), :] = made[j * 80 : (j + 1) * 80]
                    return carry

                lax.fori_loop(0, 2, step, 0)

            def put_back(pair_index, out):
                both = contract(pick[pair_index], drow[pair_index], ((0,), (0,))).astype(BF)
                out[pair_index * 2] = both[0:128]
                out[pair_index * 2 + 1] = both[128:256]

            def gate_grads(pair_index):
                chosen = pick[pair_index].astype(F32)
                for e in range(2):
                    column = dg[e, pl.ds(pl.multiple_of(pair_index * 80, 80), 80), :]
                    line = jnp.sum(chosen[e * 80 : (e + 1) * 80] * column, axis=0, keepdims=True)
                    dgate_out[pair_index * 2, e : e + 1, :] = line[:, 0:128]
                    dgate_out[pair_index * 2 + 1, e : e + 1, :] = line[:, 128:256]

            home = GatherShort(place, cots, pool, landing, gather_sems)
            spread_rows.relay_a()
            spread_rows.relay_b()
            spread_rows.finish_near()
            side_pairs(0, 0, lambda p: pull(p, rows, x_rows))
            side_pairs(1, 0, lambda p: pull(p, rows, x_rows))
            expert_loads[0].wait()
            expert_loads[1].wait()
            work(0)
            side_pairs(1, 0, lambda p: put_back(p, cots))
            near_swap = home.swap(0)
            spread_rows.relay_far()
            side_pairs(0, 0, lambda p: put_back(p, cots))
            columns.second()
            spread_rows.finish_far()
            side_pairs(0, 1, lambda p: pull(p, rows, x_rows))
            side_pairs(1, 1, lambda p: pull(p, rows, x_rows))
            near_swap.wait_recv()
            home.near()
            work(1)
            side_pairs(1, 1, lambda p: put_back(p, cots))
            far_swap = home.swap(1)
            side_pairs(0, 1, lambda p: put_back(p, cots))
            dgate_out[...] = jnp.zeros_like(dgate_out)
            all_pairs(gate_grads)
            small_back = []
            dgate[me] = dgate_out[me]
            for (c, h, d), device in peers.items():
                slot = c * 8 + h * 4 + d
                pair = (dgate_sems.at[0, slot], dgate_sems.at[1, c * 8 + h * 4 + (4 - d) % 4])
                small_back.append(send(dgate_out.at[group_index(place, c, h, d)], dgate.at[me], pair, device))
            far_swap.wait_recv()
            home.first()
            spread_rows.drain()
            columns.third()

            copies, far = {}, []
            other_lo = (place.lo + 1) % 2
            order = [
                (e, left, right, out, m)
                for left, right, out, m in ((x_rows, dhg, eg, 0), (x_rows, dhu, eu, 1), (c_rows, gact, ed, 2))
                for e in range(2)
            ]

            def forward(step):
                copies[step].wait()
                e, _, _, out, m = order[step]
                if e == 0:
                    for d, (index, device) in enumerate(y_line):
                        pair = (far_sems.at[0, m * 4 + d], far_sems.at[1, m * 4 + d])
                        far.append(send(out.at[0, :, index], far_p.at[d, m], pair, device))
                else:
                    pair = (far_sems.at[0, m * 4 + 3], far_sems.at[1, m * 4 + 3])
                    far.append(send(out.at[1, other_lo], far_q.at[m], pair, lo_device))

            for step, (e, left, right, out, m) in enumerate(order):
                slot = step % 2
                if step >= 2:
                    forward(step - 2)

                def weight_grad(i, carry):
                    tile = pl.ds(pl.multiple_of(i * 384, 128), 384)
                    grads = contract(left[e, :, tile], right[e], ((0,), (0,))).astype(BF)
                    wg[slot, i // 2, pl.ds(i % 2 * 2, 2)] = grads.reshape(2, 192, 512)
                    return carry

                lax.fori_loop(0, 4, weight_grad, 0)
                copies[step] = pltpu.make_async_copy(wg.at[slot], out.at[e], stage_sems.at[slot])
                copies[step].start()
                if step == 2:
                    home.second()
            forward(4)
            forward(5)

            def outputs(i, carry):
                e, m = i // 2, i % 2
                part = pl.ds(pl.multiple_of(m * 320, 320), 320)
                made = contract(gact[e, part, :], wd[e], ((1,), (0,))).astype(BF)
                for j in range(4):
                    drow[m * 4 + j, pl.ds(pl.multiple_of(e * 80, 80), 80), :] = made[j * 80 : (j + 1) * 80]
                return carry

            lax.fori_loop(0, 4, outputs, 0)
            all_pairs(lambda p: put_back(p, rows))
            outward = Gather(place, rows, eo_pool, None, None, eo_sems)
            out_swaps = [outward.swap(0), outward.swap(1)]
            for copy in out_swaps:
                copy.wait_recv()
            for h in range(2):
                for d in range(4):
                    outward.join(h, d)
            home.finish(dn2r)
            for copy in small_back:
                copy.wait_recv()
            for copy in small + small_back:
                copy.wait_send()
            home.drain()
            outward.drain()
            columns.finish()

        pl.run_scoped(
            forward, low(128, 1536), low(128, 1536), low(1536, 1536), low(1536, 1024), low(1536, 1536)
        )
        pl.run_scoped(
            experts, low(2, 640, 1536), low(2, 640, 1536), low(8, 160, 256),
            high(2, 640, 1), high(2, 640, 1), low(2, 640, 512), low(2, 640, 512), low(2, 640, 512),
            low(8, 160, 1536), high(2, 640, 512), high(16, 8, 128),
        )

    def late(
        x_ref, cot, big, w_v, attnc, dqc, dbrc, dkvs, dgt, dbr, dap, delta, dq, dk, dy1, dkv,
        land_a, land_b, land_c, land_d, mine, stage, sum_p, sum_q, land_p2, land_q2, experts, mixed, gt, *rest,
    ):
        buffers = {name: rest[i * 6 : i * 6 + 6] for i, name in enumerate(STREAMS)}
        place = Place()
        context = place.lo * 4 + place.y
        y_line, z_line, x_line = (place.line(axis) for axis in "yzx")
        sibling, cross, lo_device = place.at(core=1), place.at(hi=1, core=1), place.at(lo=1)
        other_lo = (place.lo + 1) % 2
        load_o = pltpu.make_async_copy(wo, big.at[:, 0:1536], weight_sems.at[0])
        load_o.start()
        load_v = pltpu.make_async_copy(wv, w_v, weight_sems.at[1])
        load_v.start()
        load_x = pltpu.make_async_copy(x_far, x_ref, weight_sems.at[3])
        load_x.start()
        load_cot = pltpu.make_async_copy(cot_far, cot, weight_sems.at[4])
        load_cot.start()
        others = [device for line in (y_line, z_line, x_line) for _, device in line] + [sibling, cross]
        for device in others:
            pl.semaphore_signal(ready, inc=1, device_id=device, device_id_type=MESH)
        pl.semaphore_wait(ready, len(others))
        pending = []

        def share(i, source, both):
            pair = (pair_sems.at[0, i], pair_sems.at[1, i])
            copy = send(source, both, pair, sibling)
            pending.append(copy)
            return copy

        lower = pl.ds(128, 128)
        share_attn = share(0, attn, attnc.at[lower])
        attnc[0:128, :] = attn[...]

        home = Gather(place, None, eo_pool, home_halves, home_wholes, home_sems)
        home.first(1)
        home.first(0)

        dgt[...] = jnp.zeros_like(dgt)
        for g in range(16):
            dgt[2 * g : 2 * g + 2, :] = dgate[g, 0:2, :]
        weights = gates[...]
        dgates = dgt[...].T
        dlogits = weights * (dgates - jnp.sum(weights * dgates, axis=1, keepdims=True))
        dlogits = dlogits.astype(BF)
        dn2 = dn2r[...] + contract(dlogits[:, 0:32], wr[...], ((1,), (0,)))
        y = y1[...]
        root = inverse_root(y)
        scaled = dn2 * gain_moe[...].reshape(1, 1536)
        inner = jnp.mean(scaled * y, axis=-1, keepdims=True)
        load_cot.wait()
        dy = cot[...].astype(F32) + root * scaled - y * (root * root * root * inner)
        dy1[...] = dy
        low = dy.astype(BF)
        dbr[0] = low[:, 0:768]
        dbr[1] = low[:, 768:1536]
        share_dbr = share(1, dbr.at[1 - place.core], dbrc.at[lower])
        dbrc[0:128, :] = dbr[place.core]

        load_o.wait()
        for j in range(4):
            back = contract(low, big[j * 384 : (j + 1) * 384, 0:1536], ((1,), (1,)))
            grads = to_pairs([back[:, r * 128 : (r + 1) * 128] for r in range(3)])
            outs = to_pairs(
                [attn[:, j * 384 + r * 128 : j * 384 + (r + 1) * 128].astype(F32) for r in range(3)]
            )
            grads = jnp.concatenate(grads, axis=0).astype(BF)
            dap[j] = grads
            product = (grads.astype(F32) * jnp.concatenate(outs, axis=0)).T
            for s in range(2):
                delta[j * 2 + s] = jnp.sum(product[s * 64 : (s + 1) * 64], axis=0, keepdims=True)
        load_columns = []
        for side in range(2):
            for c in range(8):
                at = side * 8 + c
                load_columns.append(
                    pltpu.make_async_copy(
                        n1t_all.at[side, c], big.at[:, at * 128 : (at + 1) * 128], column_load_sems.at[at]
                    )
                )
                load_columns[-1].start()

        home.second(1)
        home.second(0)
        streams = Streams(place, buffers, dense_sems, mine)
        gain_rows = (dn2 * y * root).astype(BF)
        column = jnp.where(lax.broadcasted_iota(jnp.int32, (128, 128), 1) == 32, 1.0, 0.0).astype(BF)
        narrow_left = jnp.concatenate([n2[...], gain_rows], axis=0)
        narrow_right = jnp.concatenate([dlogits, column], axis=0)
        for tile in range(4):
            part = contract(
                narrow_left[:, tile * 384 : (tile + 1) * 384], narrow_right, ((0,), (0,))
            ).astype(BF)
            for half in range(2):
                streams.put("o2", tile, half, part, 128)
        share_attn.wait_recv()
        share_dbr.wait_recv()
        for tile in range(4):
            for half in range(2):
                grads = contract(
                    attnc[:, tile * 384 : (tile + 1) * 384], dbrc[:, half * 384 : (half + 1) * 384],
                    ((0,), (0,)),
                ).astype(BF)
                streams.put("o1", tile, half, grads[:, 0:256])
                streams.put("o2", tile, half, grads[:, 256:384])
        streams.launch("o1", 0)
        streams.launch("o2", 0)

        cosine, sine = turn[0], turn[1]
        lane = lax.broadcasted_iota(jnp.int32, (1, 128), 1)
        freqs = jnp.exp((lane % 32).astype(F32) * (-math.log(10000.0) / 32))
        sign = jnp.where(lane % 64 < 32, -1.0, 1.0)

        def turn_back(u, cos, sin):
            return u * cos - swap_halves(u) * sin

        def attend(j, carry):
            lanes = pl.ds(pl.multiple_of(j * 128, 128), 128)
            turned = [jnp.zeros((128, 384), F32) for _ in range(2)]
            for block in range(2):
                part = slice(block * 4, (block + 1) * 4)
                keys = kv[0, part, :, lanes].reshape(512, 128)
                values = kv[1, part, :, lanes].reshape(512, 128)
                grad_keys = jnp.zeros((512, 128), F32)
                grad_values = jnp.zeros((512, 128), F32)
                seen = visible(place, block * 512, 512)
                for s in range(2):
                    queries = qp[j] * half_mask(s)
                    grads = dap[j] * half_mask(s)
                    scores = contract(keys, queries, ((1,), (1,)))
                    probs = jnp.exp(jnp.where(seen, scores, floor_score) - lse[j * 2 + s])
                    back = contract(values, grads, ((1,), (1,)))
                    grad_scores = (probs * (back - delta[j * 2 + s])).astype(BF)
                    grad_values = grad_values + contract(probs.astype(BF), grads, ((1,), (0,)))
                    grad_keys = grad_keys + contract(grad_scores, queries, ((1,), (0,)))
                    turned[s] = turned[s] + contract(keys, grad_scores, ((0,), (0,)))
                dkv[part, j, 1] = grad_values.astype(BF).reshape(4, 128, 128)
                for b in range(4):
                    shift = ((block * 4 + b - context) * 128).astype(F32) * freqs
                    cos, sin = jnp.cos(shift), sign * jnp.sin(shift)
                    raw = turn_back(
                        grad_keys[b * 128 : (b + 1) * 128],
                        cosine * cos - sine * sin, sine * cos + cosine * sin,
                    )
                    dkv[block * 4 + b, j, 0] = raw.astype(BF)
            joined = jnp.concatenate([turned[0][0:64], turned[1][64:128]], axis=0).T * 0.125
            blocks = from_pairs([joined[r * 128 : (r + 1) * 128] for r in range(3)])
            for r, part in enumerate(blocks):
                lanes = pl.ds(pl.multiple_of((j % 2) * 384 + r * 128, 128), 128)
                dq[j // 2, :, lanes] = turn_back(part, cosine, sine).astype(BF)
            return carry

        def attend_core(core):
            def step(i, carry):
                return attend(core * 2 + i, carry)

            lax.fori_loop(0, 2, step, 0)

        kv_sent = []

        def kv_push(src, dst, slot, device):
            copy = send(src, dst, (kv_sems.at[0, slot], kv_sems.at[1, slot]), device)
            kv_sent.append(copy)
            return copy

        def kv_add(out, count, terms):
            def body(i, carry):
                a, b, c = i // 4, i // 2 % 2, i % 2
                block = out(a)
                total = block[b, c].astype(F32)
                for term in terms:
                    total = total + term(a)[b, c].astype(F32)
                block[b, c] = total.astype(BF)
                return carry

            lax.fori_loop(0, count * 4, body, 0)

        other = 1 - place.core
        first, later = pl.ds(other * 2, 2), pl.ds(place.core * 2, 2)
        attend_core(other)
        share_dq = share(2, dq.at[other], dqc.at[lower])
        share_dkv = share(3, dkv.at[:, first], dkvs)
        lead = kv_push(dkv.at[pl.ds(other_lo * 4, 4), first], land_a, 0, lo_device)
        streams.step("o1", 0)
        streams.step("o2", 0)
        attend_core(place.core)
        dqc[0:128, :] = dq[place.core]
        share_dq.wait_recv()
        for load in load_columns:
            load.wait()
        own_lanes = pl.ds(pl.multiple_of(context * 128, 128), 128)
        their_lanes = pl.ds(pl.multiple_of(1024 + context * 128, 128), 128)
        for tile in range(4):
            rows = slice(tile * 384, (tile + 1) * 384)
            left = jnp.concatenate([big[rows, own_lanes], big[rows, their_lanes]], axis=1)
            for half in range(2):
                grads = contract(left, dqc[:, half * 384 : (half + 1) * 384], ((1,), (0,))).astype(BF)
                streams.put("q1", tile, half, grads[:, 0:256])
                streams.put("q2", tile, half, grads[:, 256:384])
        streams.launch("q1", 0)
        streams.launch("q2", 0)
        share_dkv.wait_recv()
        own_right = jnp.concatenate(
            [dkv[:, place.core * 2 + h, which].reshape(1024, 128) for h in range(2) for which in range(2)],
            axis=1,
        )
        their_right = jnp.concatenate(
            [dkvs[:, h, which].reshape(1024, 128) for h in range(2) for which in range(2)], axis=1
        )
        for tile in range(4):
            rows = slice(tile * 384, (tile + 1) * 384)
            grads = contract(big[rows, 0:1024], own_right, ((1,), (0,))) + contract(
                big[rows, 1024:2048], their_right, ((1,), (0,))
            )
            grads = grads.astype(BF)
            for half in range(2):
                streams.put("s1", tile, half, grads[:, half * 256 : half * 256 + 128])
                streams.put("s2", tile, half, grads[:, half * 256 + 128 : half * 256 + 256])
        streams.launch("s1", 0)
        streams.launch("s2", 0)
        load_q = pltpu.make_async_copy(wq, big.at[:, 0:1536], weight_sems.at[0])
        load_k = pltpu.make_async_copy(wk, big.at[:, 1536:2048], weight_sems.at[2])
        load_q.start()
        load_k.start()

        legs = []
        for d, (index, device) in enumerate(y_line):
            for lo in range(2):
                legs.append(
                    kv_push(dkv.at[lo * 4 + index, later], land_c.at[d, lo], 4 + d * 2 + lo, device)
                )
        lead.wait_recv()
        share_dkv.wait_send()
        pending.pop()
        kv_add(lambda a: dkv.at[place.lo * 4 + a, first], 4, [lambda a: land_a.at[a]])
        legs_b = [
            kv_push(dkv.at[place.lo * 4 + index, first], land_b.at[d], 1 + d, device)
            for d, (index, device) in enumerate(y_line)
        ]
        home.third()

        mats = (eg, eu, ed)
        second = []

        def fold_expert(m):
            mat = mats[m]
            arrived = [far_p.at[0, 0]] * 3 + [far_q.at[0]]
            for i, block in enumerate(arrived):
                sems = (far_sems.at[0, m * 4 + i], far_sems.at[1, m * 4 + i])
                copy = pltpu.make_async_remote_copy(
                    src_ref=block, dst_ref=block, send_sem=sems[0], recv_sem=sems[1],
                    device_id=sibling, device_id_type=MESH,
                )
                copy.wait()
            steps = []
            for lo in range(2):
                terms = [mat.at[0, lo, place.y]]
                for d in range(3):
                    terms.append(far_p.at[d, m, lo])
                steps.append((terms, sum_p.at[lo, m]))
            for y_at in range(4):
                steps.append(([mat.at[1, place.lo, y_at], far_q.at[m, y_at]], sum_q.at[y_at, m]))

            def fetch(step):
                loads = []
                for i, term in enumerate(steps[step][0]):
                    loads.append(
                        pltpu.make_async_copy(term, stage.at[step % 2, i], fold_sems.at[step % 2, i])
                    )
                    loads[-1].start()
                return loads

            ready = fetch(0)
            for step, (terms, out) in enumerate(steps):
                following = fetch(step + 1) if step + 1 < len(steps) else None
                for load in ready:
                    load.wait()

                def fold(i, carry):
                    part = pl.ds(pl.multiple_of(i * 48, 16), 48)
                    total = stage[step % 2, 0, part].astype(F32)
                    for term in range(1, len(terms)):
                        total = total + stage[step % 2, term, part].astype(F32)
                    out[part] = total.astype(BF)
                    return carry

                lax.fori_loop(0, 4, fold, 0)
                ready = following
            pair = (expert_sems.at[0, 4 + m * 4], expert_sems.at[1, 4 + m * 4])
            second.append(send(sum_p.at[other_lo, m], land_p2.at[m], pair, lo_device))
            for d, (index, device) in enumerate(y_line):
                pair = (expert_sems.at[0, 5 + m * 4 + d], expert_sems.at[1, 5 + m * 4 + d])
                second.append(send(sum_q.at[index, m], land_q2.at[d, m], pair, device))

        fold_expert(0)
        fold_expert(1)
        streams.step("o1", 1)
        streams.step("o2", 1)
        streams.step("q2", 0)
        streams.step("s1", 0)
        streams.step("s2", 0)
        streams.step("q1", 0)
        fold_expert(2)
        for copy in legs:
            copy.wait_recv()
        kv_add(
            lambda a: dkv.at[a * 4 + place.y, later], 2,
            [lambda a, d=d: land_c.at[d, a] for d in range(3)],
        )
        leg_d = kv_push(dkv.at[other_lo * 4 + place.y, later], land_d, 10, lo_device)
        streams.step("q2", 1)
        streams.step("s1", 1)
        streams.step("s2", 1)
        streams.step("q1", 1)
        for name in STREAMS:
            streams.land(name, 2)
        own_quarter = place.core * 2 + place.hi
        gathered = []
        for i, (a, b) in enumerate(((0, 1), (1, 0), (1, 1))):
            pair = (quarter_sems.at[0, i], quarter_sems.at[1, i])
            gathered.append(send(mine, quarters.at[own_quarter], pair, place.at(hi=a, core=b)))
        own_quarters = pltpu.make_async_copy(mine, quarters.at[own_quarter], weight_sems.at[5])
        own_quarters.start()

        for copy in legs_b:
            copy.wait_recv()

        def key_grads(core, terms):
            for i in range(2):
                for which in range(2):
                    total = dkv[context, core * 2 + i, which].astype(F32)
                    for term in terms:
                        total = total + term(i, which).astype(F32)
                    lanes = pl.ds(pl.multiple_of((which * 4 + core * 2 + i) * 128, 128), 128)
                    dk[:, lanes] = total.astype(BF)

        key_grads(other, [lambda i, w, d=d: land_b[d, i, w] for d in range(3)])
        leg_d.wait_recv()
        key_grads(place.core, [lambda i, w: land_d[i, w]])
        load_q.wait()
        load_k.wait()
        load_v.wait()
        load_x.wait()
        x = x_ref[...].astype(F32)
        root = inverse_root(x)
        queries = jnp.concatenate([dq[0], dq[1]], axis=1)
        for j in range(4):
            part = slice(j * 384, (j + 1) * 384)
            gt[:, part] = (
                contract(queries, big[part, 0:1536], ((1,), (1,)))
                + contract(dk[:, 0:512], big[part, 1536:2048], ((1,), (1,)))
                + contract(dk[:, 512:1024], w_v[part, :], ((1,), (1,)))
            )
        scaled = gt[...] * gain_attn[...].reshape(1, 1536)
        inner = jnp.mean(scaled * x, axis=-1, keepdims=True)
        gt[...] = dy1[...] + root * scaled - x * (root * root * root * inner)

        outs = [pltpu.make_async_copy(gt, gt_far, out_sems.at[0])]
        outs[0].start()
        home.finish(mixed, [y1])
        outs.append(pltpu.make_async_copy(mixed, mixed_far, out_sems.at[1]))
        outs[1].start()
        home.drain()
        for copy in gathered:
            copy.wait_recv()
        for m in range(3):
            for copy in second[m * 4 : m * 4 + 4]:
                copy.wait_recv()

            def finish(i, carry):
                part = pl.ds(pl.multiple_of(i * 48, 16), 48)
                experts[m, 0, part] = sum_p[place.lo, m, part].astype(F32) + land_p2[m, part].astype(F32)
                total = sum_q[place.y, m, part].astype(F32)
                for d in range(3):
                    total = total + land_q2[d, m, part].astype(F32)
                experts[m, 1, part] = total
                return carry

            lax.fori_loop(0, 4, finish, 0)
            outs.append(pltpu.make_async_copy(experts.at[m], experts_far.at[m], out_sems.at[2 + m]))
            outs[-1].start()
        for copy in pending + kv_sent + gathered + second + streams.sent:
            copy.wait_send()
        own_quarters.wait()
        for copy in outs:
            copy.wait()

    pl.run_scoped(
        early, low(16, 128, 1536), low(16, 128, 1536), high(16, 8, 128), high(16, 8, 128),
        low(8, 128, 1536), low(7, 128, 1536), low(1536, 128),
        low(2, 2, 4, 192, 512), low(2, 1536, 512), low(2, 512, 1536),
    )
    buffers = []
    for _, width, _ in STREAMS.values():
        buffers += [
            low(4, 4, 4, 48, width), low(3, 4, 4, 48, width), low(4, 4, 48, width),
            low(3, 4, 48, width), low(4, 48, width), low(3, 48, width),
        ]
    pl.run_scoped(
        late, low(128, 1536), low(128, 1536), low(1536, 2048), low(1536, 512),
        low(256, 1536), low(256, 768), low(256, 768), low(8, 2, 2, 128, 128),
        high(128, 128), low(2, 128, 768), low(4, 384, 128), high(8, 1, 384),
        low(2, 128, 768), low(128, 1024), high(128, 1536), low(8, 4, 2, 128, 128),
        low(4, 2, 2, 128, 128), low(3, 2, 2, 128, 128), low(3, 2, 2, 2, 128, 128), low(2, 2, 128, 128),
        low(48, ALL_WIDE), low(2, 4, 192, 512),
        low(2, 3, 192, 512), low(4, 3, 192, 512), low(3, 192, 512), low(3, 3, 192, 512),
        high(3, 2, 192, 512), low(128, 1536), high(128, 1536), *buffers,
    )


def run_layer(*operands):
    vmem = pl.BlockSpec(memory_space=pltpu.VMEM)
    hbm = pl.BlockSpec(memory_space=pl.ANY)
    sems = pltpu.SemaphoreType.DMA
    struct = jax.ShapeDtypeStruct
    return pl.pallas_call(
        layer_kernel,
        out_shape=(
            struct((128, 1536), BF), struct((128, 1536), F32), struct((4, 48, ALL_WIDE), BF),
            struct((3, 2, 192, 512), F32),
            *[struct((2, 2, 4, 192, 512), BF)] * 3,
            struct((3, 3, 2, 192, 512), BF), struct((3, 4, 192, 512), BF), struct((2, 8, 1536, 128), BF),
        ),
        in_specs=[hbm, vmem, hbm, vmem, vmem, vmem] + [hbm] * 7,
        out_specs=[hbm] * 10,
        scratch_shapes=[
            low(2, 8, 128, 512), low(4, 384, 128), high(8, 1, 384), low(128, 1536), high(128, 1536),
            low(128, 1536), high(128, 128), high(2, 128, 128), high(128, 1536), high(16, 8, 128),
            low(8, 128, 1536), low(2, 2, 64, 1536), low(5, 128, 1536),
            pltpu.SemaphoreType.REGULAR, sems((6,)), sems((3,)), sems, sems((2, 18)), sems((2, 8)),
            sems((2, 8)),
            sems((2, 16)), sems((2, 16)), sems((2, 9)), sems((2, 16)), sems((2,)), sems((2, 2)),
            sems((2, 16)), sems, sems((2, 12)),
            sems((16,)), sems((2, 4)), sems((2, 11)), sems((2, 9 * len(STREAMS))), sems((2, 3)),
            sems((2, 11)), sems((2, 4)), sems((2, 16)), sems((5,)),
        ],
        compiler_params=pltpu.CompilerParams(
            collective_id=0, has_side_effects=True, vmem_limit_bytes=63 << 20
        ),
    )(*operands)


def finish_kernel(
    mixed, gt, quarters, experts, gain, wq, wk, wv,
    mixed_out, gt_out, gq, gk, gv, go, ga, gm, gr, og, ou, od,
    rows_q, rows_kv, sems,
):
    place = Place()
    start = ((place.lo * 4 + place.y) * 4 + place.z) * 48
    rows = pl.ds(pl.multiple_of(start, 16), 48)
    loads = [
        pltpu.make_async_copy(wq.at[rows, :], rows_q, sems.at[0]),
        pltpu.make_async_copy(wk.at[rows, :], rows_kv.at[0], sems.at[1]),
        pltpu.make_async_copy(wv.at[rows, :], rows_kv.at[1], sems.at[2]),
    ]
    for load in loads:
        load.start()
    mixed_out[0] = mixed[...]
    gt_out[0] = gt[...]
    for q in range(4):
        go[:, q * 384 : (q + 1) * 384] = quarters[q, :, 0:384].astype(F32)
        gq[:, q * 384 : (q + 1) * 384] = quarters[q, :, 512:896].astype(F32)
        gk[:, q * 128 : (q + 1) * 128] = quarters[q, :, 896:1024].astype(F32)
        gv[:, q * 128 : (q + 1) * 128] = quarters[q, :, 1024:1152].astype(F32)
    narrow = quarters[0, :, 384:512].astype(F32) + quarters[2, :, 384:512].astype(F32)
    og[...] = experts[0]
    ou[...] = experts[1]
    od[...] = experts[2]
    for load in loads:
        load.wait()
    line = jnp.sum(gq[...] * rows_q[...].astype(F32), axis=1, keepdims=True)
    line = line + jnp.sum(gk[...] * rows_kv[0].astype(F32), axis=1, keepdims=True)
    line = line + jnp.sum(gv[...] * rows_kv[1].astype(F32), axis=1, keepdims=True)
    column = lax.broadcasted_iota(jnp.int32, (48, 1536), 1) - lax.broadcasted_iota(jnp.int32, (48, 1536), 0)
    own_gain = jnp.sum(jnp.where(column == start, gain[...].reshape(1, 1536), 0.0), axis=1, keepdims=True)
    both = jnp.where(
        lax.broadcasted_iota(jnp.int32, (48, 128), 1) == 33, line / own_gain, narrow
    )
    flat = jnp.concatenate([both, jnp.zeros((80, 128), F32)], axis=0).T
    gr[...] = flat[0:32, 0:48]
    gm[...] = flat[32:33, 0:48]
    ga[...] = flat[33:34, 0:48]


def run_finish(*operands):
    vmem = pl.BlockSpec(memory_space=pltpu.VMEM)
    hbm = pl.BlockSpec(memory_space=pl.ANY)
    f32 = lambda *shape: jax.ShapeDtypeStruct(shape, F32)
    return pl.pallas_call(
        finish_kernel,
        out_shape=(
            jax.ShapeDtypeStruct((1, 128, 1536), BF), f32(1, 128, 1536),
            f32(48, 1536), f32(48, 512), f32(48, 512), f32(48, 1536), f32(1, 48), f32(1, 48), f32(32, 48),
            f32(2, 192, 512), f32(2, 192, 512), f32(2, 192, 512),
        ),
        in_specs=[vmem] * 5 + [hbm] * 3,
        out_specs=[vmem] * 12,
        scratch_shapes=[low(48, 1536), low(2, 48, 512), pltpu.SemaphoreType.DMA((3,))],
        compiler_params=pltpu.CompilerParams(vmem_limit_bytes=63 << 20),
    )(*operands)


def shards(
    tokens, expert_ids, w_query, w_key, w_value, w_out, gain_attn, gain_moe, w_router,
    w_gate, w_up, w_down, cotangent,
):
    mixed, gt, quarters, experts, *_ = run_layer(
        tokens[0], expert_ids[0].T, cotangent[0], gain_attn, gain_moe, w_router.T,
        w_query, w_key, w_value, w_out, w_gate.reshape(2, 2, 4, 192, 512), w_up, w_down,
    )
    mixed, gt, gq, gk, gv, go, ga, gm, gr, og, ou, od = run_finish(
        mixed, gt, quarters, experts, gain_attn, w_query, w_key, w_value
    )
    return (mixed, gt, gq, gk, gv, go, ga.reshape(48), gm.reshape(48), gr.T, og, ou, od.transpose(0, 2, 1))


def solution(mesh):
    in_specs = (
        P(("expert", "dp"), "context", None),
        P(("expert", "dp"), "context", None),
        P(),
        P(),
        P(),
        P(),
        P(),
        P(),
        P(),
        P(("expert", "dp"), None, None),
        P(("expert", "dp"), None, None),
        P(("expert", "dp"), None, None),
        P(("expert", "dp"), "context", None),
    )
    out_specs = (
        P(("expert", "dp"), "context", None),
        P(("expert", "dp"), "context", None),
        P(("context", "dp"), None),
        P(("context", "dp"), None),
        P(("context", "dp"), None),
        P(("context", "dp"), None),
        P(("context", "dp")),
        P(("context", "dp")),
        P(("context", "dp"), None),
        P(("expert", "dp"), "context", None),
        P(("expert", "dp"), "context", None),
        P(("expert", "dp"), None, "context"),
    )
    return jax.shard_map(shards, mesh=mesh, in_specs=in_specs, out_specs=out_specs, check_vma=False)
```
